256 devices in a mesh: audio: 16 (over y_lo, x, core), score: 16 (over y_hi, z).
Axes of the slice: x: 4, y: 4 (y_hi: 2, y_lo: 2; y = y_hi * 2 + y_lo), z: 8, core: 2. Of those that a mesh axis runs over, the one named last changes fastest.
Arguments:
- hidden_in: bfloat16 [32768, 1280], P('audio'), may hold values from -6 to 6
- up_weight: bfloat16 [1280, 5120], P(None, 'score'), may hold values from -0.15625 to 0.15625
- down_weight: bfloat16 [5120, 1280], P('score'), may hold values from -0.078125 to 0.078125
- head_weight: bfloat16 [1280, 768], replicated, may hold values from -0.15625 to 0.15625
- score_embed: bfloat16 [32768, 768], P(('audio', 'score')), may hold values from -0.21875 to 0.21875
- pair_index: int32 [16, 2048], P('audio'), may hold values from 0 to 2047, each once within a row
Outputs:
- up_grad: float32 [1280, 5120], P('audio', 'score')
- down_grad: float32 [5120, 1280], P('score', 'audio')
- score_grad: float32 [32768, 768], P(('audio', 'score'))
The draws below stay inside these ranges and needn't reach their ends.
Inputs may be any that keep to these rules, and one draw needn't show every extreme that they name: Each row of pair_index names every one of the 2048 score rows of its group exactly once.
All inputs are finite; a program needn't handle non-finite values.
Results may differ from the reference program's by a relative error of at most 0.025.
Values may be sent and summed in bfloat16 or wider, within the bound.
No kernel may reach another device: no remote copies, remote signals or barrier semaphores. Data moves between devices by JAX's collectives and lax.ppermute only.
A program may use at most 128 MiB of HBM per device.

```python
import jax
import jax.numpy as jnp
from jax import lax

WIDTH = 1280
FF = 5120
EMBED = 768
GROUP = 2048
PAIRS = 32768
N_AUDIO = 16
N_SCORE = 16


def steps_of(key, shape, shards, smallest, top_value):
    def one(dim, shards_of):
        heights = jax.random.uniform(jax.random.fold_in(jax.random.fold_in(key, 6), dim), (shards_of,), jnp.float32, smallest / len(shards), top_value / len(shards))
        return jnp.repeat(jnp.exp(heights), shape[dim] // shards_of).reshape((-1,) + (1,) * (len(shape) - dim - 1))

    level = one(*shards[0])
    for cut in shards[1:]:
        level = level * one(*cut)
    return level


def bell_draw(rng, shape, width, limit, split=(), held_as=jnp.bfloat16):
    result = jax.random.normal(rng, shape, jnp.float32) * width
    if len(split) > 0:
        result = steps_of(rng, shape, split, -0.22, 0.18) * result
    return jnp.clip(result, min=-limit, max=limit).astype(held_as)


def setup_inputs(seed: int = 0) -> dict:
    arg_keys = jax.random.split(jax.random.key(seed), 7)
    hidden_in = bell_draw(arg_keys[0], (PAIRS, WIDTH), 1.0, 6.0, ((0, 16),))
    up_weight = bell_draw(arg_keys[1], (WIDTH, FF), WIDTH ** -0.5, 0.15625, ((1, 16),))
    down_weight = bell_draw(arg_keys[2], (FF, WIDTH), FF ** -0.5, 0.078125, ((0, 16),))
    head_weight = bell_draw(arg_keys[3], (WIDTH, EMBED), WIDTH ** -0.5, 0.15625)
    score_embed = bell_draw(arg_keys[4], (PAIRS, EMBED), EMBED ** -0.5, 0.21875, ((0, 256),))
    pair_index = jax.vmap(lambda own: jax.random.permutation(own, GROUP))(jax.random.split(arg_keys[5], N_AUDIO)).reshape((N_AUDIO, GROUP)).astype(jnp.int32)
    return {"hidden_in": hidden_in, "up_weight": up_weight, "down_weight": down_weight, "head_weight": head_weight, "score_embed": score_embed, "pair_index": pair_index}


logit_scale = 8.0
logit_bias = -3.0
epsilon = 1e-06
gelu_root = 0.7978845608028654
gelu_cubic = 0.044715

def gelu_slope(pre):
    inner = gelu_root * (pre + gelu_cubic * pre * pre * pre)
    tangent = jnp.tanh(inner)
    return 0.5 * (1.0 + tangent) + 0.5 * pre * (1.0 - tangent * tangent) * gelu_root * (1.0 + 3.0 * gelu_cubic * pre * pre)

def unit_rows(values):
    wide = values.astype(jnp.float32)
    inverse = lax.rsqrt(lax.optimization_barrier(jnp.sum(wide * wide, axis=-1, keepdims=True)) + epsilon)
    return (wide * inverse, inverse)

def unit_backward(unit_wide, inverse, grad_unit):
    inner = lax.optimization_barrier(jnp.sum(unit_wide * grad_unit, axis=-1, keepdims=True))
    return inverse * (grad_unit - unit_wide * inner)

def pair_coeffs(left, right, partner, first_col):
    logits = logit_scale * jnp.einsum('ie,je->ij', left.astype(jnp.float32), right.astype(jnp.float32)) + logit_bias
    columns = first_col + jnp.arange(right.shape[0], dtype=jnp.int32)
    sign = jnp.where(partner[:, None] == columns[None, :], 1.0, -1.0)
    return (-logit_scale * sign * jax.nn.sigmoid(-sign * logits)).astype(jnp.bfloat16)

def reference(hidden_in, up_weight, down_weight, head_weight, score_embed, pair_index):
    slice_width = FF // N_SCORE
    up_total = jnp.zeros((WIDTH, FF), jnp.float32)
    down_total = jnp.zeros((FF, WIDTH), jnp.float32)
    score_parts = []
    down_split = down_weight.reshape(N_SCORE, slice_width, WIDTH).astype(jnp.float32)
    for group in range(N_AUDIO):
        block = hidden_in[group * GROUP:(group + 1) * GROUP]
        wide_in = block.astype(jnp.float32)
        square_mean = lax.optimization_barrier(jnp.mean(wide_in * wide_in, axis=-1, keepdims=True))
        normed = (wide_in * lax.rsqrt(square_mean + epsilon)).astype(jnp.bfloat16)
        pre_act = jnp.dot(normed, up_weight, preferred_element_type=jnp.float32)
        act_out = jax.nn.gelu(pre_act, approximate=True).astype(jnp.bfloat16)
        act_split = act_out.reshape(GROUP, N_SCORE, slice_width).astype(jnp.float32)
        parts = jnp.einsum('gkf,kfw->kgw', act_split, down_split).astype(jnp.bfloat16)
        parts = lax.optimization_barrier(parts)
        layer_out = (wide_in + lax.optimization_barrier(jnp.sum(parts.astype(jnp.float32), axis=0))).astype(jnp.bfloat16)
        audio_wide, audio_inverse = unit_rows(jnp.dot(layer_out, head_weight, preferred_element_type=jnp.float32))
        audio_unit = audio_wide.astype(jnp.bfloat16)
        score_wide, score_inverse = unit_rows(score_embed[group * GROUP:(group + 1) * GROUP])
        score_unit = score_wide.astype(jnp.bfloat16)
        coeffs = pair_coeffs(audio_unit, score_unit, pair_index[group], 0)
        grad_audio = jnp.dot(coeffs, score_unit, preferred_element_type=jnp.float32)
        grad_score = jnp.dot(coeffs.T, audio_unit, preferred_element_type=jnp.float32)
        score_parts.append(unit_backward(score_wide, score_inverse, grad_score))
        grad_embed = unit_backward(audio_wide, audio_inverse, grad_audio).astype(jnp.bfloat16)
        grad_layer = jnp.dot(grad_embed, head_weight.T, preferred_element_type=jnp.float32).astype(jnp.bfloat16)
        grad_act = jnp.dot(grad_layer, down_weight.T, preferred_element_type=jnp.float32)
        grad_pre = (grad_act * gelu_slope(pre_act)).astype(jnp.bfloat16)
        up_total = up_total + jnp.dot(normed.T, grad_pre, preferred_element_type=jnp.float32)
        down_total = down_total + jnp.dot(act_out.T, grad_layer, preferred_element_type=jnp.float32)
    return (up_total, down_total, jnp.concatenate(score_parts, axis=0))
```

```python
import jax
import jax.numpy as jnp
from jax import lax
from jax.sharding import Mesh, PartitionSpec as P

logit_scale = 8.0
logit_bias = -3.0
epsilon = 1e-06
gelu_root = 0.7978845608028654
gelu_cubic = 0.044715

AUDIO = ("ylo", "x", "core")
SCORE = ("yhi", "z")
f32 = jnp.float32
bf16 = jnp.bfloat16


def dot(left, right, dims):
    return lax.dot_general(left, right, (dims, ((), ())), preferred_element_type=f32)


def gelu_slope(pre):
    inner = gelu_root * (pre + gelu_cubic * pre * pre * pre)
    tangent = jnp.tanh(inner)
    return 0.5 * (1.0 + tangent) + 0.5 * pre * (1.0 - tangent * tangent) * gelu_root * (
        1.0 + 3.0 * gelu_cubic * pre * pre
    )


def unit_rows(values):
    wide = values.astype(f32)
    inverse = lax.rsqrt(jnp.sum(wide * wide, axis=-1, keepdims=True) + epsilon)
    return (wide * inverse, inverse)


def unit_backward(unit_wide, inverse, grad_unit):
    inner = jnp.sum(unit_wide * grad_unit, axis=-1, keepdims=True)
    return inverse * (grad_unit - unit_wide * inner)


def pair_coeffs(left, right, partner, first_column):
    logits = logit_scale * dot(left, right, ((1,), (1,))) + logit_bias
    columns = first_column + lax.iota(jnp.int32, right.shape[0])
    sign = jnp.where(partner[:, None] == columns[None, :], 1.0, -1.0)
    return (-logit_scale * sign * jax.nn.sigmoid(-sign * logits)).astype(bf16)


def swap(value, axis):
    return lax.ppermute(value, axis, [(0, 1), (1, 0)])


def per_device(hidden_in, up_weight, down_weight, head_weight, score_embed, pair_index):
    y_hi, z = lax.axis_index("yhi"), lax.axis_index("z")
    group_rows = hidden_in.shape[0]
    own_rows = group_rows // 8
    half = group_rows // 2
    score_wide, score_inverse = unit_rows(score_embed)
    score_half = lax.all_gather(score_wide.astype(bf16), "z", axis=0, tiled=True)
    down_head = dot(down_weight, head_weight, ((1,), (0,))).astype(bf16)
    square_mean = jnp.mean(jnp.square(hidden_in.astype(f32)), axis=-1, keepdims=True)
    normed = (hidden_in.astype(f32) * lax.rsqrt(square_mean + epsilon)).astype(bf16)
    pre_act = dot(normed, up_weight, ((1,), (0,)))
    act_out = jax.nn.gelu(pre_act, approximate=True).astype(bf16)
    part = dot(act_out, down_head, ((1,), (0,))).astype(bf16)
    summed = lax.psum_scatter(part, "z", scatter_dimension=0, tiled=True)
    own_hidden = lax.dynamic_slice_in_dim(hidden_in, z * own_rows, own_rows, 0)
    own_proj = dot(own_hidden, head_weight, ((1,), (0,)))
    audio_proj = own_proj + (summed.astype(f32) + swap(summed, "yhi").astype(f32))
    audio_wide, audio_inverse = unit_rows(audio_proj)
    audio_unit = audio_wide.astype(bf16)
    partners = lax.dynamic_slice_in_dim(pair_index[0], z * own_rows, own_rows, 0)
    coeffs = pair_coeffs(audio_unit, score_half, partners, y_hi * half)
    grad_audio = dot(coeffs, score_half, ((1,), (0,)))
    grad_audio = grad_audio + swap(grad_audio.astype(bf16), "yhi").astype(f32)
    grad_embed = unit_backward(audio_wide, audio_inverse, grad_audio).astype(bf16)
    grad_all = lax.all_gather(grad_embed, "z", axis=0, tiled=True)
    grad_score = lax.psum_scatter(
        dot(coeffs, audio_unit, ((0,), (0,))).astype(bf16), "z", scatter_dimension=0, tiled=True
    ).astype(f32)
    score_grad = unit_backward(score_wide, score_inverse, grad_score)
    grad_act = dot(grad_all, down_head, ((1,), (1,)))
    grad_pre = (grad_act * gelu_slope(pre_act)).astype(bf16)
    up_part = dot(normed, grad_pre, ((0,), (0,)))
    act_grad = dot(act_out, grad_all, ((0,), (0,))).astype(bf16)
    down_part = dot(head_weight, act_grad, ((1,), (1,)))
    both = jnp.concatenate([up_part.astype(bf16), down_part.astype(bf16)], axis=1)
    both = both.reshape(8, 2, 80, both.shape[1])
    core = lax.axis_index("core")
    keep = lax.dynamic_index_in_dim(both, core, 1, keepdims=False)
    give = lax.dynamic_index_in_dim(both, 1 - core, 1, keepdims=False)
    chip = (keep.astype(f32) + swap(give, "core").astype(f32)).astype(bf16)
    landed = lax.all_to_all(chip, ("ylo", "x"), 0, 0)
    total = jnp.sum(landed.astype(f32), axis=0)
    ff = up_weight.shape[1]
    return (total[:, :ff], total[:, ff:].T, score_grad)


def solution(mesh):
    fine = Mesh(mesh.devices.reshape(2, 4, 2, 2, 8), ("ylo", "x", "core", "yhi", "z"))
    in_specs = (
        P(AUDIO, None),
        P(None, SCORE),
        P(SCORE, None),
        P(),
        P(AUDIO + SCORE, None),
        P(AUDIO, None),
    )
    out_specs = (P(AUDIO, SCORE), P(SCORE, AUDIO), P(AUDIO + SCORE, None))
    return jax.shard_map(
        per_device, mesh=fine, in_specs=in_specs, out_specs=out_specs, check_vma=False
    )
```

```python
import functools

import jax
import jax.numpy as jnp
from jax import lax
from jax.experimental import pallas as pl
from jax.experimental.pallas import tpu as pltpu
from jax.sharding import Mesh, PartitionSpec as P

logit_scale = 8.0
logit_bias = -3.0
epsilon = 1e-06
gelu_root = 0.7978845608028654
gelu_cubic = 0.044715

AUDIO = ("ylo", "x", "core")
SCORE = ("yhi", "z")
RING = 8
VMEM_BYTES = 40 * 1024 * 1024
f32 = jnp.float32
bf16 = jnp.bfloat16


def dot(left, right, dims=((1,), (0,))):
    return lax.dot_general(left, right, (dims, ((), ())), preferred_element_type=f32)


def unit_rows(values):
    wide = values.astype(f32)
    inverse = lax.rsqrt(jnp.sum(wide * wide, axis=-1, keepdims=True) + epsilon)
    return (wide * inverse, inverse)


def unit_backward(unit_wide, inverse, grad_unit):
    inner = jnp.sum(unit_wide * grad_unit, axis=-1, keepdims=True)
    return inverse * (grad_unit - unit_wide * inner)


def pair_coeffs(left, right, partner, first_column):
    logits = logit_scale * dot(left, right, ((1,), (1,))) + logit_bias
    columns = first_column + lax.iota(jnp.int32, right.shape[0])
    sign = jnp.where(partner[:, None] == columns[None, :], 1.0, -1.0)
    return (-logit_scale * sign * jax.nn.sigmoid(-sign * logits)).astype(bf16)


def swap(value, axis):
    return lax.ppermute(value, axis, [(0, 1), (1, 0)])


def shift(value, step):
    return lax.ppermute(value, "z", [(i, (i + step) % RING) for i in range(RING)])


def forward_kernel(index_ref, hidden_ref, up_ref, down_head_ref, part_ref, normed_t_ref, act_t_ref, slope_ref):
    wide = hidden_ref[...].astype(f32)
    square_mean = jnp.mean(wide * wide, axis=-1, keepdims=True)
    normed = wide * lax.rsqrt(square_mean + epsilon)
    normed_t_ref[...] = normed.T.astype(bf16)
    pre = dot(normed.astype(bf16), up_ref[...])
    tangent = jnp.tanh(gelu_root * (pre + gelu_cubic * (pre * pre * pre)))
    act = 0.5 * pre * (1.0 + tangent)
    slope_ref[...] = 0.5 * (1.0 + tangent) + 0.5 * pre * (1.0 - tangent * tangent) * gelu_root * (
        1.0 + 3.0 * gelu_cubic * pre * pre
    )
    act_t_ref[...] = act.T.astype(bf16)
    part_ref[...] = dot(act.astype(bf16), down_head_ref[...]).astype(bf16)


def forward_blocks(offsets, position, hidden_in, up_weight, down_head):
    count = len(offsets)
    rows = hidden_in.shape[0] // RING
    width, ff = up_weight.shape
    embed = down_head.shape[1]
    index = lax.rem(position + jnp.array([o % RING for o in offsets], jnp.int32), RING)
    return pl.pallas_call(
        forward_kernel,
        grid_spec=pltpu.PrefetchScalarGridSpec(
            num_scalar_prefetch=1,
            grid=(count,),
            in_specs=[
                pl.BlockSpec((rows, width), lambda i, index: (index[i], 0)),
                pl.BlockSpec((width, ff), lambda i, index: (0, 0)),
                pl.BlockSpec((ff, embed), lambda i, index: (0, 0)),
            ],
            out_specs=[
                pl.BlockSpec((rows, embed), lambda i, index: (i, 0)),
                pl.BlockSpec((width, rows), lambda i, index: (0, i)),
                pl.BlockSpec((ff, rows), lambda i, index: (0, i)),
                pl.BlockSpec((rows, ff), lambda i, index: (i, 0)),
            ],
        ),
        out_shape=[
            jax.ShapeDtypeStruct((count * rows, embed), bf16),
            jax.ShapeDtypeStruct((width, count * rows), bf16),
            jax.ShapeDtypeStruct((ff, count * rows), bf16),
            jax.ShapeDtypeStruct((count * rows, ff), f32),
        ],
        compiler_params=pltpu.CompilerParams(vmem_limit_bytes=VMEM_BYTES),
        cost_estimate=pl.CostEstimate(
            flops=2 * count * rows * ff * (width + embed),
            bytes_accessed=2 * count * rows * (2 * width + embed + 3 * ff) + 2 * ff * (width + embed),
            transcendentals=count * rows * ff,
        ),
    )(index, hidden_in, up_weight, down_head)


def backward_kernel(pieces, first, last, *refs):
    grads = refs[:pieces]
    down_head_ref, normed_t_ref, act_t_ref, slope_ref = refs[pieces : pieces + 4]
    rest = refs[pieces + 4 :]
    if not first:
        up_in, act_in = rest[:2]
        rest = rest[2:]
    if last:
        core_ref, head_ref, keep_ref, give_ref, up_acc, act_acc = rest
    else:
        up_acc, act_acc = rest
    tile = 256
    start = 0
    grad_pre = []
    for grad_ref in grads:
        count = grad_ref.shape[0]
        grad_act = dot(grad_ref[...], down_head_ref[...], ((1,), (1,)))
        grad_pre.append((grad_act * slope_ref[start : start + count, :]).astype(bf16))
        start += count
    start = 0
    act_sum = None
    for grad_ref in grads:
        count = grad_ref.shape[0]
        term = dot(act_t_ref[:, start : start + count], grad_ref[...])
        act_sum = term if act_sum is None else act_sum + term
        start += count
    if not first:
        act_sum = act_sum + act_in[...]
    act_acc[...] = act_sum
    grad_pre = jnp.concatenate(grad_pre, axis=0) if len(grad_pre) > 1 else grad_pre[0]

    for m in range(0, up_acc.shape[0], tile):
        up_sum = dot(normed_t_ref[m : m + tile, :], grad_pre)
        if not first:
            up_sum = up_sum + up_in[m : m + tile, :]
        up_acc[m : m + tile, :] = up_sum
    if last:
        core = core_ref[0]
        ff = up_acc.shape[1]
        act_grad = act_acc[...].astype(bf16)
        act_acc_rows = keep_ref.shape[1]
        for half, out_ref in ((core, keep_ref), (1 - core, give_ref)):
            for chip in range(keep_ref.shape[0]):
                at = pl.multiple_of((2 * chip + half) * act_acc_rows, act_acc_rows)
                out_ref[chip, :, :ff] = up_acc[pl.ds(at, act_acc_rows), :].astype(bf16)
        for m in range(0, up_acc.shape[0], tile):
            up_acc[m : m + tile, :] = dot(head_ref[m : m + tile, :], act_grad, ((1,), (1,)))
        for half, out_ref in ((core, keep_ref), (1 - core, give_ref)):
            for chip in range(keep_ref.shape[0]):
                at = pl.multiple_of((2 * chip + half) * act_acc_rows, act_acc_rows)
                out_ref[chip, :, ff:] = up_acc[pl.ds(at, act_acc_rows), :].astype(bf16)


def backward_blocks(grads, saved, down_head, sums, last=None):
    _, normed_t, act_t, slope = saved
    width, rows = normed_t.shape
    ff, embed = down_head.shape
    args = list(grads) + [down_head, normed_t, act_t, slope]
    specs = [pl.BlockSpec(memory_space=pltpu.VMEM)] * len(args)
    aliases = {}
    if sums is not None:
        if last is None:
            aliases = {len(args): 0, len(args) + 1: 1}
        args += list(sums)
        specs += [pl.BlockSpec(memory_space=pltpu.VMEM)] * 2
    flops = 2 * rows * ff * (2 * embed + width)
    if last is None:
        shapes = [jax.ShapeDtypeStruct((width, ff), f32), jax.ShapeDtypeStruct((ff, embed), f32)]
        scratch = []
    else:
        args += list(last)
        specs += [pl.BlockSpec(memory_space=pltpu.SMEM), pl.BlockSpec(memory_space=pltpu.VMEM)]
        shapes = [jax.ShapeDtypeStruct((8, width // 16, 2 * ff), bf16)] * 2
        scratch = [pltpu.VMEM((width, ff), f32), pltpu.VMEM((ff, embed), f32)]
        flops += 2 * width * ff * embed
    return pl.pallas_call(
        functools.partial(backward_kernel, len(grads), sums is None, last is not None),
        in_specs=specs,
        out_specs=[pl.BlockSpec(memory_space=pltpu.VMEM)] * 2,
        out_shape=shapes,
        scratch_shapes=scratch,
        input_output_aliases=aliases,
        compiler_params=pltpu.CompilerParams(vmem_limit_bytes=VMEM_BYTES),
        cost_estimate=pl.CostEstimate(
            flops=flops, bytes_accessed=8 * 1024 * 1024, transcendentals=0
        ),
    )(*args)


def add(left, right):
    return (left.astype(f32) + right.astype(f32)).astype(bf16)


def per_device(hidden_in, up_weight, down_weight, head_weight, score_embed, pair_index):
    y_hi, z, core = lax.axis_index("yhi"), lax.axis_index("z"), lax.axis_index("core")
    own_rows = hidden_in.shape[0] // RING
    cut = own_rows // 2
    group_half = hidden_in.shape[0] // 2
    score_wide, score_inverse = unit_rows(score_embed)
    score_half = lax.all_gather(score_wide.astype(bf16), "z", axis=0, tiled=True)
    down_head = dot(down_weight, head_weight).astype(bf16)
    saved = {
        0: None,
    }
    run = lambda *offsets: forward_blocks(offsets, z, hidden_in, up_weight, down_head)
    saved[4] = run(4)
    part = saved[4][0]
    fore, back = shift(part[:cut], 1), shift(part[cut:], -1)
    saved[3] = run(3, -3)
    ahead, behind = saved[3][0][:own_rows], saved[3][0][own_rows:]
    fore = jnp.concatenate([add(fore, ahead[:cut]), ahead[cut:]], axis=0)
    back = jnp.concatenate([behind[:cut], add(back, behind[cut:])], axis=0)
    for step in (2, 1):
        fore, back = shift(fore, 1), shift(back, -1)
        saved[step] = run(step, -step)
        fore = add(fore, saved[step][0][:own_rows])
        back = add(back, saved[step][0][own_rows:])
    fore, back = shift(fore, 1), shift(back, -1)
    saved[0] = run(0)
    summed = (fore.astype(f32) + back.astype(f32) + saved[0][0].astype(f32)).astype(bf16)
    own_hidden = lax.dynamic_slice_in_dim(hidden_in, z * own_rows, own_rows, 0)
    own_proj = dot(own_hidden, head_weight)
    audio_proj = own_proj + (summed.astype(f32) + swap(summed, "yhi").astype(f32))
    audio_wide, audio_inverse = unit_rows(audio_proj)
    audio_unit = audio_wide.astype(bf16)
    partners = lax.dynamic_slice_in_dim(pair_index[0], z * own_rows, own_rows, 0)
    coeffs = pair_coeffs(audio_unit, score_half, partners, y_hi * group_half)
    grad_audio = dot(coeffs, score_half)
    grad_audio = grad_audio + swap(grad_audio.astype(bf16), "yhi").astype(f32)
    grad_embed = unit_backward(audio_wide, audio_inverse, grad_audio).astype(bf16)
    grad_score = lax.psum_scatter(
        dot(coeffs, audio_unit, ((0,), (0,))).astype(bf16), "z", scatter_dimension=0, tiled=True
    ).astype(f32)
    score_grad = unit_backward(score_wide, score_inverse, grad_score)
    sums = backward_blocks([grad_embed], saved[0], down_head, None)
    fore = back = grad_embed
    for step in (1, 2, 3):
        fore, back = shift(fore, 1), shift(back, -1)
        sums = backward_blocks([back, fore], saved[step], down_head, sums)
    fore, back = shift(fore[:cut], 1), shift(back[cut:], -1)
    keep, give = backward_blocks(
        [fore, back], saved[4], down_head, sums, (core.astype(jnp.int32)[None], head_weight)
    )
    chip = add(keep, swap(give, "core"))
    landed = lax.all_to_all(chip, ("ylo", "x"), 0, 0)
    total = jnp.sum(landed.astype(f32), axis=0)
    ff = up_weight.shape[1]
    return (total[:, :ff], total[:, ff:].T, score_grad)


def solution(mesh):
    fine = Mesh(mesh.devices.reshape(2, 4, 2, 2, RING), ("ylo", "x", "core", "yhi", "z"))
    in_specs = (
        P(AUDIO, None),
        P(None, SCORE),
        P(SCORE, None),
        P(),
        P(AUDIO + SCORE, None),
        P(AUDIO, None),
    )
    out_specs = (P(AUDIO, SCORE), P(SCORE, AUDIO), P(AUDIO + SCORE, None))
    return jax.shard_map(
        per_device, mesh=fine, in_specs=in_specs, out_specs=out_specs, check_vma=False
    )
```

```python
import functools

import jax
import jax.numpy as jnp
from jax import lax
from jax.experimental import pallas as pl
from jax.experimental.pallas import tpu as pltpu
from jax.sharding import Mesh, PartitionSpec as P

logit_scale = 8.0
logit_bias = -3.0
epsilon = 1e-06
gelu_root = 0.7978845608028654
gelu_cubic = 0.044715

AUDIO = ("ylo", "x", "core")
SCORE = ("yhi", "z")
RING = 8
VMEM_BYTES = 20 * 1024 * 1024
f32 = jnp.float32
bf16 = jnp.bfloat16


def dot(left, right, dims=((1,), (0,))):
    return lax.dot_general(left, right, (dims, ((), ())), preferred_element_type=f32)


def unit_rows(values):
    wide = values.astype(f32)
    inverse = lax.rsqrt(jnp.sum(wide * wide, axis=-1, keepdims=True) + epsilon)
    return (wide * inverse, inverse)


def unit_backward(unit_wide, inverse, grad_unit):
    inner = jnp.sum(unit_wide * grad_unit, axis=-1, keepdims=True)
    return inverse * (grad_unit - unit_wide * inner)


def pair_coeffs(left, right, partner, first_column):
    logits = logit_scale * dot(left, right, ((1,), (1,))) + logit_bias
    columns = first_column + lax.iota(jnp.int32, right.shape[0])
    sign = jnp.where(partner[:, None] == columns[None, :], 1.0, -1.0)
    return (-logit_scale * sign * jax.nn.sigmoid(-sign * logits)).astype(bf16)


def swap(value, axis):
    return lax.ppermute(value, axis, [(0, 1), (1, 0)])


def shift(value, step):
    return lax.ppermute(value, "z", [(i, (i + step) % RING) for i in range(RING)])


def forward_kernel(index_ref, hidden_ref, up_ref, down_head_ref, part_ref, normed_t_ref, act_t_ref, slope_ref):
    wide = hidden_ref[...].astype(f32)
    square_mean = jnp.mean(wide * wide, axis=-1, keepdims=True)
    normed = wide * lax.rsqrt(square_mean + epsilon)
    normed_t_ref[...] = normed.T.astype(bf16)
    pre = dot(normed.astype(bf16), up_ref[...], ((1,), (1,)))
    tangent = jnp.tanh(gelu_root * (pre + gelu_cubic * (pre * pre * pre)))
    act = 0.5 * pre * (1.0 + tangent)
    slope_ref[...] = 0.5 * (1.0 + tangent) + 0.5 * pre * (1.0 - tangent * tangent) * gelu_root * (
        1.0 + 3.0 * gelu_cubic * pre * pre
    )
    act_t_ref[...] = act.T.astype(bf16)
    part_ref[...] = dot(act.astype(bf16), down_head_ref[...]).astype(bf16)


def forward_blocks(offsets, position, hidden_in, up_t, down_head):
    count = len(offsets)
    rows = hidden_in.shape[0] // RING
    ff, width = up_t.shape
    embed = down_head.shape[1]
    index = lax.rem(position + jnp.array([o % RING for o in offsets], jnp.int32), RING)
    return pl.pallas_call(
        forward_kernel,
        grid_spec=pltpu.PrefetchScalarGridSpec(
            num_scalar_prefetch=1,
            grid=(count,),
            in_specs=[
                pl.BlockSpec((rows, width), lambda i, index: (index[i], 0)),
                pl.BlockSpec((ff, width), lambda i, index: (0, 0)),
                pl.BlockSpec((ff, embed), lambda i, index: (0, 0)),
            ],
            out_specs=[
                pl.BlockSpec((rows, embed), lambda i, index: (i, 0)),
                pl.BlockSpec((width, rows), lambda i, index: (0, i)),
                pl.BlockSpec((ff, rows), lambda i, index: (0, i)),
                pl.BlockSpec((rows, ff), lambda i, index: (i, 0)),
            ],
        ),
        out_shape=[
            jax.ShapeDtypeStruct((count * rows, embed), bf16),
            jax.ShapeDtypeStruct((width, count * rows), bf16),
            jax.ShapeDtypeStruct((ff, count * rows), bf16),
            jax.ShapeDtypeStruct((count * rows, ff), f32),
        ],
        compiler_params=pltpu.CompilerParams(vmem_limit_bytes=VMEM_BYTES),
        cost_estimate=pl.CostEstimate(
            flops=2 * count * rows * ff * (width + embed),
            bytes_accessed=2 * count * rows * (2 * width + embed + 3 * ff) + 2 * ff * (width + embed),
            transcendentals=count * rows * ff,
        ),
    )(index, hidden_in, up_t, down_head)


def backward_kernel(pieces, first, last, *refs):
    grads = refs[:pieces]
    down_head_ref, normed_t_ref, act_t_ref, slope_ref = refs[pieces : pieces + 4]
    rest = refs[pieces + 4 :]
    if not first:
        up_in, act_in = rest[:2]
        rest = rest[2:]
    if last:
        core_ref, head_ref, keep_ref, give_ref, up_acc, act_acc = rest
    else:
        up_acc, act_acc = rest
    tile = 256
    start = 0
    grad_pre = []
    for grad_ref in grads:
        count = grad_ref.shape[0]
        grad_act = dot(grad_ref[...], down_head_ref[...], ((1,), (1,)))
        grad_pre.append((grad_act * slope_ref[start : start + count, :]).astype(bf16))
        start += count
    start = 0
    act_sum = None
    for grad_ref in grads:
        count = grad_ref.shape[0]
        term = dot(act_t_ref[:, start : start + count], grad_ref[...])
        act_sum = term if act_sum is None else act_sum + term
        start += count
    if not first:
        act_sum = act_sum + act_in[...]
    act_acc[...] = act_sum
    grad_pre = jnp.concatenate(grad_pre, axis=0) if len(grad_pre) > 1 else grad_pre[0]

    for m in range(0, up_acc.shape[0], tile):
        up_sum = dot(normed_t_ref[m : m + tile, :], grad_pre)
        if not first:
            up_sum = up_sum + up_in[m : m + tile, :]
        up_acc[m : m + tile, :] = up_sum
    if last:
        core = core_ref[0]
        ff = up_acc.shape[1]
        act_grad = act_acc[...].astype(bf16)
        act_acc_rows = keep_ref.shape[1]
        for half, out_ref in ((core, keep_ref), (1 - core, give_ref)):
            for chip in range(keep_ref.shape[0]):
                at = pl.multiple_of((2 * chip + half) * act_acc_rows, act_acc_rows)
                out_ref[chip, :, :ff] = up_acc[pl.ds(at, act_acc_rows), :].astype(bf16)
        for m in range(0, up_acc.shape[0], tile):
            up_acc[m : m + tile, :] = dot(head_ref[m : m + tile, :], act_grad, ((1,), (1,)))
        for half, out_ref in ((core, keep_ref), (1 - core, give_ref)):
            for chip in range(keep_ref.shape[0]):
                at = pl.multiple_of((2 * chip + half) * act_acc_rows, act_acc_rows)
                out_ref[chip, :, ff:] = up_acc[pl.ds(at, act_acc_rows), :].astype(bf16)


def backward_blocks(grads, saved, down_head, sums, last=None):
    _, normed_t, act_t, slope = saved
    width, rows = normed_t.shape
    ff, embed = down_head.shape
    args = list(grads) + [down_head, normed_t, act_t, slope]
    specs = [pl.BlockSpec(memory_space=pltpu.VMEM)] * len(args)
    aliases = {}
    if sums is not None:
        if last is None:
            aliases = {len(args): 0, len(args) + 1: 1}
        args += list(sums)
        specs += [pl.BlockSpec(memory_space=pltpu.VMEM)] * 2
    flops = 2 * rows * ff * (2 * embed + width)
    if last is None:
        shapes = [jax.ShapeDtypeStruct((width, ff), f32), jax.ShapeDtypeStruct((ff, embed), f32)]
        scratch = []
    else:
        args += list(last)
        specs += [pl.BlockSpec(memory_space=pltpu.SMEM), pl.BlockSpec(memory_space=pltpu.VMEM)]
        shapes = [jax.ShapeDtypeStruct((8, width // 16, 2 * ff), bf16)] * 2
        scratch = [pltpu.VMEM((width, ff), f32), pltpu.VMEM((ff, embed), f32)]
        flops += 2 * width * ff * embed
    return pl.pallas_call(
        functools.partial(backward_kernel, len(grads), sums is None, last is not None),
        in_specs=specs,
        out_specs=[pl.BlockSpec(memory_space=pltpu.VMEM)] * 2,
        out_shape=shapes,
        scratch_shapes=scratch,
        input_output_aliases=aliases,
        compiler_params=pltpu.CompilerParams(vmem_limit_bytes=VMEM_BYTES),
        cost_estimate=pl.CostEstimate(
            flops=flops, bytes_accessed=8 * 1024 * 1024, transcendentals=0
        ),
    )(*args)


def add(left, right):
    return (left.astype(f32) + right.astype(f32)).astype(bf16)


def per_device(hidden_in, up_weight, down_weight, head_weight, score_embed, pair_index):
    y_hi, z, core = lax.axis_index("yhi"), lax.axis_index("z"), lax.axis_index("core")
    own_rows = hidden_in.shape[0] // RING
    cut = own_rows // 2
    group_half = hidden_in.shape[0] // 2
    score_wide, score_inverse = unit_rows(score_embed)
    score_half = lax.all_gather(score_wide.astype(bf16), "z", axis=0, tiled=True)
    down_head = dot(down_weight, head_weight).astype(bf16)
    saved = {}
    up_t = up_weight.T
    run = lambda *offsets: forward_blocks(offsets, z, hidden_in, up_t, down_head)
    saved[4] = run(4)
    part = saved[4][0]
    fore, back = shift(part[:cut], 1), shift(part[cut:], -1)
    saved[3] = run(3, -3)
    ahead, behind = saved[3][0][:own_rows], saved[3][0][own_rows:]
    fore = jnp.concatenate([add(fore, ahead[:cut]), ahead[cut:]], axis=0)
    back = jnp.concatenate([behind[:cut], add(back, behind[cut:])], axis=0)
    for step in (2, 1):
        fore, back = shift(fore, 1), shift(back, -1)
        saved[step] = run(step, -step)
        fore = add(fore, saved[step][0][:own_rows])
        back = add(back, saved[step][0][own_rows:])
    fore, back = shift(fore, 1), shift(back, -1)
    saved[0] = run(0)
    summed = (fore.astype(f32) + back.astype(f32) + saved[0][0].astype(f32)).astype(bf16)
    own_hidden = lax.dynamic_slice_in_dim(hidden_in, z * own_rows, own_rows, 0)
    own_proj = dot(own_hidden, head_weight)
    audio_proj = own_proj + (summed.astype(f32) + swap(summed, "yhi").astype(f32))
    audio_wide, audio_inverse = unit_rows(audio_proj)
    audio_unit = audio_wide.astype(bf16)
    partners = lax.dynamic_slice_in_dim(pair_index[0], z * own_rows, own_rows, 0)
    coeffs = pair_coeffs(audio_unit, score_half, partners, y_hi * group_half)
    grad_audio = dot(coeffs, score_half)
    grad_audio = grad_audio + swap(grad_audio.astype(bf16), "yhi").astype(f32)
    grad_embed = unit_backward(audio_wide, audio_inverse, grad_audio).astype(bf16)
    score_part = dot(coeffs, audio_unit, ((0,), (0,))).astype(bf16)
    fore = back = grad_embed
    arrived, saved_at = [grad_embed], 0
    sums = None
    for step in (1, 2, 3, 4):
        if step < 4:
            fore, back = shift(fore, 1), shift(back, -1)
        else:
            fore, back = shift(fore[:cut], 1), shift(back[cut:], -1)
        sums = backward_blocks(arrived, saved[saved_at], down_head, sums)
        fore, back, sums = lax.optimization_barrier((fore, back, sums))
        if step == 2:
            fore, back, score_part = lax.optimization_barrier((fore, back, score_part))
            grad_score = lax.psum_scatter(score_part, "z", scatter_dimension=0, tiled=True)
        arrived, saved_at = [back, fore], step
    keep, give = backward_blocks(
        [fore, back], saved[4], down_head, sums, (core.astype(jnp.int32)[None], head_weight)
    )
    score_grad = unit_backward(score_wide, score_inverse, grad_score.astype(f32))
    chip = add(keep, swap(give, "core"))
    landed = lax.all_to_all(chip, ("ylo", "x"), 0, 0)
    total = jnp.sum(landed.astype(f32), axis=0)
    ff = up_weight.shape[1]
    return (total[:, :ff], total[:, ff:].T, score_grad)


def solution(mesh):
    fine = Mesh(mesh.devices.reshape(2, 4, 2, 2, RING), ("ylo", "x", "core", "yhi", "z"))
    in_specs = (
        P(AUDIO, None),
        P(None, SCORE),
        P(SCORE, None),
        P(),
        P(AUDIO + SCORE, None),
        P(AUDIO, None),
    )
    out_specs = (P(AUDIO, SCORE), P(SCORE, AUDIO), P(AUDIO + SCORE, None))
    return jax.shard_map(
        per_device, mesh=fine, in_specs=in_specs, out_specs=out_specs, check_vma=False
    )
```

```python
import functools

import jax
import jax.numpy as jnp
from jax import lax
from jax.experimental import pallas as pl
from jax.experimental.pallas import tpu as pltpu
from jax.sharding import Mesh, PartitionSpec as P

logit_scale = 8.0
logit_bias = -3.0
epsilon = 1e-06
gelu_root = 0.7978845608028654
gelu_cubic = 0.044715

AUDIO = ("ylo", "x", "core")
SCORE = ("yhi", "z")
RING = 8
VMEM_BYTES = 56 * 1024 * 1024
f32 = jnp.float32
bf16 = jnp.bfloat16


def dot(left, right, dims=((1,), (0,))):
    return lax.dot_general(left, right, (dims, ((), ())), preferred_element_type=f32)


def unit_rows(values):
    wide = values.astype(f32)
    inverse = lax.rsqrt(jnp.sum(wide * wide, axis=-1, keepdims=True) + epsilon)
    return (wide * inverse, inverse)


def unit_backward(unit_wide, inverse, grad_unit):
    inner = jnp.sum(unit_wide * grad_unit, axis=-1, keepdims=True)
    return inverse * (grad_unit - unit_wide * inner)


def pair_coeffs(left, right, partner, columns):
    logits = logit_scale * dot(left, right, ((1,), (1,))) + logit_bias
    sign = jnp.where(partner[:, None] == columns[None, :], 1.0, -1.0)
    return (-logit_scale * sign * jax.nn.sigmoid(-sign * logits)).astype(bf16)


def swap(value, axis):
    return lax.ppermute(value, axis, [(0, 1), (1, 0)])


def shift(value, step):
    perm = [(i, (i + step) % RING) for i in range(RING)]
    perm += [(RING + i, RING + (i - step) % RING) for i in range(RING)]
    return lax.ppermute(value, ("core", "z"), perm)


GROUPS = (
    ((1, 4),),
    ((1, 3), (1, -3), (0, 4)),
    ((1, 2), (1, -2), (0, 3), (0, -3)),
    ((1, 1), (1, -1), (0, 2), (0, -2)),
    ((1, 0), (0, 1), (0, -1), (0, 0)),
)
BLOCKS = tuple(block for group in GROUPS for block in group)


def block_index(half, place, direction):
    halves = jnp.array([block[0] for block in BLOCKS], jnp.int32)
    offsets = jnp.array([block[1] for block in BLOCKS], jnp.int32)
    return lax.rem(half + halves, 2) * RING + lax.rem(place + direction * offsets + RING, RING)


def forward_kernel(others, index_ref, hidden_ref, up_ref, down_head_ref, *outs):
    normed_t_ref, act_t_ref, slope_ref = outs[-3:]
    wide = hidden_ref[...].astype(f32)
    square_mean = jnp.mean(wide * wide, axis=-1, keepdims=True)
    normed = wide * lax.rsqrt(square_mean + epsilon)
    normed_t_ref[0] = normed.T.astype(bf16)
    pre = dot(normed.astype(bf16), up_ref[...], ((1,), (1,)))
    tangent = jnp.tanh(gelu_root * (pre + gelu_cubic * (pre * pre * pre)))
    act = 0.5 * pre * (1.0 + tangent)
    slope_ref[0] = 0.5 * (1.0 + tangent) + 0.5 * pre * (1.0 - tangent * tangent) * gelu_root * (
        1.0 + 3.0 * gelu_cubic * pre * pre
    )
    act_t_ref[0] = act.T.astype(bf16)
    part = dot(act.astype(bf16), down_head_ref[...]).astype(bf16)
    if len(outs) == 4:
        outs[0][...] = part
    else:
        step = pl.program_id(0)

        @pl.when(step < others)
        def _():
            outs[0][...] = part

        @pl.when(step >= others)
        def _():
            outs[1][...] = part


def forward_blocks(group, index, hidden_in, up_t, down_head):
    members = GROUPS[group]
    first = sum(len(g) for g in GROUPS[:group])
    count = len(members)
    others = sum(half for half, _ in members)
    rows = hidden_in.shape[0] // (2 * RING)
    ff, width = up_t.shape
    embed = down_head.shape[1]
    part_specs = [pl.BlockSpec((rows, embed), lambda i, index: (jnp.minimum(i, others - 1), 0))]
    part_shapes = [jax.ShapeDtypeStruct((others * rows, embed), bf16)]
    if count > others:
        part_specs.append(pl.BlockSpec((rows, embed), lambda i, index: (jnp.maximum(i - others, 0), 0)))
        part_shapes.append(jax.ShapeDtypeStruct(((count - others) * rows, embed), bf16))
    out = pl.pallas_call(
        functools.partial(forward_kernel, others),
        grid_spec=pltpu.PrefetchScalarGridSpec(
            num_scalar_prefetch=1,
            grid=(count,),
            in_specs=[
                pl.BlockSpec((rows, width), lambda i, index: (index[first + i], 0)),
                pl.BlockSpec((ff, width), lambda i, index: (0, 0)),
                pl.BlockSpec((ff, embed), lambda i, index: (0, 0)),
            ],
            out_specs=part_specs
            + [
                pl.BlockSpec((1, width, rows), lambda i, index: (i, 0, 0)),
                pl.BlockSpec((1, ff, rows), lambda i, index: (i, 0, 0)),
                pl.BlockSpec((1, rows, ff), lambda i, index: (i, 0, 0)),
            ],
        ),
        out_shape=part_shapes
        + [
            jax.ShapeDtypeStruct((count, width, rows), bf16),
            jax.ShapeDtypeStruct((count, ff, rows), bf16),
            jax.ShapeDtypeStruct((count, rows, ff), f32),
        ],
        compiler_params=pltpu.CompilerParams(vmem_limit_bytes=VMEM_BYTES),
        cost_estimate=pl.CostEstimate(
            flops=2 * count * rows * ff * (width + embed),
            bytes_accessed=2 * count * rows * (2 * width + embed + 3 * ff) + 2 * ff * (width + embed),
            transcendentals=count * rows * ff,
        ),
    )(index, hidden_in, up_t, down_head)
    return out[0], out[1] if count > others else None, out[-3:]


def backward_kernel(count, first, last, *refs):
    grads = [ref[...] for ref in refs[:count]]
    normed_t = [ref[0] for ref in refs[count : 4 * count : 3]]
    act_t = [ref[0] for ref in refs[count + 1 : 4 * count : 3]]
    slope = [ref[0] for ref in refs[count + 2 : 4 * count : 3]]
    join = lambda parts, axis: jnp.concatenate(parts, axis=axis) if count > 1 else parts[0]
    grad, normed_t, act_t, slope = join(grads, 0), join(normed_t, 1), join(act_t, 1), join(slope, 0)
    down_head_ref = refs[4 * count]
    rest = refs[4 * count + 1 :]
    if not first:
        up_in, act_in = rest[:2]
        rest = rest[2:]
    if last:
        core_ref, head_ref, keep_ref, give_ref, up_acc, act_acc = rest
    else:
        up_acc, act_acc = rest
    tile = 256
    width, ff = up_acc.shape
    grad_act = dot(grad, down_head_ref[...], ((1,), (1,)))
    grad_pre = (grad_act * slope).astype(bf16)
    act_sum = dot(act_t, grad)
    if not first:
        act_sum = act_sum + act_in[...]
    if not last:
        act_acc[...] = act_sum
    for m in range(0, width, tile):
        up_sum = dot(normed_t[m : m + tile, :], grad_pre)
        if not first:
            up_sum = up_sum + up_in[m : m + tile, :]
        up_acc[m : m + tile, :] = up_sum
    if last:
        core = core_ref[0]
        act_grad = act_sum.astype(bf16)
        rows = keep_ref.shape[1]
        for side in range(2):
            for half, out_ref in ((core, keep_ref), (1 - core, give_ref)):
                for chip in range(keep_ref.shape[0]):
                    at = pl.multiple_of((2 * chip + half) * rows, rows)
                    out_ref[chip, :, side * ff : (side + 1) * ff] = up_acc[pl.ds(at, rows), :].astype(bf16)
            if side == 0:
                for m in range(0, width, tile):
                    up_acc[m : m + tile, :] = dot(head_ref[m : m + tile, :], act_grad, ((1,), (1,)))


def backward_blocks(items, down_head, sums, last=None):
    whole = pl.BlockSpec(memory_space=pltpu.VMEM)
    args = [grad for grad, _, _ in items]
    specs = [whole] * len(items)
    for _, saved, at in items:
        for array in saved:
            args.append(array)
            specs.append(pl.BlockSpec((1,) + array.shape[1:], lambda i, at=at: (at, 0, 0)))
    ff, embed = down_head.shape
    rows, width = items[0][0].shape[0], items[0][1][0].shape[1]
    args.append(down_head)
    specs.append(whole)
    aliases = {}
    if sums is not None:
        if last is None:
            aliases = {len(args): 0, len(args) + 1: 1}
        args += list(sums)
        specs += [whole] * 2
    flops = 2 * len(items) * rows * ff * (2 * embed + width)
    if last is None:
        shapes = [jax.ShapeDtypeStruct((width, ff), f32), jax.ShapeDtypeStruct((ff, embed), f32)]
        scratch = []
    else:
        args += list(last)
        specs += [pl.BlockSpec(memory_space=pltpu.SMEM), whole]
        shapes = [jax.ShapeDtypeStruct((8, width // 16, 2 * ff), bf16)] * 2
        scratch = [pltpu.VMEM((width, ff), f32), pltpu.VMEM((ff, embed), f32)]
        flops += 2 * width * ff * embed
    return pl.pallas_call(
        functools.partial(backward_kernel, len(items), sums is None, last is not None),
        grid=(1,),
        in_specs=specs,
        out_specs=[whole] * 2,
        out_shape=shapes,
        scratch_shapes=scratch,
        input_output_aliases=aliases,
        compiler_params=pltpu.CompilerParams(vmem_limit_bytes=VMEM_BYTES),
        cost_estimate=pl.CostEstimate(flops=flops, bytes_accessed=8 * 1024 * 1024, transcendentals=0),
    )(*args)


def total_of(*terms):
    return sum(term.astype(f32) for term in terms)


def per_device(hidden_in, up_weight, down_weight, head_weight, score_embed, pair_index):
    y_hi, z, core = (lax.axis_index(name).astype(jnp.int32) for name in ("yhi", "z", "core"))
    rows = hidden_in.shape[0] // (2 * RING)
    group_half = RING * rows
    own_start = y_hi * group_half + z * rows
    score_wide, score_inverse = unit_rows(score_embed)
    score_unit = score_wide.astype(bf16)
    score_pair = jnp.concatenate([score_unit, swap(score_unit, "yhi")], axis=0)
    score_all = lax.all_gather(score_pair, "z", axis=0, tiled=True)
    down_head = dot(down_weight, head_weight).astype(bf16)
    up_t = up_weight.T
    index = block_index(y_hi, z, 1 - 2 * core)
    run = lambda group: forward_blocks(group, index, hidden_in, up_t, down_head)
    saved = {}

    def keep_saved(group, arrays):
        for at, block in enumerate(GROUPS[group]):
            saved[block] = (arrays, at)

    other, _, arrays = run(0)
    keep_saved(0, arrays)
    came = swap(other, "yhi")
    fore = back = None
    for group in range(1, len(GROUPS)):
        other, own, arrays = run(group)
        keep_saved(group, arrays)
        coming = swap(other, "yhi")
        if group == 1:
            fore = shift(total_of(own, came).astype(bf16), 1)
        elif group == 2:
            fore = total_of(own[:rows], came[:rows], fore).astype(bf16)
            back = total_of(own[rows:], came[rows:]).astype(bf16)
            fore, back = shift(fore, 1), shift(back, -1)
        else:
            fore = total_of(own[:rows], came[:rows], fore).astype(bf16)
            back = total_of(own[rows : 2 * rows], came[rows:], back).astype(bf16)
            fore, back = shift(fore, 1), shift(back, -1)
        came = coming
    mlp = total_of(own[2 * rows :], came, fore, back)
    own_hidden = lax.dynamic_slice_in_dim(hidden_in, own_start, rows, 0)
    audio_wide, audio_inverse = unit_rows(dot(own_hidden, head_weight) + mlp)
    audio_unit = audio_wide.astype(bf16)
    partners = lax.dynamic_slice_in_dim(pair_index[0], own_start, rows, 0)
    column = lax.iota(jnp.int32, score_all.shape[0])
    column_half = lax.rem(y_hi + lax.rem(column // rows, 2), 2)
    column = column_half * group_half + column // (2 * rows) * rows + lax.rem(column, rows)
    coeffs = pair_coeffs(audio_unit, score_all, partners, column)
    grad_embed = unit_backward(audio_wide, audio_inverse, dot(coeffs, score_all)).astype(bf16)
    score_part = dot(coeffs, audio_unit, ((0,), (0,))).astype(bf16)
    grad_pair = lax.psum_scatter(score_part, "z", scatter_dimension=0, tiled=True)
    item = lambda grad, half, offset: (grad,) + saved[(half, offset)]
    fore = back = grad_embed
    crossed = {0: swap(grad_embed, "yhi")}
    items = [item(grad_embed, 0, 0)]
    sums = None
    for step in (1, 2, 3, 4):
        if step < 4:
            fore, back = shift(fore, 1), shift(back, -1)
        else:
            fore, back = shift(fore, 1), None
        sums = backward_blocks(items, down_head, sums)
        if step < 4:
            fore, back, sums = lax.optimization_barrier((fore, back, sums))
            items = [item(back, 0, step), item(fore, 0, -step)]
        else:
            fore, sums = lax.optimization_barrier((fore, sums))
            items = [item(fore, 0, 4)]
        items += [item(grad, 1, offset) for offset, grad in crossed.items()]
        if step < 4:
            crossed = {step: swap(back, "yhi"), -step: swap(fore, "yhi")}
        else:
            crossed = swap(fore, "yhi")
    sums = backward_blocks(items, down_head, sums)
    crossed, sums = lax.optimization_barrier((crossed, sums))
    keep, give = backward_blocks([item(crossed, 1, 4)], down_head, sums, (core[None], head_weight))
    chip = total_of(keep, swap(give, "core")).astype(bf16)
    landed = lax.all_to_all(chip, ("ylo", "x"), 0, 0)
    total = jnp.sum(landed.astype(f32), axis=0)
    ff = up_weight.shape[1]
    grad_score = total_of(grad_pair[:rows], swap(grad_pair[rows:], "yhi"))
    score_grad = unit_backward(score_wide, score_inverse, grad_score)
    return (total[:, :ff], total[:, ff:].T, score_grad)


def solution(mesh):
    fine = Mesh(mesh.devices.reshape(2, 4, 2, 2, RING), ("ylo", "x", "core", "yhi", "z"))
    in_specs = (
        P(AUDIO, None),
        P(None, SCORE),
        P(SCORE, None),
        P(),
        P(AUDIO + SCORE, None),
        P(AUDIO, None),
    )
    out_specs = (P(AUDIO, SCORE), P(SCORE, AUDIO), P(AUDIO + SCORE, None))
    return jax.shard_map(
        per_device, mesh=fine, in_specs=in_specs, out_specs=out_specs, check_vma=False
    )
```

```python
import functools

import jax
import jax.numpy as jnp
from jax import lax
from jax.experimental import pallas as pl
from jax.experimental.pallas import tpu as pltpu
from jax.sharding import Mesh, PartitionSpec as P

logit_scale = 8.0
logit_bias = -3.0
epsilon = 1e-06
gelu_root = 0.7978845608028654
gelu_cubic = 0.044715

AUDIO = ("ylo", "x", "core")
SCORE = ("yhi", "z")
RING = 8
VMEM_BYTES = 56 * 1024 * 1024
f32 = jnp.float32
bf16 = jnp.bfloat16


def dot(left, right, dims=((1,), (0,))):
    return lax.dot_general(left, right, (dims, ((), ())), preferred_element_type=f32)


def unit_rows(values):
    wide = values.astype(f32)
    inverse = lax.rsqrt(jnp.sum(wide * wide, axis=-1, keepdims=True) + epsilon)
    return (wide * inverse, inverse)


def unit_backward(unit_wide, inverse, grad_unit):
    inner = jnp.sum(unit_wide * grad_unit, axis=-1, keepdims=True)
    return inverse * (grad_unit - unit_wide * inner)


def pair_coeffs(left, right, partner, first_column):
    logits = logit_scale * dot(left, right, ((1,), (1,))) + logit_bias
    columns = first_column + lax.iota(jnp.int32, right.shape[0])
    sign = jnp.where(partner[:, None] == columns[None, :], 1.0, -1.0)
    return (-logit_scale * sign * jax.nn.sigmoid(-sign * logits)).astype(bf16)


def swap(value, axis):
    return lax.ppermute(value, axis, [(0, 1), (1, 0)])


def shift(value, step):
    perm = [(i, (i + step) % RING) for i in range(RING)]
    perm += [(RING + i, RING + (i - step) % RING) for i in range(RING)]
    return lax.ppermute(value, ("core", "z"), perm)


def forward_kernel(first, index_ref, hidden_ref, up_ref, *refs):
    if first:
        down_ref, head_ref, part_ref, normed_t_ref, act_t_ref, slope_ref, down_head_ref = refs
        down_head_ref[...] = dot(down_ref[...], head_ref[...]).astype(bf16)
    else:
        down_head_ref, part_ref, normed_t_ref, act_t_ref, slope_ref = refs
    wide = hidden_ref[...].astype(f32)
    square_mean = jnp.mean(wide * wide, axis=-1, keepdims=True)
    normed = (wide * lax.rsqrt(square_mean + epsilon)).astype(bf16)
    pre = dot(normed, up_ref[...], ((1,), (1,)))
    tangent = jnp.tanh(gelu_root * (pre + gelu_cubic * (pre * pre * pre)))
    act = (0.5 * pre * (1.0 + tangent)).astype(bf16)
    part_ref[...] = dot(act, down_head_ref[...]).astype(bf16)
    slope = 0.5 * (1.0 + tangent) + 0.5 * pre * (1.0 - tangent * tangent) * gelu_root * (
        1.0 + 3.0 * gelu_cubic * pre * pre
    )
    slope_ref[...] = slope.astype(bf16)
    normed_t_ref[...] = normed.T
    act_t_ref[...] = act.T


def forward_blocks(offsets, place, direction, hidden_in, up_t, *weights):
    count = len(offsets)
    first = len(weights) == 2
    rows = hidden_in.shape[0] // RING
    ff, width = up_t.shape
    embed = weights[-1].shape[1]
    index = lax.rem(place + direction * jnp.array(offsets, jnp.int32) + RING, RING)
    weight_specs = [pl.BlockSpec(w.shape, lambda i, index: (0, 0)) for w in weights]
    extra_specs = [pl.BlockSpec((ff, embed), lambda i, index: (0, 0))] if first else []
    extra_shapes = [jax.ShapeDtypeStruct((ff, embed), bf16)] if first else []
    return pl.pallas_call(
        functools.partial(forward_kernel, first),
        grid_spec=pltpu.PrefetchScalarGridSpec(
            num_scalar_prefetch=1,
            grid=(count,),
            in_specs=[
                pl.BlockSpec((rows, width), lambda i, index: (index[i], 0)),
                pl.BlockSpec((ff, width), lambda i, index: (0, 0)),
            ]
            + weight_specs,
            out_specs=[
                pl.BlockSpec((rows, embed), lambda i, index: (i, 0)),
                pl.BlockSpec((width, rows), lambda i, index: (0, i)),
                pl.BlockSpec((ff, rows), lambda i, index: (0, i)),
                pl.BlockSpec((rows, ff), lambda i, index: (i, 0)),
            ]
            + extra_specs,
        ),
        out_shape=[
            jax.ShapeDtypeStruct((count * rows, embed), bf16),
            jax.ShapeDtypeStruct((width, count * rows), bf16),
            jax.ShapeDtypeStruct((ff, count * rows), bf16),
            jax.ShapeDtypeStruct((count * rows, ff), bf16),
        ]
        + extra_shapes,
        compiler_params=pltpu.CompilerParams(vmem_limit_bytes=VMEM_BYTES),
        cost_estimate=pl.CostEstimate(
            flops=2 * count * rows * ff * (width + embed),
            bytes_accessed=2 * count * rows * (2 * width + embed + 2 * ff) + 2 * ff * (width + embed),
            transcendentals=count * rows * ff,
        ),
    )(index, hidden_in, up_t, *weights)


def backward_kernel(count, first, last, *refs):
    grads = [ref[...] for ref in refs[:count]]
    down_head_ref = refs[count]
    refs = refs[count + 1 :]
    saved = []
    taken = 0
    while taken < count:
        saved.append([ref[...] for ref in refs[:3]])
        taken += saved[-1][2].shape[0] // grads[0].shape[0]
        refs = refs[3:]
    join = lambda parts, axis: jnp.concatenate(parts, axis=axis) if len(parts) > 1 else parts[0]
    grad = join(grads, 0)
    normed_t, act_t, slope = (join([kept[i] for kept in saved], axis) for i, axis in ((0, 1), (1, 1), (2, 0)))
    if not first:
        up_in, act_in = refs[:2]
        refs = refs[2:]
    if last:
        core_ref, head_ref, keep_ref, give_ref, up_acc = refs
    else:
        up_acc, act_acc = refs
    tile = 256
    width, ff = up_acc.shape
    grad_act = dot(grad, down_head_ref[...], ((1,), (1,)))
    grad_pre = (grad_act * slope.astype(f32)).astype(bf16)
    act_sum = dot(act_t, grad)
    if not first:
        act_sum = act_sum + act_in[...]
    if not last:
        act_acc[...] = act_sum
    for m in range(0, width, tile):
        up_sum = dot(normed_t[m : m + tile, :], grad_pre)
        if not first:
            up_sum = up_sum + up_in[m : m + tile, :]
        up_acc[m : m + tile, :] = up_sum
    if last:
        core = core_ref[0]
        act_grad = act_sum.astype(bf16)
        rows = keep_ref.shape[1]
        for side in range(2):
            for half, out_ref in ((core, keep_ref), (1 - core, give_ref)):
                for chip in range(keep_ref.shape[0]):
                    at = pl.multiple_of((2 * chip + half) * rows, rows)
                    out_ref[chip, :, side * ff : (side + 1) * ff] = up_acc[pl.ds(at, rows), :].astype(bf16)
            if side == 0:
                for m in range(0, width, tile):
                    up_acc[m : m + tile, :] = dot(head_ref[m : m + tile, :], act_grad, ((1,), (1,)))


def backward_blocks(grads, saved, down_head, sums, last=None):
    whole = pl.BlockSpec(memory_space=pltpu.VMEM)
    args = list(grads) + [down_head] + [array for kept in saved for array in kept]
    aliases = {}
    if sums is not None:
        if last is None:
            aliases = {len(args): 0, len(args) + 1: 1}
        args += list(sums)
    specs = [whole] * len(args)
    ff, embed = down_head.shape
    rows, width = sum(grad.shape[0] for grad in grads), saved[0][0].shape[0]
    flops = 2 * rows * ff * (2 * embed + width)
    if last is None:
        shapes = [jax.ShapeDtypeStruct((width, ff), f32), jax.ShapeDtypeStruct((ff, embed), f32)]
        scratch = []
    else:
        args += list(last)
        specs += [pl.BlockSpec(memory_space=pltpu.SMEM), whole]
        shapes = [jax.ShapeDtypeStruct((8, width // 16, 2 * ff), bf16)] * 2
        scratch = [pltpu.VMEM((width, ff), f32)]
        flops += 2 * width * ff * embed
    return pl.pallas_call(
        functools.partial(backward_kernel, len(grads), sums is None, last is not None),
        in_specs=specs,
        out_specs=[whole] * 2,
        out_shape=shapes,
        scratch_shapes=scratch,
        input_output_aliases=aliases,
        compiler_params=pltpu.CompilerParams(vmem_limit_bytes=VMEM_BYTES),
        cost_estimate=pl.CostEstimate(flops=flops, bytes_accessed=8 * 1024 * 1024, transcendentals=0),
    )(*args)


def total_of(*terms):
    return sum(term.astype(f32) for term in terms)


def per_device(hidden_in, up_weight, down_weight, head_weight, score_embed, pair_index):
    y_hi, z, core = (lax.axis_index(name).astype(jnp.int32) for name in ("yhi", "z", "core"))
    rows = hidden_in.shape[0] // RING
    group_half = hidden_in.shape[0] // 2
    direction = 1 - 2 * core
    up_t = up_weight.T
    part, *kept, down_head = forward_blocks((4,), z, direction, hidden_in, up_t, down_weight, head_weight)
    saved = {4: kept}
    fore = shift(part, 1)
    score_wide, score_inverse = unit_rows(score_embed)
    score_unit, up_t = lax.optimization_barrier((score_wide.astype(bf16), up_t))
    score_half = lax.all_gather(score_unit, "z", axis=0, tiled=True)
    back = None
    for step in (3, 2, 1):
        part, *saved[step] = forward_blocks((step, -step), z, direction, hidden_in, up_t, down_head)
        fore = total_of(fore, part[:rows]).astype(bf16)
        back = part[rows:] if back is None else total_of(back, part[rows:]).astype(bf16)
        fore, back = shift(fore, 1), shift(back, -1)
    part, *saved[0] = forward_blocks((0,), z, direction, hidden_in, up_t, down_head)
    own_hidden = lax.dynamic_slice_in_dim(hidden_in, z * rows, rows, 0)
    own_proj = dot(own_hidden, head_weight)
    summed = total_of(part, fore, back).astype(bf16)
    audio_proj = own_proj + total_of(summed, swap(summed, "yhi"))
    audio_wide, audio_inverse = unit_rows(audio_proj)
    audio_unit = audio_wide.astype(bf16)
    partners = lax.dynamic_slice_in_dim(pair_index[0], z * rows, rows, 0)
    coeffs = pair_coeffs(audio_unit, score_half, partners, y_hi * group_half)
    grad_audio = dot(coeffs, score_half)
    grad_audio = grad_audio + swap(grad_audio.astype(bf16), "yhi").astype(f32)
    grad_embed = unit_backward(audio_wide, audio_inverse, grad_audio).astype(bf16)
    score_part = dot(coeffs, audio_unit, ((0,), (0,))).astype(bf16)
    fore, back = shift(grad_embed, 1), shift(grad_embed, -1)
    grads, kept, sums = [grad_embed, back, fore], [saved[0], saved[1]], None
    for step in (2, 3, 4):
        fore, back = shift(fore, 1), shift(back, -1) if step < 4 else None
        sums = backward_blocks(grads, kept, down_head, sums)
        if step == 2:
            fore, back, sums, score_part = lax.optimization_barrier((fore, back, sums, score_part))
            grad_score = lax.psum_scatter(score_part, "z", scatter_dimension=0, tiled=True)
        elif step == 3:
            fore, back, sums = lax.optimization_barrier((fore, back, sums))
        else:
            fore, sums = lax.optimization_barrier((fore, sums))
        grads, kept = [back, fore], [saved[step]]
    keep, give = backward_blocks([fore], [saved[4]], down_head, sums, (core[None], head_weight))
    chip = total_of(keep, swap(give, "core")).astype(bf16)
    landed = lax.all_to_all(chip, ("ylo", "x"), 0, 0)
    total = jnp.sum(landed.astype(f32), axis=0)
    ff = up_weight.shape[1]
    score_grad = unit_backward(score_wide, score_inverse, grad_score.astype(f32))
    return (total[:, :ff], total[:, ff:].T, score_grad)


def solution(mesh):
    fine = Mesh(mesh.devices.reshape(2, 4, 2, 2, RING), ("ylo", "x", "core", "yhi", "z"))
    in_specs = (
        P(AUDIO, None),
        P(None, SCORE),
        P(SCORE, None),
        P(),
        P(AUDIO + SCORE, None),
        P(AUDIO, None),
    )
    out_specs = (P(AUDIO, SCORE), P(SCORE, AUDIO), P(AUDIO + SCORE, None))
    return jax.shard_map(
        per_device, mesh=fine, in_specs=in_specs, out_specs=out_specs, check_vma=False
    )
```

```python
import functools

import jax
import jax.numpy as jnp
from jax import lax
from jax.experimental import pallas as pl
from jax.experimental.pallas import tpu as pltpu
from jax.sharding import Mesh, PartitionSpec as P

logit_scale = 8.0
logit_bias = -3.0
epsilon = 1e-06
gelu_root = 0.7978845608028654
gelu_cubic = 0.044715

AUDIO = ("ylo", "x", "core")
SCORE = ("yhi", "z")
RING = 8
VMEM_BYTES = 56 * 1024 * 1024
f32 = jnp.float32
bf16 = jnp.bfloat16


def dot(left, right, dims=((1,), (0,))):
    return lax.dot_general(left, right, (dims, ((), ())), preferred_element_type=f32)


def unit_rows(values):
    wide = values.astype(f32)
    inverse = lax.rsqrt(jnp.sum(wide * wide, axis=-1, keepdims=True) + epsilon)
    return (wide * inverse, inverse)


def unit_backward(unit_wide, inverse, grad_unit):
    inner = jnp.sum(unit_wide * grad_unit, axis=-1, keepdims=True)
    return inverse * (grad_unit - unit_wide * inner)


def pair_coeffs(left, right, partner, first_column):
    logits = logit_scale * dot(left, right, ((1,), (1,))) + logit_bias
    columns = first_column + lax.iota(jnp.int32, right.shape[0])
    sign = jnp.where(partner[:, None] == columns[None, :], 1.0, -1.0)
    return (-logit_scale * sign * jax.nn.sigmoid(-sign * logits)).astype(bf16)


def swap(value, axis):
    return lax.ppermute(value, axis, [(0, 1), (1, 0)])


def shift(value, step):
    perm = [(i, (i + step) % RING) for i in range(RING)]
    perm += [(RING + i, RING + (i - step) % RING) for i in range(RING)]
    return lax.ppermute(value, ("core", "z"), perm)


def forward_kernel(count, index_ref, *refs):
    hidden = [ref[...] for ref in refs[:count]]
    up_ref, down_head_ref, part_ref, normed_t_ref, act_t_ref, slope_ref = refs[count:]
    rows = hidden[0].shape[0]
    wide = (jnp.concatenate(hidden, axis=0) if count > 1 else hidden[0]).astype(f32)
    square_mean = jnp.mean(wide * wide, axis=-1, keepdims=True)
    normed = (wide * lax.rsqrt(square_mean + epsilon)).astype(bf16)
    part = None
    for side in range(2):
        pre = dot(normed, up_ref[side], ((1,), (1,)))
        tangent = jnp.tanh(gelu_root * (pre + gelu_cubic * (pre * pre * pre)))
        act = (0.5 * pre * (1.0 + tangent)).astype(bf16)
        term = dot(act, down_head_ref[side])
        part = term if part is None else part + term
        slope = 0.5 * (1.0 + tangent) + 0.5 * pre * (1.0 - tangent * tangent) * gelu_root * (
            1.0 + 3.0 * gelu_cubic * pre * pre
        )
        slope = slope.astype(bf16)
        act_t = act.T
        for i in range(count):
            slope_ref[i, side] = slope[i * rows : (i + 1) * rows, :]
            act_t_ref[i, side] = act_t[:, i * rows : (i + 1) * rows]
    part_ref[...] = part.astype(bf16)
    normed_t = normed.T
    for i in range(count):
        normed_t_ref[i] = normed_t[:, i * rows : (i + 1) * rows]


def forward_blocks(offsets, half, place, direction, hidden_in, up_pair, down_head):
    count = len(offsets)
    rows = hidden_in.shape[0] // (2 * RING)
    _, ff, width = up_pair.shape
    embed = down_head.shape[2]
    index = half * RING + lax.rem(place + direction * jnp.array(offsets, jnp.int32) + RING, RING)
    out = pl.pallas_call(
        functools.partial(forward_kernel, count),
        grid_spec=pltpu.PrefetchScalarGridSpec(
            num_scalar_prefetch=1,
            grid=(1,),
            in_specs=[pl.BlockSpec((rows, width), lambda i, index, at=at: (index[at], 0)) for at in range(count)]
            + [
                pl.BlockSpec((2, ff, width), lambda i, index: (0, 0, 0)),
                pl.BlockSpec((2, ff, embed), lambda i, index: (0, 0, 0)),
            ],
            out_specs=[
                pl.BlockSpec((count * rows, embed), lambda i, index: (0, 0)),
                pl.BlockSpec((count, width, rows), lambda i, index: (0, 0, 0)),
                pl.BlockSpec((count, 2, ff, rows), lambda i, index: (0, 0, 0, 0)),
                pl.BlockSpec((count, 2, rows, ff), lambda i, index: (0, 0, 0, 0)),
            ],
        ),
        out_shape=[
            jax.ShapeDtypeStruct((count * rows, embed), bf16),
            jax.ShapeDtypeStruct((count, width, rows), bf16),
            jax.ShapeDtypeStruct((count, 2, ff, rows), bf16),
            jax.ShapeDtypeStruct((count, 2, rows, ff), bf16),
        ],
        compiler_params=pltpu.CompilerParams(vmem_limit_bytes=VMEM_BYTES),
        cost_estimate=pl.CostEstimate(
            flops=4 * count * rows * ff * (width + embed),
            bytes_accessed=2 * count * rows * (2 * width + embed + 4 * ff) + 4 * ff * (width + embed),
            transcendentals=2 * count * rows * ff,
        ),
    )(index, *([hidden_in] * count), up_pair, down_head)
    return [out[0][at * rows : (at + 1) * rows] for at in range(count)], out[1:]


def backward_kernel(count, first, last, *refs):
    join = lambda parts, axis: jnp.concatenate(parts, axis=axis) if count > 1 else parts[0]
    grad = join([ref[...] for ref in refs[:count]], 0)
    kept = refs[count : 4 * count]
    normed_t = join([ref[0] for ref in kept[0::3]], 1)
    down_head_ref = refs[4 * count]
    refs = refs[4 * count + 1 :]
    if not first:
        up_in, act_in = refs[:2]
        refs = refs[2:]
    if last:
        place_ref, head_ref, keep_ref, give_ref, up_acc = refs
        core, half = place_ref[0], place_ref[1]
    else:
        up_acc, act_acc = refs
    tile = 256
    _, width, ff = up_acc.shape
    for side in range(2):
        act_t = join([ref[0, side] for ref in kept[1::3]], 1)
        slope = join([ref[0, side] for ref in kept[2::3]], 0)
        grad_act = dot(grad, down_head_ref[side], ((1,), (1,)))
        grad_pre = (grad_act * slope.astype(f32)).astype(bf16)
        act_sum = dot(act_t, grad)
        if not first:
            act_sum = act_sum + act_in[side]
        if not last:
            act_acc[side] = act_sum
        for m in range(0, width, tile):
            up_sum = dot(normed_t[m : m + tile, :], grad_pre)
            if not first:
                up_sum = up_sum + up_in[side, m : m + tile, :]
            up_acc[side, m : m + tile, :] = up_sum
        if last:
            act_grad = act_sum.astype(bf16)
            rows = keep_ref.shape[1]
            slot = lax.rem(half + side, 2)
            for part in range(2):
                for which, out_ref in ((core, keep_ref), (1 - core, give_ref)):
                    for chip in range(keep_ref.shape[0] // 2):
                        at = pl.multiple_of((2 * chip + which) * rows, rows)
                        out_ref[2 * chip + slot, :, part * ff : (part + 1) * ff] = up_acc[
                            side, pl.ds(at, rows), :
                        ].astype(bf16)
                if part == 0:
                    for m in range(0, width, tile):
                        up_acc[side, m : m + tile, :] = dot(head_ref[m : m + tile, :], act_grad, ((1,), (1,)))


def backward_blocks(items, down_head, sums, last=None):
    whole = pl.BlockSpec(memory_space=pltpu.VMEM)
    args = [grad for grad, _, _ in items]
    specs = [whole] * len(items)
    for _, saved, at in items:
        for array in saved:
            args.append(array)
            zeros = (0,) * (array.ndim - 1)
            specs.append(pl.BlockSpec((1,) + array.shape[1:], lambda i, at=at, zeros=zeros: (at,) + zeros))
    _, ff, embed = down_head.shape
    rows, width = items[0][0].shape[0], items[0][1][0].shape[1]
    args.append(down_head)
    specs.append(whole)
    aliases = {}
    if sums is not None:
        if last is None:
            aliases = {len(args): 0, len(args) + 1: 1}
        args += list(sums)
        specs += [whole] * 2
    flops = 4 * len(items) * rows * ff * (2 * embed + width)
    if last is None:
        shapes = [jax.ShapeDtypeStruct((2, width, ff), f32), jax.ShapeDtypeStruct((2, ff, embed), f32)]
        scratch = []
    else:
        args += list(last)
        specs += [pl.BlockSpec(memory_space=pltpu.SMEM), whole]
        shapes = [jax.ShapeDtypeStruct((16, width // 16, 2 * ff), bf16)] * 2
        scratch = [pltpu.VMEM((2, width, ff), f32)]
        flops += 4 * width * ff * embed
    return pl.pallas_call(
        functools.partial(backward_kernel, len(items), sums is None, last is not None),
        grid=(1,),
        in_specs=specs,
        out_specs=[whole] * 2,
        out_shape=shapes,
        scratch_shapes=scratch,
        input_output_aliases=aliases,
        compiler_params=pltpu.CompilerParams(vmem_limit_bytes=VMEM_BYTES),
        cost_estimate=pl.CostEstimate(flops=flops, bytes_accessed=12 * 1024 * 1024, transcendentals=0),
    )(*args)


def total_of(*terms):
    return sum(term.astype(f32) for term in terms)


def from_partner(value, core):
    cut = value.shape[0] // 2
    mine = swap(lax.dynamic_slice_in_dim(value, core * cut, cut, 0), "yhi")
    other = swap(mine, "core")
    halves = [jnp.where(core == 0, mine, other), jnp.where(core == 0, other, mine)]
    return jnp.concatenate([value] + halves, axis=0).reshape((2,) + value.shape)


def per_device(hidden_in, up_weight, down_weight, head_weight, score_embed, pair_index):
    y_hi, z, core = (lax.axis_index(name).astype(jnp.int32) for name in ("yhi", "z", "core"))
    rows = hidden_in.shape[0] // (2 * RING)
    group_half = RING * rows
    direction = 1 - 2 * core
    up_pair = from_partner(up_weight.T, core)
    score_wide, score_inverse = unit_rows(score_embed)
    down_head, score_unit = lax.optimization_barrier(
        (dot(down_weight, head_weight).astype(bf16), score_wide.astype(bf16))
    )
    score_half = lax.all_gather(score_unit, "z", axis=0, tiled=True)
    down_head = from_partner(down_head, core)
    saved, parts = {}, {}

    def forward(*offsets):
        found, arrays = forward_blocks(offsets, y_hi, z, direction, hidden_in, up_pair, down_head)
        for at, offset in enumerate(offsets):
            parts[offset] = found[at]
            saved[offset] = (arrays, at)

    forward(4)
    fore, back = shift(parts[4], 1), None
    forward(3, -3)
    for step in (3, 2, 1):
        fore = total_of(fore, parts[step]).astype(bf16)
        back = parts[-step] if back is None else total_of(back, parts[-step]).astype(bf16)
        fore, back = shift(fore, 1), shift(back, -1)
        if step == 3:
            forward(2, -2, 1, -1, 0)
    own_start = y_hi * group_half + z * rows
    own_hidden = lax.dynamic_slice_in_dim(hidden_in, own_start, rows, 0)
    own_proj = dot(own_hidden, head_weight)
    audio_wide, audio_inverse = unit_rows(own_proj + total_of(parts[0], fore, back))
    audio_own = audio_wide.astype(bf16)
    audio_unit = jnp.concatenate([audio_own, swap(audio_own, "yhi")], axis=0)
    far_start = (1 - y_hi) * group_half + z * rows
    partners = jnp.concatenate(
        [lax.dynamic_slice_in_dim(pair_index[0], start, rows, 0) for start in (own_start, far_start)]
    )
    coeffs = pair_coeffs(audio_unit, score_half, partners, y_hi * group_half)
    grad_audio = dot(coeffs, score_half)
    grad_audio = grad_audio[:rows] + swap(grad_audio[rows:].astype(bf16), "yhi").astype(f32)
    grad_embed = unit_backward(audio_wide, audio_inverse, grad_audio).astype(bf16)
    score_part = dot(coeffs, audio_unit, ((0,), (0,))).astype(bf16)
    item = lambda grad, offset: (grad,) + saved[offset]
    items = [item(grad_embed, 0)]
    fore = back = grad_embed
    for step in (1, 2):
        fore, back = shift(fore, 1), shift(back, -1)
        items += [item(back, step), item(fore, -step)]
    fore, back, score_part = lax.optimization_barrier((fore, back, score_part))
    grad_score = lax.psum_scatter(score_part, "z", scatter_dimension=0, tiled=True)
    fore, back = shift(fore, 1), shift(back, -1)
    sums = backward_blocks(items, down_head, None)
    fore, back, sums = lax.optimization_barrier((fore, back, sums))
    items = [item(back, 3), item(fore, -3), item(shift(fore, 1), 4)]
    place = jnp.stack([core, y_hi])
    keep, give = backward_blocks(items, down_head, sums, (place, head_weight))
    chip = total_of(keep, swap(give, "core")).astype(bf16)
    landed = lax.all_to_all(chip, ("ylo", "x", "yhi"), 0, 0)
    total = jnp.sum(landed.astype(f32), axis=0)
    ff = up_weight.shape[1]
    score_grad = unit_backward(score_wide, score_inverse, grad_score.astype(f32))
    return (total[:, :ff], total[:, ff:].T, score_grad)


def solution(mesh):
    fine = Mesh(mesh.devices.reshape(2, 4, 2, 2, RING), ("ylo", "x", "core", "yhi", "z"))
    in_specs = (
        P(AUDIO, None),
        P(None, SCORE),
        P(SCORE, None),
        P(),
        P(AUDIO + SCORE, None),
        P(AUDIO, None),
    )
    out_specs = (P(AUDIO, SCORE), P(SCORE, AUDIO), P(AUDIO + SCORE, None))
    return jax.shard_map(
        per_device, mesh=fine, in_specs=in_specs, out_specs=out_specs, check_vma=False
    )
```

```python
import functools

import jax
import jax.numpy as jnp
from jax import lax
from jax.experimental import pallas as pl
from jax.experimental.pallas import tpu as pltpu
from jax.sharding import Mesh, PartitionSpec as P

logit_scale = 8.0
logit_bias = -3.0
epsilon = 1e-06
gelu_root = 0.7978845608028654
gelu_cubic = 0.044715

AUDIO = ("ylo", "x", "core")
SCORE = ("yhi", "z")
RING = 8
VMEM_BYTES = 56 * 1024 * 1024
f32 = jnp.float32
bf16 = jnp.bfloat16


def dot(left, right, dims=((1,), (0,))):
    return lax.dot_general(left, right, (dims, ((), ())), preferred_element_type=f32)


def unit_rows(values):
    wide = values.astype(f32)
    inverse = lax.rsqrt(jnp.sum(wide * wide, axis=-1, keepdims=True) + epsilon)
    return (wide * inverse, inverse)


def unit_backward(unit_wide, inverse, grad_unit):
    inner = jnp.sum(unit_wide * grad_unit, axis=-1, keepdims=True)
    return inverse * (grad_unit - unit_wide * inner)


def pair_coeffs(left, right, partner, first_column):
    logits = logit_scale * dot(left, right, ((1,), (1,))) + logit_bias
    columns = first_column + lax.iota(jnp.int32, right.shape[0])
    sign = jnp.where(partner[:, None] == columns[None, :], 1.0, -1.0)
    return (-logit_scale * sign * jax.nn.sigmoid(-sign * logits)).astype(bf16)


def swap(value, axis):
    return lax.ppermute(value, axis, [(0, 1), (1, 0)])


def shift(value, step):
    perm = [(i, (i + step) % RING) for i in range(RING)]
    perm += [(RING + i, RING + (i - step) % RING) for i in range(RING)]
    return lax.ppermute(value, ("core", "z"), perm)


GROUPS = (
    (((1, 4),), ((1, 3), (1, -3)), ((0, 4),)),
    (((1, 2), (1, -2)), ((0, 3), (0, -3))),
    (((1, 1), (1, -1), (1, 0)), ((0, 2), (0, -2))),
    (((0, 1), (0, -1), (0, 0)),),
)
MEMBERS = tuple(tuple(block for piece in group for block in piece) for group in GROUPS)
BLOCKS = tuple(block for members in MEMBERS for block in members)


def block_index(half, place, direction):
    halves = jnp.array([block[0] for block in BLOCKS], jnp.int32)
    offsets = jnp.array([block[1] for block in BLOCKS], jnp.int32)
    return lax.rem(half + halves, 2) * RING + lax.rem(place + direction * offsets + RING, RING)


def forward_kernel(pieces, first, index_ref, *refs):
    count = sum(pieces)
    hidden = [ref[...] for ref in refs[:count]]
    refs = refs[count:]
    if first:
        up_ref, down_ref, head_ref = refs[:3]
        down_head_ref = refs[-1]
        down_head_ref[...] = dot(down_ref[...], head_ref[...]).astype(bf16)
        refs = refs[3:-1]
    else:
        up_ref, down_head_ref = refs[:2]
        refs = refs[2:]
    part_refs = refs[: len(pieces)]
    normed_t_ref, act_t_ref, slope_ref = refs[len(pieces) :]
    rows = hidden[0].shape[0]
    wide = jnp.concatenate(hidden, axis=0).astype(f32)
    square_mean = jnp.mean(wide * wide, axis=-1, keepdims=True)
    normed = (wide * lax.rsqrt(square_mean + epsilon)).astype(bf16)
    pre = dot(normed, up_ref[...], ((1,), (1,)))
    tangent = jnp.tanh(gelu_root * (pre + gelu_cubic * (pre * pre * pre)))
    act = (0.5 * pre * (1.0 + tangent)).astype(bf16)
    part = dot(act, down_head_ref[...]).astype(bf16)
    at = 0
    for size, part_ref in zip(pieces, part_refs):
        part_ref[...] = part[at * rows : (at + size) * rows, :]
        at += size
    slope = 0.5 * (1.0 + tangent) + 0.5 * pre * (1.0 - tangent * tangent) * gelu_root * (
        1.0 + 3.0 * gelu_cubic * pre * pre
    )
    slope = slope.astype(bf16)
    normed_t, act_t = normed.T, act.T
    for i in range(count):
        span = slice(i * rows, (i + 1) * rows)
        slope_ref[i] = slope[span, :]
        normed_t_ref[i] = normed_t[:, span]
        act_t_ref[i] = act_t[:, span]


def forward_blocks(group, index, hidden_in, up_t, *weights):
    pieces = tuple(len(piece) for piece in GROUPS[group])
    count = sum(pieces)
    start = sum(len(members) for members in MEMBERS[:group])
    first = len(weights) == 2
    rows = hidden_in.shape[0] // (2 * RING)
    ff, width = up_t.shape
    embed = weights[-1].shape[1]
    flat = lambda i, index: (0, 0)
    cube = lambda i, index: (0, 0, 0)
    shapes = [jax.ShapeDtypeStruct((size * rows, embed), bf16) for size in pieces]
    shapes += [jax.ShapeDtypeStruct((count,) + dims, bf16) for dims in ((width, rows), (ff, rows), (rows, ff))]
    shapes += [jax.ShapeDtypeStruct((ff, embed), bf16)] if first else []
    out = pl.pallas_call(
        functools.partial(forward_kernel, pieces, first),
        grid_spec=pltpu.PrefetchScalarGridSpec(
            num_scalar_prefetch=1,
            grid=(1,),
            in_specs=[
                pl.BlockSpec((rows, width), lambda i, index, at=start + at: (index[at], 0)) for at in range(count)
            ]
            + [pl.BlockSpec(w.shape, flat) for w in (up_t,) + weights],
            out_specs=[pl.BlockSpec(shape.shape, cube if len(shape.shape) == 3 else flat) for shape in shapes],
        ),
        out_shape=shapes,
        compiler_params=pltpu.CompilerParams(vmem_limit_bytes=VMEM_BYTES),
        cost_estimate=pl.CostEstimate(
            flops=2 * count * rows * ff * (width + embed),
            bytes_accessed=2 * count * rows * (2 * width + embed + 2 * ff) + 2 * ff * (width + embed),
            transcendentals=count * rows * ff,
        ),
    )(index, *([hidden_in] * count), up_t, *weights)
    parts, kept = out[: len(pieces)], out[len(pieces) : len(pieces) + 3]
    return parts, kept, out[-1]


def backward_kernel(count, blocks, first, last, *refs):
    join = lambda parts, axis: jnp.concatenate(parts, axis=axis) if len(parts) > 1 else parts[0]
    grad = join([ref[...] for ref in refs[:count]], 0)
    kept = refs[count : count + 3 * blocks]
    normed_t, act_t, slope = (join([ref[0] for ref in kept[i::3]], axis) for i, axis in ((0, 1), (1, 1), (2, 0)))
    refs = refs[count + 3 * blocks :]
    down_head_ref, refs = refs[0], refs[1:]
    if not first:
        up_in, act_in = refs[:2]
        refs = refs[2:]
    if last:
        core_ref, head_ref, keep_ref, give_ref, up_acc = refs
    else:
        up_acc, act_acc = refs
    tile = 256
    width, ff = up_acc.shape
    grad_act = dot(grad, down_head_ref[...], ((1,), (1,)))
    grad_pre = (grad_act * slope.astype(f32)).astype(bf16)
    act_sum = dot(act_t, grad)
    if not first:
        act_sum = act_sum + act_in[...]
    if not last:
        act_acc[...] = act_sum
    for m in range(0, width, tile):
        up_sum = dot(normed_t[m : m + tile, :], grad_pre)
        if not first:
            up_sum = up_sum + up_in[m : m + tile, :]
        up_acc[m : m + tile, :] = up_sum
    if last:
        core = core_ref[0]
        act_grad = act_sum.astype(bf16)
        rows = keep_ref.shape[1]
        for side in range(2):
            for half, out_ref in ((core, keep_ref), (1 - core, give_ref)):
                for chip in range(keep_ref.shape[0]):
                    at = pl.multiple_of((2 * chip + half) * rows, rows)
                    out_ref[chip, :, side * ff : (side + 1) * ff] = up_acc[pl.ds(at, rows), :].astype(bf16)
            if side == 0:
                for m in range(0, width, tile):
                    up_acc[m : m + tile, :] = dot(head_ref[m : m + tile, :], act_grad, ((1,), (1,)))


def backward_blocks(items, down_head, sums, last=None):
    whole = pl.BlockSpec(memory_space=pltpu.VMEM)
    args = [grad for grad, _ in items]
    specs = [whole] * len(items)
    places = [place for _, blocks in items for place in blocks]
    for kept, at in places:
        for array in kept:
            args.append(array)
            specs.append(pl.BlockSpec((1,) + array.shape[1:], lambda i, at=at: (at, 0, 0)))
    ff, embed = down_head.shape
    rows, width = sum(grad.shape[0] for grad, _ in items), places[0][0][0].shape[1]
    args.append(down_head)
    specs.append(whole)
    aliases = {}
    if sums is not None:
        if last is None:
            aliases = {len(args): 0, len(args) + 1: 1}
        args += list(sums)
        specs += [whole] * 2
    flops = 2 * rows * ff * (2 * embed + width)
    if last is None:
        shapes = [jax.ShapeDtypeStruct((width, ff), f32), jax.ShapeDtypeStruct((ff, embed), f32)]
        scratch = []
    else:
        args += list(last)
        specs += [pl.BlockSpec(memory_space=pltpu.SMEM), whole]
        shapes = [jax.ShapeDtypeStruct((8, width // 16, 2 * ff), bf16)] * 2
        scratch = [pltpu.VMEM((width, ff), f32)]
        flops += 2 * width * ff * embed
    return pl.pallas_call(
        functools.partial(backward_kernel, len(items), len(places), sums is None, last is not None),
        grid=(1,),
        in_specs=specs,
        out_specs=[whole] * 2,
        out_shape=shapes,
        scratch_shapes=scratch,
        input_output_aliases=aliases,
        compiler_params=pltpu.CompilerParams(vmem_limit_bytes=VMEM_BYTES),
        cost_estimate=pl.CostEstimate(flops=flops, bytes_accessed=8 * 1024 * 1024, transcendentals=0),
    )(*args)


def total_of(*terms):
    return sum(term.astype(f32) for term in terms)


def per_device(hidden_in, up_weight, down_weight, head_weight, score_embed, pair_index):
    y_hi, z, core = (lax.axis_index(name).astype(jnp.int32) for name in ("yhi", "z", "core"))
    rows = hidden_in.shape[0] // (2 * RING)
    group_half = RING * rows
    index = block_index(y_hi, z, 1 - 2 * core)
    up_t = up_weight.T
    saved = {}

    def forward(group, *weights):
        parts, kept, down_head = forward_blocks(group, index, hidden_in, up_t, *weights)
        for at, block in enumerate(MEMBERS[group]):
            saved[block] = (kept, at)
        return parts, down_head

    (other4, other3, own4), down_head = forward(0, down_weight, head_weight)
    came4, came3 = swap(other4, "yhi"), swap(other3, "yhi")
    score_wide, score_inverse = unit_rows(score_embed)
    score_unit, up_t = lax.optimization_barrier((score_wide.astype(bf16), up_t))
    score_half = lax.all_gather(score_unit, "z", axis=0, tiled=True)
    (other2, own3), _ = forward(1, down_head)
    came2 = swap(other2, "yhi")
    fore = shift(total_of(own4, came4).astype(bf16), 1)
    (other1, own2), _ = forward(2, down_head)
    came1 = swap(other1, "yhi")
    fore = shift(total_of(own3[:rows], came3[:rows], fore).astype(bf16), 1)
    back = shift(total_of(own3[rows:], came3[rows:]).astype(bf16), -1)
    (own1,), _ = forward(3, down_head)
    for own, came in ((own2, came2), (own1, came1)):
        fore = shift(total_of(own[:rows], came[:rows], fore).astype(bf16), 1)
        back = shift(total_of(own[rows : 2 * rows], came[rows : 2 * rows], back).astype(bf16), -1)
    own_start = y_hi * group_half + z * rows
    own_hidden = lax.dynamic_slice_in_dim(hidden_in, own_start, rows, 0)
    own_proj = dot(own_hidden, head_weight)
    audio_wide, audio_inverse = unit_rows(own_proj + total_of(own1[2 * rows :], came1[2 * rows :], fore, back))
    audio_own = audio_wide.astype(bf16)
    audio_unit = jnp.concatenate([audio_own, swap(audio_own, "yhi")], axis=0)
    far_start = (1 - y_hi) * group_half + z * rows
    partners = jnp.concatenate(
        [lax.dynamic_slice_in_dim(pair_index[0], start, rows, 0) for start in (own_start, far_start)]
    )
    coeffs = pair_coeffs(audio_unit, score_half, partners, y_hi * group_half)
    grad_audio = dot(coeffs, score_half)
    grad_audio = grad_audio[:rows] + swap(grad_audio[rows:].astype(bf16), "yhi").astype(f32)
    grad_embed = unit_backward(audio_wide, audio_inverse, grad_audio).astype(bf16)
    score_part = dot(coeffs, audio_unit, ((0,), (0,))).astype(bf16)
    item = lambda grad, *blocks: (grad, [saved[block] for block in blocks])
    pair = lambda step, half: ((half, step), (half, -step))
    both = lambda up, down: jnp.concatenate([up, down], axis=0)
    crossed0 = swap(grad_embed, "yhi")
    fore, back = shift(grad_embed, 1), shift(grad_embed, -1)
    fore, back, crossed0, score_part = lax.optimization_barrier((fore, back, crossed0, score_part))
    grad_score = lax.psum_scatter(score_part, "z", scatter_dimension=0, tiled=True)
    ring1 = both(back, fore)
    crossed1 = swap(ring1, "yhi")
    fore, back = shift(fore, 1), shift(back, -1)
    ring2 = both(back, fore)
    crossed2 = swap(ring2, "yhi")
    fore, back = shift(fore, 1), shift(back, -1)
    items = [item(grad_embed, (0, 0)), item(crossed0, (1, 0)), item(ring1, *pair(1, 0)), item(crossed1, *pair(1, 1))]
    sums = backward_blocks(items + [item(ring2, *pair(2, 0))], down_head, None)
    fore, back, sums = lax.optimization_barrier((fore, back, sums))
    ring3 = both(back, fore)
    crossed3 = swap(ring3, "yhi")
    ring4 = shift(fore, 1)
    crossed4 = swap(ring4, "yhi")
    items = [item(ring3, *pair(3, 0)), item(crossed2, *pair(2, 1)), item(ring4, (0, 4))]
    sums = backward_blocks(items, down_head, sums)
    crossed4, sums = lax.optimization_barrier((crossed4, sums))
    items = [item(crossed3, *pair(3, 1)), item(crossed4, (1, 4))]
    keep, give = backward_blocks(items, down_head, sums, (core[None], head_weight))
    chip = total_of(keep, swap(give, "core")).astype(bf16)
    landed = lax.all_to_all(chip, ("ylo", "x"), 0, 0)
    total = jnp.sum(landed.astype(f32), axis=0)
    ff = up_weight.shape[1]
    score_grad = unit_backward(score_wide, score_inverse, grad_score.astype(f32))
    return (total[:, :ff], total[:, ff:].T, score_grad)


def solution(mesh):
    fine = Mesh(mesh.devices.reshape(2, 4, 2, 2, RING), ("ylo", "x", "core", "yhi", "z"))
    in_specs = (
        P(AUDIO, None),
        P(None, SCORE),
        P(SCORE, None),
        P(),
        P(AUDIO + SCORE, None),
        P(AUDIO, None),
    )
    out_specs = (P(AUDIO, SCORE), P(SCORE, AUDIO), P(AUDIO + SCORE, None))
    return jax.shard_map(
        per_device, mesh=fine, in_specs=in_specs, out_specs=out_specs, check_vma=False
    )
```

```python
import functools

import jax
import jax.numpy as jnp
from jax import lax
from jax.experimental import pallas as pl
from jax.experimental.pallas import tpu as pltpu
from jax.sharding import Mesh, PartitionSpec as P

logit_scale = 8.0
logit_bias = -3.0
epsilon = 1e-06
gelu_root = 0.7978845608028654
gelu_cubic = 0.044715

AUDIO = ("ylo", "x", "core")
SCORE = ("yhi", "z")
RING = 8
VMEM_BYTES = 56 * 1024 * 1024
f32 = jnp.float32
bf16 = jnp.bfloat16


def dot(left, right, dims=((1,), (0,))):
    return lax.dot_general(left, right, (dims, ((), ())), preferred_element_type=f32)


def unit_rows(values):
    wide = values.astype(f32)
    inverse = lax.rsqrt(jnp.sum(wide * wide, axis=-1, keepdims=True) + epsilon)
    return (wide * inverse, inverse)


def unit_backward(unit_wide, inverse, grad_unit):
    inner = jnp.sum(unit_wide * grad_unit, axis=-1, keepdims=True)
    return inverse * (grad_unit - unit_wide * inner)


def pair_coeffs(left, right, partner, first_column):
    logits = logit_scale * dot(left, right, ((1,), (1,))) + logit_bias
    columns = first_column + lax.iota(jnp.int32, right.shape[0])
    sign = jnp.where(partner[:, None] == columns[None, :], 1.0, -1.0)
    return (-logit_scale * sign * jax.nn.sigmoid(-sign * logits)).astype(bf16)


def swap(value, axis):
    return lax.ppermute(value, axis, [(0, 1), (1, 0)])


def shift(value, step):
    perm = [(i, (i + step) % RING) for i in range(RING)]
    perm += [(RING + i, RING + (i - step) % RING) for i in range(RING)]
    return lax.ppermute(value, ("core", "z"), perm)


GROUPS = (
    (((1, 4),), ((1, 3), (1, -3)), ((0, 4),)),
    (((1, 2), (1, -2)), ((0, 3), (0, -3))),
    (((1, 1), (1, -1), (1, 0)), ((0, 2), (0, -2))),
    (((0, 1), (0, -1), (0, 0)),),
)
MEMBERS = tuple(tuple(block for piece in group for block in piece) for group in GROUPS)


def packed_place(half, place, core):
    return (half * (2 * RING) + place * 2 + core)[None]


def block_map(block):
    half, offset = block

    def index_map(i, packed):
        own_half, place, core = packed[0] // (2 * RING), packed[0] // 2 % RING, packed[0] % 2
        along = lax.rem(place + (1 - 2 * core) * offset + RING, RING)
        return lax.rem(own_half + half, 2) * RING + along, 0

    return index_map


def forward_kernel(pieces, first, packed_ref, *refs):
    count = sum(pieces)
    hidden = [ref[...] for ref in refs[:count]]
    refs = refs[count:]
    if first:
        up_ref, down_ref, head_ref = refs[:3]
        down_head_ref = refs[-1]
        down_head_ref[...] = dot(down_ref[...], head_ref[...]).astype(bf16)
        refs = refs[3:-1]
    else:
        up_ref, down_head_ref = refs[:2]
        refs = refs[2:]
    part_refs = refs[: len(pieces)]
    act_t_ref, slope_ref = refs[len(pieces) :]
    rows = hidden[0].shape[0]
    wide = jnp.concatenate(hidden, axis=0).astype(f32)
    square_mean = jnp.mean(wide * wide, axis=-1, keepdims=True)
    inverse = lax.rsqrt(square_mean + epsilon)
    normed = (wide * inverse).astype(bf16)
    pre = dot(normed, up_ref[...], ((1,), (1,)))
    tangent = jnp.tanh(gelu_root * (pre + gelu_cubic * (pre * pre * pre)))
    act = (0.5 * pre * (1.0 + tangent)).astype(bf16)
    part = dot(act, down_head_ref[...]).astype(bf16)
    at = 0
    for size, part_ref in zip(pieces, part_refs):
        part_ref[...] = part[at * rows : (at + size) * rows, :]
        at += size
    slope = 0.5 * (1.0 + tangent) + 0.5 * pre * (1.0 - tangent * tangent) * gelu_root * (
        1.0 + 3.0 * gelu_cubic * pre * pre
    )
    slope = (inverse * slope).astype(bf16)
    act_t = act.T
    for i in range(count):
        span = slice(i * rows, (i + 1) * rows)
        slope_ref[i] = slope[span, :]
        act_t_ref[i] = act_t[:, span]


def forward_blocks(group, packed, hidden_in, up_t, *weights):
    pieces = tuple(len(piece) for piece in GROUPS[group])
    count = sum(pieces)
    first = len(weights) == 2
    rows = hidden_in.shape[0] // (2 * RING)
    ff, width = up_t.shape
    embed = weights[-1].shape[1]
    flat = lambda i, packed: (0, 0)
    cube = lambda i, packed: (0, 0, 0)
    shapes = [jax.ShapeDtypeStruct((size * rows, embed), bf16) for size in pieces]
    shapes += [jax.ShapeDtypeStruct((count,) + dims, bf16) for dims in ((ff, rows), (rows, ff))]
    shapes += [jax.ShapeDtypeStruct((ff, embed), bf16)] if first else []
    out = pl.pallas_call(
        functools.partial(forward_kernel, pieces, first),
        grid_spec=pltpu.PrefetchScalarGridSpec(
            num_scalar_prefetch=1,
            grid=(1,),
            in_specs=[pl.BlockSpec((rows, width), block_map(block)) for block in MEMBERS[group]]
            + [pl.BlockSpec(w.shape, flat) for w in (up_t,) + weights],
            out_specs=[pl.BlockSpec(shape.shape, cube if len(shape.shape) == 3 else flat) for shape in shapes],
        ),
        out_shape=shapes,
        compiler_params=pltpu.CompilerParams(vmem_limit_bytes=VMEM_BYTES),
        cost_estimate=pl.CostEstimate(
            flops=2 * count * rows * ff * (width + embed),
            bytes_accessed=2 * count * rows * (width + embed + 2 * ff) + 2 * ff * (width + embed),
            transcendentals=count * rows * ff,
        ),
    )(packed, *([hidden_in] * count), up_t, *weights)
    parts, kept = out[: len(pieces)], out[len(pieces) : len(pieces) + 2]
    return parts, kept, out[-1]


def backward_kernel(count, blocks, first, last, packed_ref, *refs):
    join = lambda parts, axis: jnp.concatenate(parts, axis=axis) if len(parts) > 1 else parts[0]
    grad = join([ref[...] for ref in refs[:count]], 0)
    kept = refs[count : count + 3 * blocks]
    hidden = join([ref[...] for ref in kept[0::3]], 0)
    act_t, slope = join([ref[0] for ref in kept[1::3]], 1), join([ref[0] for ref in kept[2::3]], 0)
    refs = refs[count + 3 * blocks :]
    down_head_ref, refs = refs[0], refs[1:]
    if not first:
        up_in, act_in = refs[:2]
        refs = refs[2:]
    tile = 256
    grad_act = dot(grad, down_head_ref[...], ((1,), (1,)))
    grad_pre_t = (grad_act * slope.astype(f32)).astype(bf16).T
    act_sum = dot(act_t, grad)
    if not first:
        act_sum = act_sum + act_in[...]
    if last:
        head_ref, keep_ref, give_ref, total = refs
    else:
        up_acc, act_acc = refs
        act_acc[...] = act_sum
    width, ff = hidden.shape[1], act_sum.shape[0]
    for m in range(0, width, tile):
        up_sum = dot(grad_pre_t, hidden[:, m : m + tile])
        if not first:
            up_sum = up_sum + up_in[:, m : m + tile]
        if last:
            total[m : m + tile, :] = up_sum.T
        else:
            up_acc[:, m : m + tile] = up_sum
    if last:
        core = packed_ref[0] % 2
        act_grad = act_sum.astype(bf16)
        rows = keep_ref.shape[1]
        for side in range(2):
            for half, out_ref in ((core, keep_ref), (1 - core, give_ref)):
                for chip in range(keep_ref.shape[0]):
                    at = pl.multiple_of((2 * chip + half) * rows, rows)
                    out_ref[chip, :, side * ff : (side + 1) * ff] = total[pl.ds(at, rows), :].astype(bf16)
            if side == 0:
                for m in range(0, width, tile):
                    total[m : m + tile, :] = dot(head_ref[m : m + tile, :], act_grad, ((1,), (1,)))


def backward_blocks(items, packed, hidden_in, down_head, sums, head_weight=None):
    last = head_weight is not None
    whole = pl.BlockSpec(memory_space=pltpu.VMEM)
    args = [grad for grad, _ in items]
    specs = [whole] * len(items)
    places = [place for _, blocks in items for place in blocks]
    rows, width = hidden_in.shape[0] // (2 * RING), hidden_in.shape[1]
    for block, kept, at in places:
        args.append(hidden_in)
        specs.append(pl.BlockSpec((rows, width), block_map(block)))
        for array in kept:
            args.append(array)
            specs.append(pl.BlockSpec((1,) + array.shape[1:], lambda i, packed, at=at: (at, 0, 0)))
    ff, embed = down_head.shape
    args.append(down_head)
    aliases = {}
    if sums is not None:
        if not last:
            aliases = {len(args) + 1: 0, len(args) + 2: 1}
        args += list(sums)
    flops = 2 * len(places) * rows * ff * (2 * embed + width)
    if last:
        args.append(head_weight)
        shapes = [jax.ShapeDtypeStruct((8, width // 16, 2 * ff), bf16)] * 2
        scratch = [pltpu.VMEM((width, ff), f32)]
        flops += 2 * width * ff * embed
    else:
        shapes = [jax.ShapeDtypeStruct((ff, width), f32), jax.ShapeDtypeStruct((ff, embed), f32)]
        scratch = []
    specs += [whole] * (len(args) - len(specs))
    return pl.pallas_call(
        functools.partial(backward_kernel, len(items), len(places), sums is None, last),
        grid_spec=pltpu.PrefetchScalarGridSpec(
            num_scalar_prefetch=1,
            grid=(1,),
            in_specs=specs,
            out_specs=[whole] * 2,
            scratch_shapes=scratch,
        ),
        out_shape=shapes,
        input_output_aliases=aliases,
        compiler_params=pltpu.CompilerParams(vmem_limit_bytes=VMEM_BYTES),
        cost_estimate=pl.CostEstimate(flops=flops, bytes_accessed=8 * 1024 * 1024, transcendentals=0),
    )(packed, *args)


def total_of(*terms):
    return sum(term.astype(f32) for term in terms)


def per_device(hidden_in, up_weight, down_weight, head_weight, score_embed, pair_index):
    y_hi, z, core = (lax.axis_index(name).astype(jnp.int32) for name in ("yhi", "z", "core"))
    rows = hidden_in.shape[0] // (2 * RING)
    group_half = RING * rows
    packed = packed_place(y_hi, z, core)
    up_t = up_weight.T
    saved = {}

    def forward(group, *weights):
        parts, kept, down_head = forward_blocks(group, packed, hidden_in, up_t, *weights)
        for at, block in enumerate(MEMBERS[group]):
            saved[block] = (block, kept, at)
        return parts, down_head

    (other4, other3, own4), down_head = forward(0, down_weight, head_weight)
    came4, came3 = swap(other4, "yhi"), swap(other3, "yhi")
    score_wide, score_inverse = unit_rows(score_embed)
    score_unit, up_t = lax.optimization_barrier((score_wide.astype(bf16), up_t))
    score_half = lax.all_gather(score_unit, "z", axis=0, tiled=True)
    (other2, own3), _ = forward(1, down_head)
    came2 = swap(other2, "yhi")
    fore = shift(total_of(own4, came4).astype(bf16), 1)
    (other1, own2), _ = forward(2, down_head)
    came1 = swap(other1, "yhi")
    fore = shift(total_of(own3[:rows], came3[:rows], fore).astype(bf16), 1)
    back = shift(total_of(own3[rows:], came3[rows:]).astype(bf16), -1)
    (own1,), _ = forward(3, down_head)
    for own, came in ((own2, came2), (own1, came1)):
        fore = shift(total_of(own[:rows], came[:rows], fore).astype(bf16), 1)
        back = shift(total_of(own[rows : 2 * rows], came[rows : 2 * rows], back).astype(bf16), -1)
    own_start = y_hi * group_half + z * rows
    own_hidden = lax.dynamic_slice_in_dim(hidden_in, own_start, rows, 0)
    own_proj = dot(own_hidden, head_weight)
    audio_wide, audio_inverse = unit_rows(own_proj + total_of(own1[2 * rows :], came1[2 * rows :], fore, back))
    audio_own = audio_wide.astype(bf16)
    audio_unit = jnp.concatenate([audio_own, swap(audio_own, "yhi")], axis=0)
    far_start = (1 - y_hi) * group_half + z * rows
    partners = jnp.concatenate(
        [lax.dynamic_slice_in_dim(pair_index[0], start, rows, 0) for start in (own_start, far_start)]
    )
    coeffs = pair_coeffs(audio_unit, score_half, partners, y_hi * group_half)
    grad_audio = dot(coeffs, score_half)
    grad_audio = grad_audio[:rows] + swap(grad_audio[rows:].astype(bf16), "yhi").astype(f32)
    grad_embed = unit_backward(audio_wide, audio_inverse, grad_audio).astype(bf16)
    score_part = dot(coeffs, audio_unit, ((0,), (0,))).astype(bf16)
    item = lambda grad, *blocks: (grad, [saved[block] for block in blocks])
    pair = lambda step, half: ((half, step), (half, -step))
    both = lambda up, down: jnp.concatenate([up, down], axis=0)
    crossed0 = swap(grad_embed, "yhi")
    fore, back = shift(grad_embed, 1), shift(grad_embed, -1)
    fore, back, crossed0, score_part = lax.optimization_barrier((fore, back, crossed0, score_part))
    grad_score = lax.psum_scatter(score_part, "z", scatter_dimension=0, tiled=True)
    ring1 = both(back, fore)
    crossed1 = swap(ring1, "yhi")
    fore, back = shift(fore, 1), shift(back, -1)
    ring2 = both(back, fore)
    crossed2 = swap(ring2, "yhi")
    fore, back = shift(fore, 1), shift(back, -1)
    backward = lambda items, sums, *head: backward_blocks(items, packed, hidden_in, down_head, sums, *head)
    sums = backward([item(grad_embed, (0, 0)), item(crossed0, (1, 0)), item(ring1, *pair(1, 0))], None)
    fore, back, crossed1, sums = lax.optimization_barrier((fore, back, crossed1, sums))
    ring4 = shift(fore, 1)
    ring3 = both(back, fore)
    crossed3 = swap(ring3, "yhi")
    sums = backward([item(crossed1, *pair(1, 1)), item(ring2, *pair(2, 0))], sums)
    ring4, sums = lax.optimization_barrier((ring4, sums))
    crossed4 = swap(ring4, "yhi")
    sums = backward([item(ring3, *pair(3, 0)), item(crossed2, *pair(2, 1)), item(ring4, (0, 4))], sums)
    crossed4, sums = lax.optimization_barrier((crossed4, sums))
    keep, give = backward([item(crossed3, *pair(3, 1)), item(crossed4, (1, 4))], sums, head_weight)
    chip = total_of(keep, swap(give, "core")).astype(bf16)
    score_grad = unit_backward(score_wide, score_inverse, grad_score.astype(f32))
    chip, score_grad = lax.optimization_barrier((chip, score_grad))
    landed = lax.all_to_all(chip, ("ylo", "x"), 0, 0)
    total = jnp.sum(landed.astype(f32), axis=0)
    ff = up_weight.shape[1]
    return (total[:, :ff], total[:, ff:].T, score_grad)


def solution(mesh):
    fine = Mesh(mesh.devices.reshape(2, 4, 2, 2, RING), ("ylo", "x", "core", "yhi", "z"))
    in_specs = (
        P(AUDIO, None),
        P(None, SCORE),
        P(SCORE, None),
        P(),
        P(AUDIO + SCORE, None),
        P(AUDIO, None),
    )
    out_specs = (P(AUDIO, SCORE), P(SCORE, AUDIO), P(AUDIO + SCORE, None))
    return jax.shard_map(
        per_device, mesh=fine, in_specs=in_specs, out_specs=out_specs, check_vma=False
    )
```

```python
import functools

import jax
import jax.numpy as jnp
from jax import lax
from jax.experimental import pallas as pl
from jax.experimental.pallas import tpu as pltpu
from jax.sharding import Mesh, PartitionSpec as P

logit_scale = 8.0
logit_bias = -3.0
epsilon = 1e-06
gelu_root = 0.7978845608028654
gelu_cubic = 0.044715

AUDIO = ("ylo", "x", "core")
SCORE = ("yhi", "z")
RING = 8
VMEM_BYTES = 56 * 1024 * 1024
f32 = jnp.float32
bf16 = jnp.bfloat16


def dot(left, right, dims=((1,), (0,))):
    return lax.dot_general(left, right, (dims, ((), ())), preferred_element_type=f32)


def unit_rows(values):
    wide = values.astype(f32)
    inverse = lax.rsqrt(jnp.sum(wide * wide, axis=-1, keepdims=True) + epsilon)
    return (wide * inverse, inverse)


def unit_backward(unit_wide, inverse, grad_unit):
    inner = jnp.sum(unit_wide * grad_unit, axis=-1, keepdims=True)
    return inverse * (grad_unit - unit_wide * inner)


def pair_coeffs(left, right, partner, first_column):
    logits = logit_scale * dot(left, right, ((1,), (1,))) + logit_bias
    columns = first_column + lax.iota(jnp.int32, right.shape[0])
    sign = jnp.where(partner[:, None] == columns[None, :], 1.0, -1.0)
    return (-logit_scale * sign * jax.nn.sigmoid(-sign * logits)).astype(bf16)


def swap(value, axis):
    return lax.ppermute(value, axis, [(0, 1), (1, 0)])


def shift(value, step):
    perm = [(i, (i + step) % RING) for i in range(RING)]
    perm += [(RING + i, RING + (i - step) % RING) for i in range(RING)]
    return lax.ppermute(value, ("core", "z"), perm)


def shift_across(value, step):
    to = lambda core, half, place: (core * 2 + half) * RING + place % RING
    perm = [
        (to(core, half, place), to(core, 1 - half, place + (step if core == 0 else -step)))
        for core in range(2)
        for half in range(2)
        for place in range(RING)
    ]
    return lax.ppermute(value, ("core", "yhi", "z"), perm)


GROUPS = (
    (((1, 4),), ((1, 3), (1, -3)), ((0, 4),)),
    (((1, 2), (1, -2)), ((0, 3), (0, -3))),
    (((1, 1), (1, -1), (1, 0)), ((0, 2), (0, -2))),
    (((0, 1), (0, -1), (0, 0)),),
)
MEMBERS = tuple(tuple(block for piece in group for block in piece) for group in GROUPS)


def packed_place(half, place, core):
    return (half * (2 * RING) + place * 2 + core)[None]


def block_map(block):
    half, offset = block

    def index_map(i, packed):
        own_half, place, core = packed[0] // (2 * RING), packed[0] // 2 % RING, packed[0] % 2
        along = lax.rem(place + (1 - 2 * core) * offset + RING, RING)
        return lax.rem(own_half + half, 2) * RING + along, 0

    return index_map


def forward_kernel(pieces, first, packed_ref, *refs):
    count = sum(pieces)
    hidden = [ref[...] for ref in refs[:count]]
    refs = refs[count:]
    if first:
        up_ref, down_ref, head_ref = refs[:3]
        down_head_ref = refs[-1]
        down_head_ref[...] = dot(down_ref[...], head_ref[...]).astype(bf16)
        refs = refs[3:-1]
    else:
        up_ref, down_head_ref = refs[:2]
        refs = refs[2:]
    part_refs = refs[: len(pieces)]
    act_t_ref, slope_ref = refs[len(pieces) :]
    rows = hidden[0].shape[0]
    wide = jnp.concatenate(hidden, axis=0).astype(f32)
    square_mean = jnp.mean(wide * wide, axis=-1, keepdims=True)
    inverse = lax.rsqrt(square_mean + epsilon)
    normed = (wide * inverse).astype(bf16)
    pre = dot(normed, up_ref[...], ((1,), (1,)))
    tangent = jnp.tanh(gelu_root * (pre + gelu_cubic * (pre * pre * pre)))
    act = (0.5 * pre * (1.0 + tangent)).astype(bf16)
    part = dot(act, down_head_ref[...]).astype(bf16)
    at = 0
    for size, part_ref in zip(pieces, part_refs):
        part_ref[...] = part[at * rows : (at + size) * rows, :]
        at += size
    slope = 0.5 * (1.0 + tangent) + 0.5 * pre * (1.0 - tangent * tangent) * gelu_root * (
        1.0 + 3.0 * gelu_cubic * pre * pre
    )
    slope = (inverse * slope).astype(bf16)
    act_t = act.T
    for i in range(count):
        span = slice(i * rows, (i + 1) * rows)
        slope_ref[i] = slope[span, :]
        act_t_ref[i] = act_t[:, span]


def forward_blocks(group, packed, hidden_in, up_t, *weights):
    pieces = tuple(len(piece) for piece in GROUPS[group])
    count = sum(pieces)
    first = len(weights) == 2
    rows = hidden_in.shape[0] // (2 * RING)
    ff, width = up_t.shape
    embed = weights[-1].shape[1]
    flat = lambda i, packed: (0, 0)
    cube = lambda i, packed: (0, 0, 0)
    shapes = [jax.ShapeDtypeStruct((size * rows, embed), bf16) for size in pieces]
    shapes += [jax.ShapeDtypeStruct((count,) + dims, bf16) for dims in ((ff, rows), (rows, ff))]
    shapes += [jax.ShapeDtypeStruct((ff, embed), bf16)] if first else []
    out = pl.pallas_call(
        functools.partial(forward_kernel, pieces, first),
        grid_spec=pltpu.PrefetchScalarGridSpec(
            num_scalar_prefetch=1,
            grid=(1,),
            in_specs=[pl.BlockSpec((rows, width), block_map(block)) for block in MEMBERS[group]]
            + [pl.BlockSpec(w.shape, flat) for w in (up_t,) + weights],
            out_specs=[pl.BlockSpec(shape.shape, cube if len(shape.shape) == 3 else flat) for shape in shapes],
        ),
        out_shape=shapes,
        compiler_params=pltpu.CompilerParams(vmem_limit_bytes=VMEM_BYTES),
        cost_estimate=pl.CostEstimate(
            flops=2 * count * rows * ff * (width + embed),
            bytes_accessed=2 * count * rows * (width + embed + 2 * ff) + 2 * ff * (width + embed),
            transcendentals=count * rows * ff,
        ),
    )(packed, *([hidden_in] * count), up_t, *weights)
    parts, kept = out[: len(pieces)], out[len(pieces) : len(pieces) + 2]
    return parts, kept, out[-1]


def backward_kernel(count, blocks, first, last, packed_ref, *refs):
    join = lambda parts, axis: jnp.concatenate(parts, axis=axis) if len(parts) > 1 else parts[0]
    grad = join([ref[...] for ref in refs[:count]], 0)
    kept = refs[count : count + 3 * blocks]
    hidden = join([ref[...] for ref in kept[0::3]], 0)
    act_t, slope = join([ref[0] for ref in kept[1::3]], 1), join([ref[0] for ref in kept[2::3]], 0)
    refs = refs[count + 3 * blocks :]
    down_head_ref, refs = refs[0], refs[1:]
    if not first:
        up_in, act_in = refs[:2]
        refs = refs[2:]
    tile = 256
    grad_act = dot(grad, down_head_ref[...], ((1,), (1,)))
    grad_pre_t = (grad_act * slope.astype(f32)).astype(bf16).T
    act_sum = dot(act_t, grad)
    if not first:
        act_sum = act_sum + act_in[...]
    if last:
        head_ref, keep_ref, give_ref, total = refs
    else:
        up_acc, act_acc = refs
        act_acc[...] = act_sum
    width, ff = hidden.shape[1], act_sum.shape[0]
    for m in range(0, width, tile):
        up_sum = dot(grad_pre_t, hidden[:, m : m + tile])
        if not first:
            up_sum = up_sum + up_in[:, m : m + tile]
        if last:
            total[m : m + tile, :] = up_sum.T
        else:
            up_acc[:, m : m + tile] = up_sum
    if last:
        core = packed_ref[0] % 2
        act_grad = act_sum.astype(bf16)
        rows = keep_ref.shape[1]
        for side in range(2):
            for half, out_ref in ((core, keep_ref), (1 - core, give_ref)):
                for chip in range(keep_ref.shape[0]):
                    at = pl.multiple_of((2 * chip + half) * rows, rows)
                    out_ref[chip, :, side * ff : (side + 1) * ff] = total[pl.ds(at, rows), :].astype(bf16)
            if side == 0:
                for m in range(0, width, tile):
                    total[m : m + tile, :] = dot(head_ref[m : m + tile, :], act_grad, ((1,), (1,)))


def backward_blocks(items, packed, hidden_in, down_head, sums, head_weight=None):
    last = head_weight is not None
    whole = pl.BlockSpec(memory_space=pltpu.VMEM)
    args = [grad for grad, _ in items]
    specs = [whole] * len(items)
    places = [place for _, blocks in items for place in blocks]
    rows, width = hidden_in.shape[0] // (2 * RING), hidden_in.shape[1]
    for block, kept, at in places:
        args.append(hidden_in)
        specs.append(pl.BlockSpec((rows, width), block_map(block)))
        for array in kept:
            args.append(array)
            specs.append(pl.BlockSpec((1,) + array.shape[1:], lambda i, packed, at=at: (at, 0, 0)))
    ff, embed = down_head.shape
    args.append(down_head)
    aliases = {}
    if sums is not None:
        if not last:
            aliases = {len(args) + 1: 0, len(args) + 2: 1}
        args += list(sums)
    flops = 2 * len(places) * rows * ff * (2 * embed + width)
    if last:
        args.append(head_weight)
        shapes = [jax.ShapeDtypeStruct((8, width // 16, 2 * ff), bf16)] * 2
        scratch = [pltpu.VMEM((width, ff), f32)]
        flops += 2 * width * ff * embed
    else:
        shapes = [jax.ShapeDtypeStruct((ff, width), f32), jax.ShapeDtypeStruct((ff, embed), f32)]
        scratch = []
    specs += [whole] * (len(args) - len(specs))
    return pl.pallas_call(
        functools.partial(backward_kernel, len(items), len(places), sums is None, last),
        grid_spec=pltpu.PrefetchScalarGridSpec(
            num_scalar_prefetch=1,
            grid=(1,),
            in_specs=specs,
            out_specs=[whole] * 2,
            scratch_shapes=scratch,
        ),
        out_shape=shapes,
        input_output_aliases=aliases,
        compiler_params=pltpu.CompilerParams(vmem_limit_bytes=VMEM_BYTES),
        cost_estimate=pl.CostEstimate(flops=flops, bytes_accessed=8 * 1024 * 1024, transcendentals=0),
    )(packed, *args)


def score_kernel(embed_ref, grad_ref, out_ref):
    wide, inverse = unit_rows(embed_ref[...])
    out_ref[...] = unit_backward(wide, inverse, grad_ref[...].astype(f32))


def score_backward(score_embed, grad_score):
    return pl.pallas_call(
        score_kernel,
        out_shape=jax.ShapeDtypeStruct(score_embed.shape, f32),
        compiler_params=pltpu.CompilerParams(vmem_limit_bytes=VMEM_BYTES),
    )(score_embed, grad_score)


def total_of(*terms):
    return sum(term.astype(f32) for term in terms)


def per_device(hidden_in, up_weight, down_weight, head_weight, score_embed, pair_index):
    y_hi, z, core = (lax.axis_index(name).astype(jnp.int32) for name in ("yhi", "z", "core"))
    rows = hidden_in.shape[0] // (2 * RING)
    group_half = RING * rows
    packed = packed_place(y_hi, z, core)
    up_t = up_weight.T
    saved = {}

    def forward(group, *weights):
        parts, kept, down_head = forward_blocks(group, packed, hidden_in, up_t, *weights)
        for at, block in enumerate(MEMBERS[group]):
            saved[block] = (block, kept, at)
        return parts, down_head

    score_half = lax.all_gather(score_embed, "z", axis=0, tiled=True)
    (other4, other3, own4), down_head = forward(0, down_weight, head_weight)
    came4, came3 = swap(other4, "yhi"), swap(other3, "yhi")
    (other2, own3), _ = forward(1, down_head)
    came2 = swap(other2, "yhi")
    fore = shift(total_of(own4, came4).astype(bf16), 1)
    (other1, own2), _ = forward(2, down_head)
    came1 = swap(other1, "yhi")
    fore = shift(total_of(own3[:rows], came3[:rows], fore).astype(bf16), 1)
    back = shift(total_of(own3[rows:], came3[rows:]).astype(bf16), -1)
    (own1,), _ = forward(3, down_head)
    for own, came in ((own2, came2), (own1, came1)):
        fore = shift(total_of(own[:rows], came[:rows], fore).astype(bf16), 1)
        back = shift(total_of(own[rows : 2 * rows], came[rows : 2 * rows], back).astype(bf16), -1)
    score_unit = unit_rows(score_half)[0].astype(bf16)
    fore, back, score_unit = lax.optimization_barrier((fore, back, score_unit))
    own_start = y_hi * group_half + z * rows
    own_hidden = lax.dynamic_slice_in_dim(hidden_in, own_start, rows, 0)
    own_proj = dot(own_hidden, head_weight)
    audio_wide, audio_inverse = unit_rows(own_proj + total_of(own1[2 * rows :], came1[2 * rows :], fore, back))
    audio_own = audio_wide.astype(bf16)
    audio_unit = jnp.concatenate([audio_own, swap(audio_own, "yhi")], axis=0)
    far_start = (1 - y_hi) * group_half + z * rows
    partners = jnp.concatenate(
        [lax.dynamic_slice_in_dim(pair_index[0], start, rows, 0) for start in (own_start, far_start)]
    )
    coeffs = pair_coeffs(audio_unit, score_unit, partners, y_hi * group_half)
    grad_audio = dot(coeffs, score_unit)
    grad_audio = grad_audio[:rows] + swap(grad_audio[rows:].astype(bf16), "yhi").astype(f32)
    grad_embed = unit_backward(audio_wide, audio_inverse, grad_audio).astype(bf16)
    score_part = dot(coeffs, audio_unit, ((0,), (0,))).astype(bf16)
    item = lambda grad, *blocks: (grad, [saved[block] for block in blocks])
    pair = lambda step, half: ((half, step), (half, -step))
    both = lambda up, down: jnp.concatenate([up, down], axis=0)
    crossed0 = swap(grad_embed, "yhi")
    fore, back = shift(grad_embed, 1), shift(grad_embed, -1)
    fore, back, crossed0, score_part = lax.optimization_barrier((fore, back, crossed0, score_part))
    ring1 = both(back, fore)
    crossed1 = swap(ring1, "yhi")
    fore, back = shift(fore, 1), shift(back, -1)
    ring2 = both(back, fore)
    crossed2 = swap(ring2, "yhi")
    fore, back = shift(fore, 1), shift(back, -1)
    backward = lambda items, sums, *head: backward_blocks(items, packed, hidden_in, down_head, sums, *head)
    sums = backward([item(grad_embed, (0, 0)), item(crossed0, (1, 0)), item(ring1, *pair(1, 0))], None)
    sums = backward([item(crossed1, *pair(1, 1)), item(ring2, *pair(2, 0))], sums)
    fore, back, sums, score_part = lax.optimization_barrier((fore, back, sums, score_part))
    grad_score = lax.psum_scatter(score_part, "z", scatter_dimension=0, tiled=True)
    ring4, crossed4 = shift(fore, 1), shift_across(fore, 1)
    ring3 = both(back, fore)
    crossed3 = swap(ring3, "yhi")
    sums = backward([item(ring3, *pair(3, 0)), item(crossed2, *pair(2, 1))], sums)
    ring4, crossed4, sums = lax.optimization_barrier((ring4, crossed4, sums))
    items = [item(crossed3, *pair(3, 1)), item(ring4, (0, 4)), item(crossed4, (1, 4))]
    keep, give = backward(items, sums, head_weight)
    chip = total_of(keep, swap(give, "core")).astype(bf16)
    landed = lax.all_to_all(chip, ("ylo", "x"), 0, 0)
    total = jnp.sum(landed.astype(f32), axis=0)
    ff = up_weight.shape[1]
    score_grad = score_backward(score_embed, grad_score)
    return (total[:, :ff], total[:, ff:].T, score_grad)


def solution(mesh):
    fine = Mesh(mesh.devices.reshape(2, 4, 2, 2, RING), ("ylo", "x", "core", "yhi", "z"))
    in_specs = (
        P(AUDIO, None),
        P(None, SCORE),
        P(SCORE, None),
        P(),
        P(AUDIO + SCORE, None),
        P(AUDIO, None),
    )
    out_specs = (P(AUDIO, SCORE), P(SCORE, AUDIO), P(AUDIO + SCORE, None))
    return jax.shard_map(
        per_device, mesh=fine, in_specs=in_specs, out_specs=out_specs, check_vma=False
    )
```

```python
import functools

import jax
import jax.numpy as jnp
from jax import lax
from jax.experimental import pallas as pl
from jax.experimental.pallas import tpu as pltpu
from jax.sharding import Mesh, PartitionSpec as P

logit_scale = 8.0
logit_bias = -3.0
epsilon = 1e-06
gelu_root = 0.7978845608028654
gelu_cubic = 0.044715

AUDIO = ("ylo", "x", "core")
SCORE = ("yhi", "z")
RING = 8
VMEM_BYTES = 56 * 1024 * 1024
f32 = jnp.float32
bf16 = jnp.bfloat16


def dot(left, right, dims=((1,), (0,))):
    return lax.dot_general(left, right, (dims, ((), ())), preferred_element_type=f32)


def unit_rows(values):
    wide = values.astype(f32)
    inverse = lax.rsqrt(jnp.sum(wide * wide, axis=-1, keepdims=True) + epsilon)
    return (wide * inverse, inverse)


def unit_backward(unit_wide, inverse, grad_unit):
    inner = jnp.sum(unit_wide * grad_unit, axis=-1, keepdims=True)
    return inverse * (grad_unit - unit_wide * inner)


def pair_coeffs(left, right, partner, first_column):
    logits = logit_scale * dot(left, right, ((1,), (1,))) + logit_bias
    columns = first_column + lax.iota(jnp.int32, right.shape[0])
    sign = jnp.where(partner[:, None] == columns[None, :], 1.0, -1.0)
    return (-logit_scale * sign * jax.nn.sigmoid(-sign * logits)).astype(bf16)


def swap(value, axis):
    return lax.ppermute(value, axis, [(0, 1), (1, 0)])


def shift(value, step):
    perm = [(i, (i + step) % RING) for i in range(RING)]
    perm += [(RING + i, RING + (i - step) % RING) for i in range(RING)]
    return lax.ppermute(value, ("core", "z"), perm)


def shift_across(value, step):
    to = lambda core, half, place: (core * 2 + half) * RING + place % RING
    perm = [
        (to(core, half, place), to(core, 1 - half, place + (step if core == 0 else -step)))
        for core in range(2)
        for half in range(2)
        for place in range(RING)
    ]
    return lax.ppermute(value, ("core", "yhi", "z"), perm)


GROUPS = (
    (((1, 4),), ((1, 3), (1, -3)), ((0, 4),)),
    (((1, 2), (1, -2)), ((0, 3), (0, -3))),
    (((1, 1), (1, -1), (1, 0)), ((0, 2), (0, -2))),
    (((0, 1), (0, -1), (0, 0)),),
)
MEMBERS = tuple(tuple(block for piece in group for block in piece) for group in GROUPS)


def packed_place(half, place, core):
    return (half * (2 * RING) + place * 2 + core)[None]


def block_map(block):
    half, offset = block

    def index_map(i, packed):
        own_half, place, core = packed[0] // (2 * RING), packed[0] // 2 % RING, packed[0] % 2
        along = lax.rem(place + (1 - 2 * core) * offset + RING, RING)
        return lax.rem(own_half + half, 2) * RING + along, 0

    return index_map


def forward_kernel(pieces, first, packed_ref, *refs):
    count = sum(pieces)
    hidden = [ref[...] for ref in refs[:count]]
    refs = refs[count:]
    if first:
        up_ref, down_ref, head_ref = refs[:3]
        down_head_ref = refs[-1]
        down_head_ref[...] = dot(down_ref[...], head_ref[...]).astype(bf16)
        refs = refs[3:-1]
    else:
        up_ref, down_head_ref = refs[:2]
        refs = refs[2:]
    part_refs = refs[: len(pieces)]
    act_t_ref, slope_ref = refs[len(pieces) :]
    rows = hidden[0].shape[0]
    wide = jnp.concatenate(hidden, axis=0).astype(f32)
    square_mean = jnp.mean(wide * wide, axis=-1, keepdims=True)
    inverse = lax.rsqrt(square_mean + epsilon)
    normed = (wide * inverse).astype(bf16)
    pre = dot(normed, up_ref[...], ((1,), (1,)))
    tangent = jnp.tanh(gelu_root * (pre + gelu_cubic * (pre * pre * pre)))
    act = (0.5 * pre * (1.0 + tangent)).astype(bf16)
    part = dot(act, down_head_ref[...]).astype(bf16)
    at = 0
    for size, part_ref in zip(pieces, part_refs):
        part_ref[...] = part[at * rows : (at + size) * rows, :]
        at += size
    slope = 0.5 * (1.0 + tangent) + 0.5 * pre * (1.0 - tangent * tangent) * gelu_root * (
        1.0 + 3.0 * gelu_cubic * pre * pre
    )
    slope = (inverse * slope).astype(bf16)
    act_t = act.T
    for i in range(count):
        span = slice(i * rows, (i + 1) * rows)
        slope_ref[i] = slope[span, :]
        act_t_ref[i] = act_t[:, span]


def forward_blocks(group, packed, hidden_in, up_t, *weights):
    pieces = tuple(len(piece) for piece in GROUPS[group])
    count = sum(pieces)
    first = len(weights) == 2
    rows = hidden_in.shape[0] // (2 * RING)
    ff, width = up_t.shape
    embed = weights[-1].shape[1]
    flat = lambda i, packed: (0, 0)
    cube = lambda i, packed: (0, 0, 0)
    shapes = [jax.ShapeDtypeStruct((size * rows, embed), bf16) for size in pieces]
    shapes += [jax.ShapeDtypeStruct((count,) + dims, bf16) for dims in ((ff, rows), (rows, ff))]
    shapes += [jax.ShapeDtypeStruct((ff, embed), bf16)] if first else []
    out = pl.pallas_call(
        functools.partial(forward_kernel, pieces, first),
        grid_spec=pltpu.PrefetchScalarGridSpec(
            num_scalar_prefetch=1,
            grid=(1,),
            in_specs=[pl.BlockSpec((rows, width), block_map(block)) for block in MEMBERS[group]]
            + [pl.BlockSpec(w.shape, flat) for w in (up_t,) + weights],
            out_specs=[pl.BlockSpec(shape.shape, cube if len(shape.shape) == 3 else flat) for shape in shapes],
        ),
        out_shape=shapes,
        compiler_params=pltpu.CompilerParams(vmem_limit_bytes=VMEM_BYTES),
        cost_estimate=pl.CostEstimate(
            flops=2 * count * rows * ff * (width + embed),
            bytes_accessed=2 * count * rows * (width + embed + 2 * ff) + 2 * ff * (width + embed),
            transcendentals=count * rows * ff,
        ),
    )(packed, *([hidden_in] * count), up_t, *weights)
    parts, kept = out[: len(pieces)], out[len(pieces) : len(pieces) + 2]
    return parts, kept, out[-1]


def backward_kernel(count, blocks, first, last, packed_ref, *refs):
    join = lambda parts, axis: jnp.concatenate(parts, axis=axis) if len(parts) > 1 else parts[0]
    grad = join([ref[...] for ref in refs[:count]], 0)
    kept = refs[count : count + 3 * blocks]
    hidden = join([ref[...] for ref in kept[0::3]], 0)
    act_t, slope = join([ref[0] for ref in kept[1::3]], 1), join([ref[0] for ref in kept[2::3]], 0)
    refs = refs[count + 3 * blocks :]
    down_head_ref, refs = refs[0], refs[1:]
    copies = []
    if last:
        far, (keep_ref, give_ref, total), near, sems = refs[:3], refs[3:6], refs[6:9], refs[9]
        copies = [pltpu.make_async_copy(far[i], near[i], sems.at[i]) for i in range(3)]
        for copy in copies:
            copy.start()
        act_in, up_in, head_ref = near
    elif not first:
        up_in, act_in, up_acc, act_acc = refs
    else:
        up_acc, act_acc = refs
    tile = 256
    grad_act = dot(grad, down_head_ref[...], ((1,), (1,)))
    grad_pre_t = (grad_act * slope.astype(f32)).astype(bf16).T
    act_sum = dot(act_t, grad)
    for copy in copies[:2]:
        copy.wait()
    if not first:
        act_sum = act_sum + act_in[...]
    if not last:
        act_acc[...] = act_sum
    width, ff = hidden.shape[1], act_sum.shape[0]
    for m in range(0, width, tile):
        up_sum = dot(grad_pre_t, hidden[:, m : m + tile])
        if not first:
            up_sum = up_sum + up_in[:, m : m + tile]
        if last:
            total[m : m + tile, :] = up_sum.T
        else:
            up_acc[:, m : m + tile] = up_sum
    if last:
        core = packed_ref[0] % 2
        act_grad = act_sum.astype(bf16)
        rows = keep_ref.shape[1]
        for side in range(2):
            for half, out_ref in ((core, keep_ref), (1 - core, give_ref)):
                for chip in range(keep_ref.shape[0]):
                    at = pl.multiple_of((2 * chip + half) * rows, rows)
                    out_ref[chip, :, side * ff : (side + 1) * ff] = total[pl.ds(at, rows), :].astype(bf16)
            if side == 0:
                copies[2].wait()
                for m in range(0, width, tile):
                    total[m : m + tile, :] = dot(head_ref[m : m + tile, :], act_grad, ((1,), (1,)))


def backward_blocks(items, packed, hidden_in, down_head, sums, head_weight=None):
    last = head_weight is not None
    whole = pl.BlockSpec(memory_space=pltpu.VMEM)
    args = [grad for grad, _ in items]
    specs = [whole] * len(items)
    places = [place for _, blocks in items for place in blocks]
    rows, width = hidden_in.shape[0] // (2 * RING), hidden_in.shape[1]
    for block, kept, at in places:
        args.append(hidden_in)
        specs.append(pl.BlockSpec((rows, width), block_map(block)))
        for array in kept:
            args.append(array)
            specs.append(pl.BlockSpec((1,) + array.shape[1:], lambda i, packed, at=at: (at, 0, 0)))
    ff, embed = down_head.shape
    args.append(down_head)
    aliases = {}
    if sums is not None:
        if not last:
            aliases = {len(args) + 1: 0, len(args) + 2: 1}
        args += [sums[1], sums[0]] if last else list(sums)
    if last:
        args.append(head_weight)
        shapes = [jax.ShapeDtypeStruct((8, width // 16, 2 * ff), bf16)] * 2
        scratch = [pltpu.VMEM((width, ff), f32)]
        scratch += [pltpu.VMEM(array.shape, array.dtype) for array in args[-3:]]
        scratch += [pltpu.SemaphoreType.DMA((3,))]
    else:
        shapes = [jax.ShapeDtypeStruct((ff, width), f32), jax.ShapeDtypeStruct((ff, embed), f32)]
        scratch = []
    specs += [whole] * (len(args) - len(specs))
    if last:
        specs[-3:] = [pl.BlockSpec(memory_space=pl.ANY)] * 3
    return pl.pallas_call(
        functools.partial(backward_kernel, len(items), len(places), sums is None, last),
        grid_spec=pltpu.PrefetchScalarGridSpec(
            num_scalar_prefetch=1,
            grid=(1,),
            in_specs=specs,
            out_specs=[whole] * 2,
            scratch_shapes=scratch,
        ),
        out_shape=shapes,
        input_output_aliases=aliases,
        compiler_params=pltpu.CompilerParams(vmem_limit_bytes=VMEM_BYTES),
        cost_estimate=pl.CostEstimate(flops=0, bytes_accessed=0, transcendentals=0),
    )(packed, *args)


def score_kernel(embed_ref, grad_ref, out_ref):
    wide, inverse = unit_rows(embed_ref[...])
    out_ref[...] = unit_backward(wide, inverse, grad_ref[...].astype(f32))


def score_backward(score_embed, grad_score):
    return pl.pallas_call(
        score_kernel,
        out_shape=jax.ShapeDtypeStruct(score_embed.shape, f32),
        compiler_params=pltpu.CompilerParams(vmem_limit_bytes=VMEM_BYTES),
    )(score_embed, grad_score)


def total_of(*terms):
    return sum(term.astype(f32) for term in terms)


def per_device(hidden_in, up_weight, down_weight, head_weight, score_embed, pair_index):
    y_hi, z, core = (lax.axis_index(name).astype(jnp.int32) for name in ("yhi", "z", "core"))
    rows = hidden_in.shape[0] // (2 * RING)
    group_half = RING * rows
    packed = packed_place(y_hi, z, core)
    up_t = up_weight.T
    saved = {}

    def forward(group, *weights):
        parts, kept, down_head = forward_blocks(group, packed, hidden_in, up_t, *weights)
        for at, block in enumerate(MEMBERS[group]):
            saved[block] = (block, kept, at)
        return parts, down_head

    score_half = lax.all_gather(score_embed, "z", axis=0, tiled=True)
    (other4, other3, own4), down_head = forward(0, down_weight, head_weight)
    came4, came3 = swap(other4, "yhi"), swap(other3, "yhi")
    (other2, own3), _ = forward(1, down_head)
    came2 = swap(other2, "yhi")
    came4, own3 = lax.optimization_barrier((came4, own3))
    fore = shift(total_of(own4, came4).astype(bf16), 1)
    (other1, own2), _ = forward(2, down_head)
    came1 = swap(other1, "yhi")
    fore = shift(total_of(own3[:rows], came3[:rows], fore).astype(bf16), 1)
    back = shift(total_of(own3[rows:], came3[rows:]).astype(bf16), -1)
    (own1,), _ = forward(3, down_head)
    for own, came in ((own2, came2), (own1, came1)):
        fore = shift(total_of(own[:rows], came[:rows], fore).astype(bf16), 1)
        back = shift(total_of(own[rows : 2 * rows], came[rows : 2 * rows], back).astype(bf16), -1)
    score_unit = unit_rows(score_half)[0].astype(bf16)
    fore, back, score_unit = lax.optimization_barrier((fore, back, score_unit))
    own_start = y_hi * group_half + z * rows
    own_hidden = lax.dynamic_slice_in_dim(hidden_in, own_start, rows, 0)
    own_proj = dot(own_hidden, head_weight)
    audio_wide, audio_inverse = unit_rows(own_proj + total_of(own1[2 * rows :], came1[2 * rows :], fore, back))
    audio_own = audio_wide.astype(bf16)
    audio_unit = jnp.concatenate([audio_own, swap(audio_own, "yhi")], axis=0)
    far_start = (1 - y_hi) * group_half + z * rows
    partners = jnp.concatenate(
        [lax.dynamic_slice_in_dim(pair_index[0], start, rows, 0) for start in (own_start, far_start)]
    )
    coeffs = pair_coeffs(audio_unit, score_unit, partners, y_hi * group_half)
    grad_audio = dot(coeffs, score_unit)
    grad_audio = grad_audio[:rows] + swap(grad_audio[rows:].astype(bf16), "yhi").astype(f32)
    grad_embed = unit_backward(audio_wide, audio_inverse, grad_audio).astype(bf16)
    score_part = dot(coeffs, audio_unit, ((0,), (0,))).astype(bf16)
    item = lambda grad, *blocks: (grad, [saved[block] for block in blocks])
    pair = lambda step, half: ((half, step), (half, -step))
    both = lambda up, down: jnp.concatenate([up, down], axis=0)
    crossed0 = swap(grad_embed, "yhi")
    fore, back = shift(grad_embed, 1), shift(grad_embed, -1)
    fore, back, crossed0, score_part = lax.optimization_barrier((fore, back, crossed0, score_part))
    ring1 = both(back, fore)
    crossed1 = swap(ring1, "yhi")
    fore, back = shift(fore, 1), shift(back, -1)
    backward = lambda items, sums, *head: backward_blocks(items, packed, hidden_in, down_head, sums, *head)
    sums = backward([item(grad_embed, (0, 0)), item(crossed0, (1, 0)), item(ring1, *pair(1, 0))], None)
    fore, back, score_part, sums = lax.optimization_barrier((fore, back, score_part, sums))
    grad_score = lax.psum_scatter(score_part, "z", scatter_dimension=0, tiled=True)
    ring2 = both(back, fore)
    crossed2 = swap(ring2, "yhi")
    fore, back = shift(fore, 1), shift(back, -1)
    sums = backward([item(crossed1, *pair(1, 1)), item(ring2, *pair(2, 0))], sums)
    fore, back, sums, crossed2 = lax.optimization_barrier((fore, back, sums, crossed2))
    ring4, crossed4 = shift(fore, 1), shift_across(fore, 1)
    ring3 = both(back, fore)
    crossed3 = swap(ring3, "yhi")
    sums = backward([item(ring3, *pair(3, 0)), item(crossed2, *pair(2, 1))], sums)
    ring4, crossed4, sums = lax.optimization_barrier((ring4, crossed4, sums))
    items = [item(crossed3, *pair(3, 1)), item(ring4, (0, 4)), item(crossed4, (1, 4))]
    keep, give = backward(items, sums, head_weight)
    chip = total_of(keep, swap(give, "core")).astype(bf16)
    score_grad = score_backward(score_embed, grad_score)
    chip, score_grad = lax.optimization_barrier((chip, score_grad))
    landed = lax.all_to_all(chip, ("ylo", "x"), 0, 0)
    total = jnp.sum(landed.astype(f32), axis=0)
    ff = up_weight.shape[1]
    return (total[:, :ff], total[:, ff:].T, score_grad)


def solution(mesh):
    fine = Mesh(mesh.devices.reshape(2, 4, 2, 2, RING), ("ylo", "x", "core", "yhi", "z"))
    in_specs = (
        P(AUDIO, None),
        P(None, SCORE),
        P(SCORE, None),
        P(),
        P(AUDIO + SCORE, None),
        P(AUDIO, None),
    )
    out_specs = (P(AUDIO, SCORE), P(SCORE, AUDIO), P(AUDIO + SCORE, None))
    return jax.shard_map(
        per_device, mesh=fine, in_specs=in_specs, out_specs=out_specs, check_vma=False
    )
```

```python
import functools

import jax
import jax.numpy as jnp
from jax import lax
from jax.experimental import pallas as pl
from jax.experimental.pallas import tpu as pltpu
from jax.sharding import Mesh, PartitionSpec as P

logit_scale = 8.0
logit_bias = -3.0
epsilon = 1e-06
gelu_root = 0.7978845608028654
gelu_cubic = 0.044715

AUDIO = ("ylo", "x", "core")
SCORE = ("yhi", "z")
RING = 8
VMEM_BYTES = 56 * 1024 * 1024
f32 = jnp.float32
bf16 = jnp.bfloat16


def dot(left, right, dims=((1,), (0,))):
    return lax.dot_general(left, right, (dims, ((), ())), preferred_element_type=f32)


def unit_rows(values):
    wide = values.astype(f32)
    inverse = lax.rsqrt(jnp.sum(wide * wide, axis=-1, keepdims=True) + epsilon)
    return (wide * inverse, inverse)


def unit_backward(unit_wide, inverse, grad_unit):
    inner = jnp.sum(unit_wide * grad_unit, axis=-1, keepdims=True)
    return inverse * (grad_unit - unit_wide * inner)


def pair_coeffs(left, right, partner, first_column):
    logits = logit_scale * dot(left, right, ((1,), (1,))) + logit_bias
    columns = first_column + lax.iota(jnp.int32, right.shape[0])
    sign = jnp.where(partner[:, None] == columns[None, :], 1.0, -1.0)
    return (-logit_scale * sign * jax.nn.sigmoid(-sign * logits)).astype(bf16)


def swap(value, axis):
    return lax.ppermute(value, axis, [(0, 1), (1, 0)])


def shift(value, step):
    perm = [(i, (i + step) % RING) for i in range(RING)]
    perm += [(RING + i, RING + (i - step) % RING) for i in range(RING)]
    return lax.ppermute(value, ("core", "z"), perm)


def shift_across(value, step):
    to = lambda core, half, place: (core * 2 + half) * RING + place % RING
    perm = [
        (to(core, half, place), to(core, 1 - half, place + (step if core == 0 else -step)))
        for core in range(2)
        for half in range(2)
        for place in range(RING)
    ]
    return lax.ppermute(value, ("core", "yhi", "z"), perm)


GROUPS = (
    (((1, 4),), ((1, 3),), ((1, -3),), ((0, 4),)),
    (((1, 2), (1, -2)), ((0, 3), (0, -3))),
    (((0, 2), (0, -2)), ((1, 1),), ((1, -1),), ((1, 0),), ((0, 1), (0, -1), (0, 0))),
)
MEMBERS = tuple(tuple(block for piece in group for block in piece) for group in GROUPS)


def packed_place(half, place, core):
    return (half * (2 * RING) + place * 2 + core)[None]


def block_map(block):
    half, offset = block

    def index_map(i, packed):
        own_half, place, core = packed[0] // (2 * RING), packed[0] // 2 % RING, packed[0] % 2
        along = lax.rem(place + (1 - 2 * core) * offset + RING, RING)
        return lax.rem(own_half + half, 2) * RING + along, 0

    return index_map


def forward_kernel(pieces, first, packed_ref, *refs):
    count = sum(pieces)
    hidden = [ref[...] for ref in refs[:count]]
    refs = refs[count:]
    if first:
        up_ref, down_ref, head_ref = refs[:3]
        down_head_ref = refs[-1]
        down_head_ref[...] = dot(down_ref[...], head_ref[...]).astype(bf16)
        refs = refs[3:-1]
    else:
        up_ref, down_head_ref = refs[:2]
        refs = refs[2:]
    part_refs = refs[: len(pieces)]
    act_t_ref, slope_ref = refs[len(pieces) :]
    rows = hidden[0].shape[0]
    wide = jnp.concatenate(hidden, axis=0).astype(f32)
    square_mean = jnp.mean(wide * wide, axis=-1, keepdims=True)
    inverse = lax.rsqrt(square_mean + epsilon)
    normed = (wide * inverse).astype(bf16)
    pre = dot(normed, up_ref[...], ((1,), (1,)))
    tangent = jnp.tanh(gelu_root * (pre + gelu_cubic * (pre * pre * pre)))
    act = (0.5 * pre * (1.0 + tangent)).astype(bf16)
    part = dot(act, down_head_ref[...]).astype(bf16)
    at = 0
    for size, part_ref in zip(pieces, part_refs):
        part_ref[...] = part[at * rows : (at + size) * rows, :]
        at += size
    slope = 0.5 * (1.0 + tangent) + 0.5 * pre * (1.0 - tangent * tangent) * gelu_root * (
        1.0 + 3.0 * gelu_cubic * pre * pre
    )
    slope = (inverse * slope).astype(bf16)
    act_t = act.T
    for i in range(count):
        span = slice(i * rows, (i + 1) * rows)
        slope_ref[i] = slope[span, :]
        act_t_ref[i] = act_t[:, span]


def forward_blocks(group, packed, hidden_in, up_t, *weights):
    pieces = tuple(len(piece) for piece in GROUPS[group])
    count = sum(pieces)
    first = len(weights) == 2
    rows = hidden_in.shape[0] // (2 * RING)
    ff, width = up_t.shape
    embed = weights[-1].shape[1]
    flat = lambda i, packed: (0, 0)
    cube = lambda i, packed: (0, 0, 0)
    shapes = [jax.ShapeDtypeStruct((size * rows, embed), bf16) for size in pieces]
    shapes += [jax.ShapeDtypeStruct((count,) + dims, bf16) for dims in ((ff, rows), (rows, ff))]
    shapes += [jax.ShapeDtypeStruct((ff, embed), bf16)] if first else []
    out = pl.pallas_call(
        functools.partial(forward_kernel, pieces, first),
        grid_spec=pltpu.PrefetchScalarGridSpec(
            num_scalar_prefetch=1,
            grid=(1,),
            in_specs=[pl.BlockSpec((rows, width), block_map(block)) for block in MEMBERS[group]]
            + [pl.BlockSpec(w.shape, flat) for w in (up_t,) + weights],
            out_specs=[pl.BlockSpec(shape.shape, cube if len(shape.shape) == 3 else flat) for shape in shapes],
        ),
        out_shape=shapes,
        compiler_params=pltpu.CompilerParams(vmem_limit_bytes=VMEM_BYTES),
        cost_estimate=pl.CostEstimate(
            flops=2 * count * rows * ff * (width + embed),
            bytes_accessed=2 * count * rows * (width + embed + 2 * ff) + 2 * ff * (width + embed),
            transcendentals=count * rows * ff,
        ),
    )(packed, *([hidden_in] * count), up_t, *weights)
    parts, kept = out[: len(pieces)], out[len(pieces) : len(pieces) + 2]
    return parts, kept, out[-1]


def backward_kernel(count, blocks, first, last, packed_ref, *refs):
    join = lambda parts, axis: jnp.concatenate(parts, axis=axis) if len(parts) > 1 else parts[0]
    grad = join([ref[...] for ref in refs[:count]], 0)
    kept = refs[count : count + 3 * blocks]
    hidden = join([ref[...] for ref in kept[0::3]], 0)
    act_t, slope = join([ref[0] for ref in kept[1::3]], 1), join([ref[0] for ref in kept[2::3]], 0)
    refs = refs[count + 3 * blocks :]
    down_head_ref, refs = refs[0], refs[1:]
    if not first:
        up_in, act_in = refs[:2]
        refs = refs[2:]
    tile = 256
    grad_act = dot(grad, down_head_ref[...], ((1,), (1,)))
    grad_pre_t = (grad_act * slope.astype(f32)).astype(bf16).T
    act_sum = dot(act_t, grad)
    if not first:
        act_sum = act_sum + act_in[...]
    if last:
        head_ref, keep_ref, give_ref, total = refs
    else:
        up_acc, act_acc = refs
        act_acc[...] = act_sum
    width, ff = hidden.shape[1], act_sum.shape[0]
    for m in range(0, width, tile):
        up_sum = dot(grad_pre_t, hidden[:, m : m + tile])
        if not first:
            up_sum = up_sum + up_in[:, m : m + tile]
        if last:
            total[m : m + tile, :] = up_sum.T
        else:
            up_acc[:, m : m + tile] = up_sum
    if last:
        core = packed_ref[0] % 2
        act_grad = act_sum.astype(bf16)
        rows = keep_ref.shape[1]
        for side in range(2):
            for half, out_ref in ((core, keep_ref), (1 - core, give_ref)):
                for chip in range(keep_ref.shape[0]):
                    at = pl.multiple_of((2 * chip + half) * rows, rows)
                    out_ref[chip, :, side * ff : (side + 1) * ff] = total[pl.ds(at, rows), :].astype(bf16)
            if side == 0:
                for m in range(0, width, tile):
                    total[m : m + tile, :] = dot(head_ref[m : m + tile, :], act_grad, ((1,), (1,)))


def backward_blocks(items, packed, hidden_in, down_head, sums, head_weight=None):
    last = head_weight is not None
    whole = pl.BlockSpec(memory_space=pltpu.VMEM)
    args = [grad for grad, _ in items]
    specs = [whole] * len(items)
    places = [place for _, blocks in items for place in blocks]
    rows, width = hidden_in.shape[0] // (2 * RING), hidden_in.shape[1]
    for block, kept, at in places:
        args.append(hidden_in)
        specs.append(pl.BlockSpec((rows, width), block_map(block)))
        for array in kept:
            args.append(array)
            specs.append(pl.BlockSpec((1,) + array.shape[1:], lambda i, packed, at=at: (at, 0, 0)))
    ff, embed = down_head.shape
    args.append(down_head)
    aliases = {}
    if sums is not None:
        if not last:
            aliases = {len(args) + 1: 0, len(args) + 2: 1}
        args += list(sums)
    flops = 2 * len(places) * rows * ff * (2 * embed + width)
    if last:
        args.append(head_weight)
        shapes = [jax.ShapeDtypeStruct((8, width // 16, 2 * ff), bf16)] * 2
        scratch = [pltpu.VMEM((width, ff), f32)]
        flops += 2 * width * ff * embed
    else:
        shapes = [jax.ShapeDtypeStruct((ff, width), f32), jax.ShapeDtypeStruct((ff, embed), f32)]
        scratch = []
    specs += [whole] * (len(args) - len(specs))
    return pl.pallas_call(
        functools.partial(backward_kernel, len(items), len(places), sums is None, last),
        grid_spec=pltpu.PrefetchScalarGridSpec(
            num_scalar_prefetch=1,
            grid=(1,),
            in_specs=specs,
            out_specs=[whole] * 2,
            scratch_shapes=scratch,
        ),
        out_shape=shapes,
        input_output_aliases=aliases,
        compiler_params=pltpu.CompilerParams(vmem_limit_bytes=VMEM_BYTES),
        cost_estimate=pl.CostEstimate(flops=flops, bytes_accessed=8 * 1024 * 1024, transcendentals=0),
    )(packed, *args)


def score_kernel(embed_ref, grad_ref, out_ref):
    wide, inverse = unit_rows(embed_ref[...])
    out_ref[...] = unit_backward(wide, inverse, grad_ref[...].astype(f32))


def score_backward(score_embed, grad_score):
    return pl.pallas_call(
        score_kernel,
        out_shape=jax.ShapeDtypeStruct(score_embed.shape, f32),
        compiler_params=pltpu.CompilerParams(vmem_limit_bytes=VMEM_BYTES),
    )(score_embed, grad_score)


def total_of(*terms):
    return sum(term.astype(f32) for term in terms)


def per_device(hidden_in, up_weight, down_weight, head_weight, score_embed, pair_index):
    y_hi, z, core = (lax.axis_index(name).astype(jnp.int32) for name in ("yhi", "z", "core"))
    rows = hidden_in.shape[0] // (2 * RING)
    group_half = RING * rows
    packed = packed_place(y_hi, z, core)
    up_t = up_weight.T
    saved = {}

    def forward(group, *weights):
        parts, kept, down_head = forward_blocks(group, packed, hidden_in, up_t, *weights)
        for at, block in enumerate(MEMBERS[group]):
            saved[block] = (block, kept, at)
        return parts, down_head

    score_half = lax.all_gather(score_embed, "z", axis=0, tiled=True)
    (other4, other3, other3b, own4), down_head = forward(0, down_weight, head_weight)
    fore, across4 = shift(own4, 1), shift_across(other4, 1)
    across3, across3b = shift_across(other3, 1), shift_across(other3b, -1)
    (other2, own3), _ = forward(1, down_head)
    came2 = swap(other2, "yhi")
    fore = shift(total_of(own3[:rows], fore, across4).astype(bf16), 1)
    back = shift(own3[rows:], -1)
    (own2, other1, other1b, other0, own1), _ = forward(2, down_head)
    fore = shift(total_of(own2[:rows], came2[:rows], fore, across3).astype(bf16), 1)
    back = shift(total_of(own2[rows:], came2[rows:], back, across3b).astype(bf16), -1)
    across1, across1b, came0 = shift_across(other1, 1), shift_across(other1b, -1), swap(other0, "yhi")
    fore = shift(total_of(own1[:rows], fore).astype(bf16), 1)
    back = shift(total_of(own1[rows : 2 * rows], back).astype(bf16), -1)
    score_unit = unit_rows(score_half)[0].astype(bf16)
    fore, back, score_unit = lax.optimization_barrier((fore, back, score_unit))
    own_start = y_hi * group_half + z * rows
    own_hidden = lax.dynamic_slice_in_dim(hidden_in, own_start, rows, 0)
    own_proj = dot(own_hidden, head_weight)
    audio_wide, audio_inverse = unit_rows(own_proj + total_of(own1[2 * rows :], came0, across1, across1b, fore, back))
    audio_own = audio_wide.astype(bf16)
    audio_unit = jnp.concatenate([audio_own, swap(audio_own, "yhi")], axis=0)
    far_start = (1 - y_hi) * group_half + z * rows
    partners = jnp.concatenate(
        [lax.dynamic_slice_in_dim(pair_index[0], start, rows, 0) for start in (own_start, far_start)]
    )
    coeffs = pair_coeffs(audio_unit, score_unit, partners, y_hi * group_half)
    grad_audio = dot(coeffs, score_unit)
    grad_audio = grad_audio[:rows] + swap(grad_audio[rows:].astype(bf16), "yhi").astype(f32)
    grad_embed = unit_backward(audio_wide, audio_inverse, grad_audio).astype(bf16)
    score_part = dot(coeffs, audio_unit, ((0,), (0,))).astype(bf16)
    item = lambda grad, *blocks: (grad, [saved[block] for block in blocks])
    pair = lambda step, half: ((half, step), (half, -step))
    both = lambda up, down: jnp.concatenate([up, down], axis=0)
    crossed0 = swap(grad_embed, "yhi")
    fore, back = shift(grad_embed, 1), shift(grad_embed, -1)
    across, across_b = shift_across(grad_embed, 1), shift_across(grad_embed, -1)
    fore, back, crossed0, score_part = lax.optimization_barrier((fore, back, crossed0, score_part))
    ring1 = both(back, fore)
    fore, back = shift(fore, 1), shift(back, -1)
    backward = lambda items, sums, *head: backward_blocks(items, packed, hidden_in, down_head, sums, *head)
    sums = backward([item(grad_embed, (0, 0)), item(crossed0, (1, 0)), item(ring1, *pair(1, 0))], None)
    fore, back, across, across_b, sums = lax.optimization_barrier((fore, back, across, across_b, sums))
    ring2 = both(back, fore)
    crossed2 = swap(ring2, "yhi")
    fore, back = shift(fore, 1), shift(back, -1)
    sums = backward([item(across_b, (1, 1)), item(across, (1, -1)), item(ring2, *pair(2, 0))], sums)
    fore, back, sums, crossed2, score_part = lax.optimization_barrier((fore, back, sums, crossed2, score_part))
    grad_score = lax.psum_scatter(score_part, "z", scatter_dimension=0, tiled=True)
    ring4, crossed4 = shift(fore, 1), shift_across(fore, 1)
    ring3 = both(back, fore)
    crossed3 = swap(ring3, "yhi")
    sums = backward([item(ring3, *pair(3, 0)), item(crossed2, *pair(2, 1))], sums)
    ring4, crossed4, sums = lax.optimization_barrier((ring4, crossed4, sums))
    items = [item(crossed3, *pair(3, 1)), item(ring4, (0, 4)), item(crossed4, (1, 4))]
    keep, give = backward(items, sums, head_weight)
    chip = total_of(keep, swap(give, "core")).astype(bf16)
    landed = lax.all_to_all(chip, ("ylo", "x"), 0, 0)
    total = jnp.sum(landed.astype(f32), axis=0)
    ff = up_weight.shape[1]
    score_grad = score_backward(score_embed, grad_score)
    return (total[:, :ff], total[:, ff:].T, score_grad)


def solution(mesh):
    fine = Mesh(mesh.devices.reshape(2, 4, 2, 2, RING), ("ylo", "x", "core", "yhi", "z"))
    in_specs = (
        P(AUDIO, None),
        P(None, SCORE),
        P(SCORE, None),
        P(),
        P(AUDIO + SCORE, None),
        P(AUDIO, None),
    )
    out_specs = (P(AUDIO, SCORE), P(SCORE, AUDIO), P(AUDIO + SCORE, None))
    return jax.shard_map(
        per_device, mesh=fine, in_specs=in_specs, out_specs=out_specs, check_vma=False
    )
```

```python
import functools

import jax
import jax.numpy as jnp
from jax import lax
from jax.experimental import pallas as pl
from jax.experimental.pallas import tpu as pltpu
from jax.sharding import Mesh, PartitionSpec as P

logit_scale = 8.0
logit_bias = -3.0
epsilon = 1e-06
gelu_root = 0.7978845608028654
gelu_cubic = 0.044715

AUDIO = ("ylo", "x", "core")
SCORE = ("yhi", "z")
RING = 8
VMEM_BYTES = 56 * 1024 * 1024
f32 = jnp.float32
bf16 = jnp.bfloat16


def dot(left, right, dims=((1,), (0,))):
    return lax.dot_general(left, right, (dims, ((), ())), preferred_element_type=f32)


def unit_rows(values):
    wide = values.astype(f32)
    inverse = lax.rsqrt(jnp.sum(wide * wide, axis=-1, keepdims=True) + epsilon)
    return (wide * inverse, inverse)


def unit_backward(unit_wide, inverse, grad_unit):
    inner = jnp.sum(unit_wide * grad_unit, axis=-1, keepdims=True)
    return inverse * (grad_unit - unit_wide * inner)


def pair_coeffs(left, right, partner, first_column):
    logits = logit_scale * dot(left, right, ((1,), (1,))) + logit_bias
    columns = first_column + lax.iota(jnp.int32, right.shape[0])
    sign = jnp.where(partner[:, None] == columns[None, :], 1.0, -1.0)
    return (-logit_scale * sign * jax.nn.sigmoid(-sign * logits)).astype(bf16)


def swap(value, axis):
    return lax.ppermute(value, axis, [(0, 1), (1, 0)])


def shift(value, step):
    perm = [(i, (i + step) % RING) for i in range(RING)]
    perm += [(RING + i, RING + (i - step) % RING) for i in range(RING)]
    return lax.ppermute(value, ("core", "z"), perm)


def shift_across(value, step):
    to = lambda core, half, place: (core * 2 + half) * RING + place % RING
    perm = [
        (to(core, half, place), to(core, 1 - half, place + (step if core == 0 else -step)))
        for core in range(2)
        for half in range(2)
        for place in range(RING)
    ]
    return lax.ppermute(value, ("core", "yhi", "z"), perm)


GROUPS = (
    (((1, 4),), ((1, 3), (1, -3)), ((0, 4),)),
    (((1, 2), (1, -2)), ((1, 1), (1, -1), (1, 0)), ((0, 3),), ((0, -3),)),
    (((0, 2), (0, -2)), ((0, 1), (0, -1), (0, 0))),
)
MEMBERS = tuple(tuple(block for piece in group for block in piece) for group in GROUPS)


def packed_place(half, place, core):
    return (half * (2 * RING) + place * 2 + core)[None]


def block_map(block):
    half, offset = block

    def index_map(i, packed):
        own_half, place, core = packed[0] // (2 * RING), packed[0] // 2 % RING, packed[0] % 2
        along = lax.rem(place + (1 - 2 * core) * offset + RING, RING)
        return lax.rem(own_half + half, 2) * RING + along, 0

    return index_map


def forward_kernel(pieces, first, packed_ref, *refs):
    count = sum(pieces)
    hidden = [ref[...] for ref in refs[:count]]
    refs = refs[count:]
    if first:
        up_ref, down_ref, head_ref = refs[:3]
        down_head_ref = refs[-1]
        down_head_ref[...] = dot(down_ref[...], head_ref[...]).astype(bf16)
        refs = refs[3:-1]
    else:
        up_ref, down_head_ref = refs[:2]
        refs = refs[2:]
    part_refs = refs[: len(pieces)]
    act_t_ref, slope_ref = refs[len(pieces) :]
    rows = hidden[0].shape[0]
    wide = jnp.concatenate(hidden, axis=0).astype(f32)
    square_mean = jnp.mean(wide * wide, axis=-1, keepdims=True)
    inverse = lax.rsqrt(square_mean + epsilon)
    normed = (wide * inverse).astype(bf16)
    pre = dot(normed, up_ref[...], ((1,), (1,)))
    tangent = jnp.tanh(gelu_root * (pre + gelu_cubic * (pre * pre * pre)))
    act = (0.5 * pre * (1.0 + tangent)).astype(bf16)
    part = dot(act, down_head_ref[...]).astype(bf16)
    at = 0
    for size, part_ref in zip(pieces, part_refs):
        part_ref[...] = part[at * rows : (at + size) * rows, :]
        at += size
    slope = 0.5 * (1.0 + tangent) + 0.5 * pre * (1.0 - tangent * tangent) * gelu_root * (
        1.0 + 3.0 * gelu_cubic * pre * pre
    )
    slope = (inverse * slope).astype(bf16)
    act_t = act.T
    for i in range(count):
        span = slice(i * rows, (i + 1) * rows)
        slope_ref[i] = slope[span, :]
        act_t_ref[i] = act_t[:, span]


def forward_blocks(group, packed, hidden_in, up_t, *weights):
    pieces = tuple(len(piece) for piece in GROUPS[group])
    count = sum(pieces)
    first = len(weights) == 2
    rows = hidden_in.shape[0] // (2 * RING)
    ff, width = up_t.shape
    embed = weights[-1].shape[1]
    flat = lambda i, packed: (0, 0)
    cube = lambda i, packed: (0, 0, 0)
    shapes = [jax.ShapeDtypeStruct((size * rows, embed), bf16) for size in pieces]
    shapes += [jax.ShapeDtypeStruct((count,) + dims, bf16) for dims in ((ff, rows), (rows, ff))]
    shapes += [jax.ShapeDtypeStruct((ff, embed), bf16)] if first else []
    out = pl.pallas_call(
        functools.partial(forward_kernel, pieces, first),
        grid_spec=pltpu.PrefetchScalarGridSpec(
            num_scalar_prefetch=1,
            grid=(1,),
            in_specs=[pl.BlockSpec((rows, width), block_map(block)) for block in MEMBERS[group]]
            + [pl.BlockSpec(w.shape, flat) for w in (up_t,) + weights],
            out_specs=[pl.BlockSpec(shape.shape, cube if len(shape.shape) == 3 else flat) for shape in shapes],
        ),
        out_shape=shapes,
        compiler_params=pltpu.CompilerParams(vmem_limit_bytes=VMEM_BYTES),
        cost_estimate=pl.CostEstimate(
            flops=2 * count * rows * ff * (width + embed),
            bytes_accessed=2 * count * rows * (width + embed + 2 * ff) + 2 * ff * (width + embed),
            transcendentals=count * rows * ff,
        ),
    )(packed, *([hidden_in] * count), up_t, *weights)
    parts, kept = out[: len(pieces)], out[len(pieces) : len(pieces) + 2]
    return parts, kept, out[-1]


def backward_kernel(count, blocks, first, last, packed_ref, *refs):
    join = lambda parts, axis: jnp.concatenate(parts, axis=axis) if len(parts) > 1 else parts[0]
    grad = join([ref[...] for ref in refs[:count]], 0)
    kept = refs[count : count + 3 * blocks]
    hidden = join([ref[...] for ref in kept[0::3]], 0)
    act_t, slope = join([ref[0] for ref in kept[1::3]], 1), join([ref[0] for ref in kept[2::3]], 0)
    refs = refs[count + 3 * blocks :]
    down_head_ref, refs = refs[0], refs[1:]
    if not first:
        up_in, act_in = refs[:2]
        refs = refs[2:]
    tile = 256
    grad_act = dot(grad, down_head_ref[...], ((1,), (1,)))
    grad_pre_t = (grad_act * slope.astype(f32)).astype(bf16).T
    act_sum = dot(act_t, grad)
    if not first:
        act_sum = act_sum + act_in[...]
    if last:
        head_ref, keep_ref, give_ref, total = refs
    else:
        up_acc, act_acc = refs
        act_acc[...] = act_sum
    width, ff = hidden.shape[1], act_sum.shape[0]
    for m in range(0, width, tile):
        up_sum = dot(grad_pre_t, hidden[:, m : m + tile])
        if not first:
            up_sum = up_sum + up_in[:, m : m + tile]
        if last:
            total[m : m + tile, :] = up_sum.T
        else:
            up_acc[:, m : m + tile] = up_sum
    if last:
        core = packed_ref[0] % 2
        act_grad = act_sum.astype(bf16)
        rows = keep_ref.shape[1]
        for side in range(2):
            for half, out_ref in ((core, keep_ref), (1 - core, give_ref)):
                for chip in range(keep_ref.shape[0]):
                    at = pl.multiple_of((2 * chip + half) * rows, rows)
                    out_ref[chip, :, side * ff : (side + 1) * ff] = total[pl.ds(at, rows), :].astype(bf16)
            if side == 0:
                for m in range(0, width, tile):
                    total[m : m + tile, :] = dot(head_ref[m : m + tile, :], act_grad, ((1,), (1,)))


def backward_blocks(items, packed, hidden_in, down_head, sums, head_weight=None):
    last = head_weight is not None
    whole = pl.BlockSpec(memory_space=pltpu.VMEM)
    args = [grad for grad, _ in items]
    specs = [whole] * len(items)
    places = [place for _, blocks in items for place in blocks]
    rows, width = hidden_in.shape[0] // (2 * RING), hidden_in.shape[1]
    for block, kept, at in places:
        args.append(hidden_in)
        specs.append(pl.BlockSpec((rows, width), block_map(block)))
        for array in kept:
            args.append(array)
            specs.append(pl.BlockSpec((1,) + array.shape[1:], lambda i, packed, at=at: (at, 0, 0)))
    ff, embed = down_head.shape
    args.append(down_head)
    aliases = {}
    if sums is not None:
        if not last:
            aliases = {len(args) + 1: 0, len(args) + 2: 1}
        args += list(sums)
    flops = 2 * len(places) * rows * ff * (2 * embed + width)
    if last:
        args.append(head_weight)
        shapes = [jax.ShapeDtypeStruct((8, width // 16, 2 * ff), bf16)] * 2
        scratch = [pltpu.VMEM((width, ff), f32)]
        flops += 2 * width * ff * embed
    else:
        shapes = [jax.ShapeDtypeStruct((ff, width), f32), jax.ShapeDtypeStruct((ff, embed), f32)]
        scratch = []
    specs += [whole] * (len(args) - len(specs))
    return pl.pallas_call(
        functools.partial(backward_kernel, len(items), len(places), sums is None, last),
        grid_spec=pltpu.PrefetchScalarGridSpec(
            num_scalar_prefetch=1,
            grid=(1,),
            in_specs=specs,
            out_specs=[whole] * 2,
            scratch_shapes=scratch,
        ),
        out_shape=shapes,
        input_output_aliases=aliases,
        compiler_params=pltpu.CompilerParams(vmem_limit_bytes=VMEM_BYTES),
        cost_estimate=pl.CostEstimate(flops=flops, bytes_accessed=8 * 1024 * 1024, transcendentals=0),
    )(packed, *args)


def score_kernel(embed_ref, grad_ref, out_ref):
    wide, inverse = unit_rows(embed_ref[...])
    out_ref[...] = unit_backward(wide, inverse, grad_ref[...].astype(f32))


def score_backward(score_embed, grad_score):
    return pl.pallas_call(
        score_kernel,
        out_shape=jax.ShapeDtypeStruct(score_embed.shape, f32),
        compiler_params=pltpu.CompilerParams(vmem_limit_bytes=VMEM_BYTES),
    )(score_embed, grad_score)


def total_of(*terms):
    return sum(term.astype(f32) for term in terms)


def per_device(hidden_in, up_weight, down_weight, head_weight, score_embed, pair_index):
    y_hi, z, core = (lax.axis_index(name).astype(jnp.int32) for name in ("yhi", "z", "core"))
    rows = hidden_in.shape[0] // (2 * RING)
    group_half = RING * rows
    packed = packed_place(y_hi, z, core)
    up_t = up_weight.T
    saved = {}

    def forward(group, *weights):
        parts, kept, down_head = forward_blocks(group, packed, hidden_in, up_t, *weights)
        for at, block in enumerate(MEMBERS[group]):
            saved[block] = (block, kept, at)
        return parts, down_head

    score_half = lax.all_gather(score_embed, "z", axis=0, tiled=True)
    (other4, other3, own4), down_head = forward(0, down_weight, head_weight)
    fore, across4, came3 = shift(own4, 1), shift_across(other4, 1), swap(other3, "yhi")
    (other2, other1, own3, own3b), _ = forward(1, down_head)
    came2, came1 = swap(other2, "yhi"), swap(other1, "yhi")
    fore = shift(total_of(own3, came3[:rows], fore, across4).astype(bf16), 1)
    back = shift(total_of(own3b, came3[rows:]).astype(bf16), -1)
    (own2, own1), _ = forward(2, down_head)
    for own, came in ((own2, came2), (own1, came1)):
        fore = shift(total_of(own[:rows], came[:rows], fore).astype(bf16), 1)
        back = shift(total_of(own[rows : 2 * rows], came[rows : 2 * rows], back).astype(bf16), -1)
    score_unit = unit_rows(score_half)[0].astype(bf16)
    fore, back, score_unit = lax.optimization_barrier((fore, back, score_unit))
    own_start = y_hi * group_half + z * rows
    own_hidden = lax.dynamic_slice_in_dim(hidden_in, own_start, rows, 0)
    own_proj = dot(own_hidden, head_weight)
    audio_wide, audio_inverse = unit_rows(own_proj + total_of(own1[2 * rows :], came1[2 * rows :], fore, back))
    audio_own = audio_wide.astype(bf16)
    audio_unit = jnp.concatenate([audio_own, swap(audio_own, "yhi")], axis=0)
    far_start = (1 - y_hi) * group_half + z * rows
    partners = jnp.concatenate(
        [lax.dynamic_slice_in_dim(pair_index[0], start, rows, 0) for start in (own_start, far_start)]
    )
    coeffs = pair_coeffs(audio_unit, score_unit, partners, y_hi * group_half)
    grad_audio = dot(coeffs, score_unit)
    grad_audio = grad_audio[:rows] + swap(grad_audio[rows:].astype(bf16), "yhi").astype(f32)
    grad_embed = unit_backward(audio_wide, audio_inverse, grad_audio).astype(bf16)
    score_part = dot(coeffs, audio_unit, ((0,), (0,))).astype(bf16)
    item = lambda grad, *blocks: (grad, [saved[block] for block in blocks])
    pair = lambda step, half: ((half, step), (half, -step))
    both = lambda up, down: jnp.concatenate([up, down], axis=0)
    crossed0 = swap(grad_embed, "yhi")
    fore, back = shift(grad_embed, 1), shift(grad_embed, -1)
    fore, back, crossed0, score_part = lax.optimization_barrier((fore, back, crossed0, score_part))
    ring1 = both(back, fore)
    crossed1 = swap(ring1, "yhi")
    fore, back = shift(fore, 1), shift(back, -1)
    backward = lambda items, sums, *head: backward_blocks(items, packed, hidden_in, down_head, sums, *head)
    sums = backward([item(grad_embed, (0, 0)), item(crossed0, (1, 0)), item(ring1, *pair(1, 0))], None)
    fore, back, sums = lax.optimization_barrier((fore, back, sums))
    ring2 = both(back, fore)
    crossed2 = swap(ring2, "yhi")
    fore, back = shift(fore, 1), shift(back, -1)
    sums = backward([item(crossed1, *pair(1, 1)), item(ring2, *pair(2, 0))], sums)
    fore, back, sums, crossed2, score_part = lax.optimization_barrier((fore, back, sums, crossed2, score_part))
    grad_score = lax.psum_scatter(score_part, "z", scatter_dimension=0, tiled=True)
    ring4, crossed4 = shift(fore, 1), shift_across(fore, 1)
    ring3 = both(back, fore)
    crossed3 = swap(ring3, "yhi")
    sums = backward([item(ring3, *pair(3, 0)), item(crossed2, *pair(2, 1))], sums)
    ring4, crossed4, sums = lax.optimization_barrier((ring4, crossed4, sums))
    items = [item(crossed3, *pair(3, 1)), item(ring4, (0, 4)), item(crossed4, (1, 4))]
    keep, give = backward(items, sums, head_weight)
    chip = total_of(keep, swap(give, "core")).astype(bf16)
    landed = lax.all_to_all(chip, ("ylo", "x"), 0, 0)
    total = jnp.sum(landed.astype(f32), axis=0)
    ff = up_weight.shape[1]
    score_grad = score_backward(score_embed, grad_score)
    return (total[:, :ff], total[:, ff:].T, score_grad)


def solution(mesh):
    fine = Mesh(mesh.devices.reshape(2, 4, 2, 2, RING), ("ylo", "x", "core", "yhi", "z"))
    in_specs = (
        P(AUDIO, None),
        P(None, SCORE),
        P(SCORE, None),
        P(),
        P(AUDIO + SCORE, None),
        P(AUDIO, None),
    )
    out_specs = (P(AUDIO, SCORE), P(SCORE, AUDIO), P(AUDIO + SCORE, None))
    return jax.shard_map(
        per_device, mesh=fine, in_specs=in_specs, out_specs=out_specs, check_vma=False
    )
```

```python
import functools

import jax
import jax.numpy as jnp
from jax import lax
from jax.experimental import pallas as pl
from jax.experimental.pallas import tpu as pltpu
from jax.sharding import Mesh, PartitionSpec as P

logit_scale = 8.0
logit_bias = -3.0
epsilon = 1e-06
gelu_root = 0.7978845608028654
gelu_cubic = 0.044715

AUDIO = ("ylo", "x", "core")
SCORE = ("yhi", "z")
RING = 8
VMEM_BYTES = 56 * 1024 * 1024
f32 = jnp.float32
bf16 = jnp.bfloat16


def dot(left, right, dims=((1,), (0,))):
    return lax.dot_general(left, right, (dims, ((), ())), preferred_element_type=f32)


def unit_rows(values):
    wide = values.astype(f32)
    inverse = lax.rsqrt(jnp.sum(wide * wide, axis=-1, keepdims=True) + epsilon)
    return (wide * inverse, inverse)


def unit_backward(unit_wide, inverse, grad_unit):
    inner = jnp.sum(unit_wide * grad_unit, axis=-1, keepdims=True)
    return inverse * (grad_unit - unit_wide * inner)


def pair_coeffs(left, right, partner, first_column):
    logits = logit_scale * dot(left, right, ((1,), (1,))) + logit_bias
    columns = first_column + lax.iota(jnp.int32, right.shape[0])
    sign = jnp.where(partner[:, None] == columns[None, :], 1.0, -1.0)
    return (-logit_scale * sign * jax.nn.sigmoid(-sign * logits)).astype(bf16)


def swap(value, axis):
    return lax.ppermute(value, axis, [(0, 1), (1, 0)])


def shift(value, step):
    perm = [(i, (i + step) % RING) for i in range(RING)]
    perm += [(RING + i, RING + (i - step) % RING) for i in range(RING)]
    return lax.ppermute(value, ("core", "z"), perm)


def shift_across(value, step):
    to = lambda core, half, place: (core * 2 + half) * RING + place % RING
    perm = [
        (to(core, half, place), to(core, 1 - half, place + (step if core == 0 else -step)))
        for core in range(2)
        for half in range(2)
        for place in range(RING)
    ]
    return lax.ppermute(value, ("core", "yhi", "z"), perm)


GROUPS = (
    (((1, 4),), ((1, 3), (1, -3)), ((0, 4),)),
    (((1, 2), (1, -2)), ((1, 1), (1, -1), (1, 0)), ((0, 3),), ((0, -3),)),
    (((0, 2), (0, -2)), ((0, 1), (0, -1), (0, 0))),
)
MEMBERS = tuple(tuple(block for piece in group for block in piece) for group in GROUPS)


def packed_place(half, place, core):
    return (half * (2 * RING) + place * 2 + core)[None]


def block_map(block):
    half, offset = block

    def index_map(i, packed):
        own_half, place, core = packed[0] // (2 * RING), packed[0] // 2 % RING, packed[0] % 2
        along = lax.rem(place + (1 - 2 * core) * offset + RING, RING)
        return lax.rem(own_half + half, 2) * RING + along, 0

    return index_map


def forward_kernel(pieces, first, packed_ref, *refs):
    count = sum(pieces)
    hidden = [ref[...] for ref in refs[:count]]
    refs = refs[count:]
    if first:
        up_ref, down_ref, head_ref = refs[:3]
        down_head_ref = refs[-1]
        down_head_ref[...] = dot(down_ref[...], head_ref[...]).astype(bf16)
        refs = refs[3:-1]
    else:
        up_ref, down_head_ref = refs[:2]
        refs = refs[2:]
    part_refs = refs[: len(pieces)]
    act_t_ref, slope_ref = refs[len(pieces) :]
    rows = hidden[0].shape[0]
    wide = jnp.concatenate(hidden, axis=0).astype(f32)
    square_mean = jnp.mean(wide * wide, axis=-1, keepdims=True)
    inverse = lax.rsqrt(square_mean + epsilon)
    normed = (wide * inverse).astype(bf16)
    pre = dot(normed, up_ref[...], ((1,), (1,)))
    tangent = jnp.tanh(gelu_root * (pre + gelu_cubic * (pre * pre * pre)))
    act = (0.5 * pre * (1.0 + tangent)).astype(bf16)
    part = dot(act, down_head_ref[...]).astype(bf16)
    at = 0
    for size, part_ref in zip(pieces, part_refs):
        part_ref[...] = part[at * rows : (at + size) * rows, :]
        at += size
    slope = 0.5 * (1.0 + tangent) + 0.5 * pre * (1.0 - tangent * tangent) * gelu_root * (
        1.0 + 3.0 * gelu_cubic * pre * pre
    )
    slope = (inverse * slope).astype(bf16)
    act_t = act.T
    for i in range(count):
        span = slice(i * rows, (i + 1) * rows)
        slope_ref[i] = slope[span, :]
        act_t_ref[i] = act_t[:, span]


def forward_blocks(group, packed, hidden_in, up_t, *weights):
    pieces = tuple(len(piece) for piece in GROUPS[group])
    count = sum(pieces)
    first = len(weights) == 2
    rows = hidden_in.shape[0] // (2 * RING)
    ff, width = up_t.shape
    embed = weights[-1].shape[1]
    flat = lambda i, packed: (0, 0)
    cube = lambda i, packed: (0, 0, 0)
    shapes = [jax.ShapeDtypeStruct((size * rows, embed), bf16) for size in pieces]
    shapes += [jax.ShapeDtypeStruct((count,) + dims, bf16) for dims in ((ff, rows), (rows, ff))]
    shapes += [jax.ShapeDtypeStruct((ff, embed), bf16)] if first else []
    out = pl.pallas_call(
        functools.partial(forward_kernel, pieces, first),
        grid_spec=pltpu.PrefetchScalarGridSpec(
            num_scalar_prefetch=1,
            grid=(1,),
            in_specs=[pl.BlockSpec((rows, width), block_map(block)) for block in MEMBERS[group]]
            + [pl.BlockSpec(w.shape, flat) for w in (up_t,) + weights],
            out_specs=[pl.BlockSpec(shape.shape, cube if len(shape.shape) == 3 else flat) for shape in shapes],
        ),
        out_shape=shapes,
        compiler_params=pltpu.CompilerParams(vmem_limit_bytes=VMEM_BYTES),
        cost_estimate=pl.CostEstimate(
            flops=2 * count * rows * ff * (width + embed),
            bytes_accessed=2 * count * rows * (width + embed + 2 * ff) + 2 * ff * (width + embed),
            transcendentals=count * rows * ff,
        ),
    )(packed, *([hidden_in] * count), up_t, *weights)
    parts, kept = out[: len(pieces)], out[len(pieces) : len(pieces) + 2]
    return parts, kept, out[-1]


def backward_kernel(count, blocks, first, last, packed_ref, *refs):
    join = lambda parts, axis: jnp.concatenate(parts, axis=axis) if len(parts) > 1 else parts[0]
    grad = join([ref[...] for ref in refs[:count]], 0)
    kept = refs[count : count + 3 * blocks]
    hidden = join([ref[...] for ref in kept[0::3]], 0)
    act_t, slope = join([ref[0] for ref in kept[1::3]], 1), join([ref[0] for ref in kept[2::3]], 0)
    refs = refs[count + 3 * blocks :]
    down_head_ref, refs = refs[0], refs[1:]
    if not first:
        up_in, act_in = refs[:2]
        refs = refs[2:]
    tile = 256
    grad_act = dot(grad, down_head_ref[...], ((1,), (1,)))
    grad_pre_t = (grad_act * slope.astype(f32)).astype(bf16).T
    act_sum = dot(act_t, grad)
    if not first:
        act_sum = act_sum + act_in[...]
    if last:
        head_ref, keep_ref, give_ref, total = refs
    else:
        up_acc, act_acc = refs
        act_acc[...] = act_sum
    width, ff = hidden.shape[1], act_sum.shape[0]
    for m in range(0, width, tile):
        up_sum = dot(grad_pre_t, hidden[:, m : m + tile])
        if not first:
            up_sum = up_sum + up_in[:, m : m + tile]
        if last:
            total[m : m + tile, :ff] = up_sum.T.astype(bf16)
        else:
            up_acc[:, m : m + tile] = up_sum
    if last:
        core = packed_ref[0] % 2
        act_grad = act_sum.astype(bf16)
        rows = keep_ref.shape[1]
        for m in range(0, width, tile):
            total[m : m + tile, ff:] = dot(head_ref[m : m + tile, :], act_grad, ((1,), (1,))).astype(bf16)
        for half, out_ref in ((core, keep_ref), (1 - core, give_ref)):
            for chip in range(keep_ref.shape[0]):
                at = pl.multiple_of((2 * chip + half) * rows, rows)
                out_ref[chip] = total[pl.ds(at, rows), :]


def backward_blocks(items, packed, hidden_in, down_head, sums, head_weight=None):
    last = head_weight is not None
    whole = pl.BlockSpec(memory_space=pltpu.VMEM)
    args = [grad for grad, _ in items]
    specs = [whole] * len(items)
    places = [place for _, blocks in items for place in blocks]
    rows, width = hidden_in.shape[0] // (2 * RING), hidden_in.shape[1]
    for block, kept, at in places:
        args.append(hidden_in)
        specs.append(pl.BlockSpec((rows, width), block_map(block)))
        for array in kept:
            args.append(array)
            specs.append(pl.BlockSpec((1,) + array.shape[1:], lambda i, packed, at=at: (at, 0, 0)))
    ff, embed = down_head.shape
    args.append(down_head)
    aliases = {}
    if sums is not None:
        if not last:
            aliases = {len(args) + 1: 0, len(args) + 2: 1}
        args += list(sums)
    if last:
        args.append(head_weight)
        shapes = [jax.ShapeDtypeStruct((8, width // 16, 2 * ff), bf16)] * 2
        scratch = [pltpu.VMEM((width, 2 * ff), bf16)]
    else:
        shapes = [jax.ShapeDtypeStruct((ff, width), f32), jax.ShapeDtypeStruct((ff, embed), f32)]
        scratch = []
    specs += [whole] * (len(args) - len(specs))
    return pl.pallas_call(
        functools.partial(backward_kernel, len(items), len(places), sums is None, last),
        grid_spec=pltpu.PrefetchScalarGridSpec(
            num_scalar_prefetch=1,
            grid=(1,),
            in_specs=specs,
            out_specs=[whole] * 2,
            scratch_shapes=scratch,
        ),
        out_shape=shapes,
        input_output_aliases=aliases,
        compiler_params=pltpu.CompilerParams(vmem_limit_bytes=VMEM_BYTES),
        cost_estimate=pl.CostEstimate(flops=0, bytes_accessed=0, transcendentals=0),
    )(packed, *args)


def score_kernel(embed_ref, grad_ref, out_ref):
    wide, inverse = unit_rows(embed_ref[...])
    out_ref[...] = unit_backward(wide, inverse, grad_ref[...].astype(f32))


def score_backward(score_embed, grad_score):
    return pl.pallas_call(
        score_kernel,
        out_shape=jax.ShapeDtypeStruct(score_embed.shape, f32),
        compiler_params=pltpu.CompilerParams(vmem_limit_bytes=VMEM_BYTES),
    )(score_embed, grad_score)


def total_of(*terms):
    return sum(term.astype(f32) for term in terms)


def per_device(hidden_in, up_weight, down_weight, head_weight, score_embed, pair_index):
    y_hi, z, core = (lax.axis_index(name).astype(jnp.int32) for name in ("yhi", "z", "core"))
    rows = hidden_in.shape[0] // (2 * RING)
    group_half = RING * rows
    packed = packed_place(y_hi, z, core)
    up_t = up_weight.T
    saved = {}

    def forward(group, *weights):
        parts, kept, down_head = forward_blocks(group, packed, hidden_in, up_t, *weights)
        for at, block in enumerate(MEMBERS[group]):
            saved[block] = (block, kept, at)
        return parts, down_head

    score_half = lax.all_gather(score_embed, "z", axis=0, tiled=True)
    (other4, other3, own4), down_head = forward(0, down_weight, head_weight)
    fore, across4, came3 = shift(own4, 1), shift_across(other4, 1), swap(other3, "yhi")
    (other2, other1, own3, own3b), _ = forward(1, down_head)
    came2, came1 = swap(other2, "yhi"), swap(other1, "yhi")
    fore = shift(total_of(own3, came3[:rows], fore, across4).astype(bf16), 1)
    back = shift(total_of(own3b, came3[rows:]).astype(bf16), -1)
    (own2, own1), _ = forward(2, down_head)
    for own, came in ((own2, came2), (own1, came1)):
        fore = shift(total_of(own[:rows], came[:rows], fore).astype(bf16), 1)
        back = shift(total_of(own[rows : 2 * rows], came[rows : 2 * rows], back).astype(bf16), -1)
    score_unit = unit_rows(score_half)[0].astype(bf16)
    fore, back, score_unit = lax.optimization_barrier((fore, back, score_unit))
    own_start = y_hi * group_half + z * rows
    own_hidden = lax.dynamic_slice_in_dim(hidden_in, own_start, rows, 0)
    own_proj = dot(own_hidden, head_weight)
    audio_wide, audio_inverse = unit_rows(own_proj + total_of(own1[2 * rows :], came1[2 * rows :], fore, back))
    audio_own = audio_wide.astype(bf16)
    audio_unit = jnp.concatenate([audio_own, swap(audio_own, "yhi")], axis=0)
    far_start = (1 - y_hi) * group_half + z * rows
    partners = jnp.concatenate(
        [lax.dynamic_slice_in_dim(pair_index[0], start, rows, 0) for start in (own_start, far_start)]
    )
    coeffs = pair_coeffs(audio_unit, score_unit, partners, y_hi * group_half)
    grad_audio = dot(coeffs, score_unit)
    grad_audio = grad_audio[:rows] + swap(grad_audio[rows:].astype(bf16), "yhi").astype(f32)
    grad_embed = unit_backward(audio_wide, audio_inverse, grad_audio).astype(bf16)
    score_part = dot(coeffs, audio_unit, ((0,), (0,))).astype(bf16)
    item = lambda grad, *blocks: (grad, [saved[block] for block in blocks])
    pair = lambda step, half: ((half, step), (half, -step))
    both = lambda up, down: jnp.concatenate([up, down], axis=0)
    fore, back = shift(grad_embed, 1), shift(grad_embed, -1)
    own_block, score_part = lax.optimization_barrier((grad_embed, score_part))
    crossed0 = swap(own_block, "yhi")
    fore, back, crossed0, score_part = lax.optimization_barrier((fore, back, crossed0, score_part))
    ring1 = both(back, fore)
    crossed1 = swap(ring1, "yhi")
    fore, back = shift(fore, 1), shift(back, -1)
    backward = lambda items, sums, *head: backward_blocks(items, packed, hidden_in, down_head, sums, *head)
    sums = backward([item(grad_embed, (0, 0)), item(crossed0, (1, 0)), item(ring1, *pair(1, 0))], None)
    fore, back, sums = lax.optimization_barrier((fore, back, sums))
    ring2 = both(back, fore)
    crossed2 = swap(ring2, "yhi")
    fore, back = shift(fore, 1), shift(back, -1)
    sums = backward([item(crossed1, *pair(1, 1)), item(ring2, *pair(2, 0))], sums)
    fore, back, sums, score_part = lax.optimization_barrier((fore, back, sums, score_part))
    grad_score = lax.psum_scatter(score_part, "z", scatter_dimension=0, tiled=True)
    ring4, crossed4 = shift(fore, 1), shift_across(fore, 1)
    ring3 = both(back, fore)
    crossed3 = swap(ring3, "yhi")
    sums = backward([item(ring3, *pair(3, 0)), item(crossed2, *pair(2, 1))], sums)
    ring4, crossed4, sums = lax.optimization_barrier((ring4, crossed4, sums))
    items = [item(crossed3, *pair(3, 1)), item(ring4, (0, 4)), item(crossed4, (1, 4))]
    keep, give = backward(items, sums, head_weight)
    chip = total_of(keep, swap(give, "core")).astype(bf16)
    landed = lax.all_to_all(chip, ("ylo", "x"), 0, 0)
    total = jnp.sum(landed.astype(f32), axis=0)
    ff = up_weight.shape[1]
    score_grad = score_backward(score_embed, grad_score)
    return (total[:, :ff], total[:, ff:].T, score_grad)


def solution(mesh):
    fine = Mesh(mesh.devices.reshape(2, 4, 2, 2, RING), ("ylo", "x", "core", "yhi", "z"))
    in_specs = (
        P(AUDIO, None),
        P(None, SCORE),
        P(SCORE, None),
        P(),
        P(AUDIO + SCORE, None),
        P(AUDIO, None),
    )
    out_specs = (P(AUDIO, SCORE), P(SCORE, AUDIO), P(AUDIO + SCORE, None))
    return jax.shard_map(
        per_device, mesh=fine, in_specs=in_specs, out_specs=out_specs, check_vma=False
    )
```

```python
import functools

import jax
import jax.numpy as jnp
from jax import lax
from jax.experimental import pallas as pl
from jax.experimental.pallas import tpu as pltpu
from jax.sharding import Mesh, PartitionSpec as P

logit_scale = 8.0
logit_bias = -3.0
epsilon = 1e-06
gelu_root = 0.7978845608028654
gelu_cubic = 0.044715

AUDIO = ("ylo", "x", "core")
SCORE = ("yhi", "z")
RING = 8
VMEM_BYTES = 56 * 1024 * 1024
f32 = jnp.float32
bf16 = jnp.bfloat16


def dot(left, right, dims=((1,), (0,))):
    return lax.dot_general(left, right, (dims, ((), ())), preferred_element_type=f32)


def unit_rows(values):
    wide = values.astype(f32)
    inverse = lax.rsqrt(jnp.sum(wide * wide, axis=-1, keepdims=True) + epsilon)
    return (wide * inverse, inverse)


def unit_backward(unit_wide, inverse, grad_unit):
    inner = jnp.sum(unit_wide * grad_unit, axis=-1, keepdims=True)
    return inverse * (grad_unit - unit_wide * inner)


def pair_coeffs(left, right, partner, first_column):
    logits = logit_scale * dot(left, right, ((1,), (1,))) + logit_bias
    columns = first_column + lax.iota(jnp.int32, right.shape[0])
    sign = jnp.where(partner[:, None] == columns[None, :], 1.0, -1.0)
    return (-logit_scale * sign * jax.nn.sigmoid(-sign * logits)).astype(bf16)


def swap(value, axis):
    return lax.ppermute(value, axis, [(0, 1), (1, 0)])


def shift(value, step):
    perm = [(i, (i + step) % RING) for i in range(RING)]
    perm += [(RING + i, RING + (i - step) % RING) for i in range(RING)]
    return lax.ppermute(value, ("core", "z"), perm)


def shift_across(value, step):
    to = lambda core, half, place: (core * 2 + half) * RING + place % RING
    perm = [
        (to(core, half, place), to(core, 1 - half, place + (step if core == 0 else -step)))
        for core in range(2)
        for half in range(2)
        for place in range(RING)
    ]
    return lax.ppermute(value, ("core", "yhi", "z"), perm)


GROUPS = (
    (((1, 4),), ((1, 3), (1, -3)), ((0, 4),)),
    (((1, 2), (1, -2)), ((1, 1), (1, -1), (1, 0)), ((0, 3),), ((0, -3),)),
    (((0, 2), (0, -2)), ((0, 1), (0, -1), (0, 0))),
)
MEMBERS = tuple(tuple(block for piece in group for block in piece) for group in GROUPS)


def packed_place(half, place, core):
    return (half * (2 * RING) + place * 2 + core)[None]


def block_map(block):
    half, offset = block

    def index_map(i, packed):
        own_half, place, core = packed[0] // (2 * RING), packed[0] // 2 % RING, packed[0] % 2
        along = lax.rem(place + (1 - 2 * core) * offset + RING, RING)
        return lax.rem(own_half + half, 2) * RING + along, 0

    return index_map


def forward_kernel(pieces, first, packed_ref, *refs):
    count = sum(pieces)
    hidden = [ref[...] for ref in refs[:count]]
    refs = refs[count:]
    if first:
        up_ref, down_ref, head_ref = refs[:3]
        down_head_ref = refs[-1]
        down_head_ref[...] = dot(down_ref[...], head_ref[...]).astype(bf16)
        refs = refs[3:-1]
    else:
        up_ref, down_head_ref = refs[:2]
        refs = refs[2:]
    part_refs = refs[: len(pieces)]
    act_t_ref, slope_ref = refs[len(pieces) :]
    rows = hidden[0].shape[0]
    wide = jnp.concatenate(hidden, axis=0).astype(f32)
    square_mean = jnp.mean(wide * wide, axis=-1, keepdims=True)
    inverse = lax.rsqrt(square_mean + epsilon)
    normed = (wide * inverse).astype(bf16)
    pre = dot(normed, up_ref[...], ((1,), (1,)))
    tangent = jnp.tanh(gelu_root * (pre + gelu_cubic * (pre * pre * pre)))
    act = (0.5 * pre * (1.0 + tangent)).astype(bf16)
    part = dot(act, down_head_ref[...]).astype(bf16)
    at = 0
    for size, part_ref in zip(pieces, part_refs):
        part_ref[...] = part[at * rows : (at + size) * rows, :]
        at += size
    slope = 0.5 * (1.0 + tangent) + 0.5 * pre * (1.0 - tangent * tangent) * gelu_root * (
        1.0 + 3.0 * gelu_cubic * pre * pre
    )
    slope = (inverse * slope).astype(bf16)
    act_t = act.T
    for i in range(count):
        span = slice(i * rows, (i + 1) * rows)
        slope_ref[i] = slope[span, :]
        act_t_ref[i] = act_t[:, span]


def forward_blocks(group, packed, hidden_in, up_t, *weights):
    pieces = tuple(len(piece) for piece in GROUPS[group])
    count = sum(pieces)
    first = len(weights) == 2
    rows = hidden_in.shape[0] // (2 * RING)
    ff, width = up_t.shape
    embed = weights[-1].shape[1]
    flat = lambda i, packed: (0, 0)
    cube = lambda i, packed: (0, 0, 0)
    shapes = [jax.ShapeDtypeStruct((size * rows, embed), bf16) for size in pieces]
    shapes += [jax.ShapeDtypeStruct((count,) + dims, bf16) for dims in ((ff, rows), (rows, ff))]
    shapes += [jax.ShapeDtypeStruct((ff, embed), bf16)] if first else []
    out = pl.pallas_call(
        functools.partial(forward_kernel, pieces, first),
        grid_spec=pltpu.PrefetchScalarGridSpec(
            num_scalar_prefetch=1,
            grid=(1,),
            in_specs=[pl.BlockSpec((rows, width), block_map(block)) for block in MEMBERS[group]]
            + [pl.BlockSpec(w.shape, flat) for w in (up_t,) + weights],
            out_specs=[pl.BlockSpec(shape.shape, cube if len(shape.shape) == 3 else flat) for shape in shapes],
        ),
        out_shape=shapes,
        compiler_params=pltpu.CompilerParams(vmem_limit_bytes=VMEM_BYTES),
        cost_estimate=pl.CostEstimate(
            flops=2 * count * rows * ff * (width + embed),
            bytes_accessed=2 * count * rows * (width + embed + 2 * ff) + 2 * ff * (width + embed),
            transcendentals=count * rows * ff,
        ),
    )(packed, *([hidden_in] * count), up_t, *weights)
    parts, kept = out[: len(pieces)], out[len(pieces) : len(pieces) + 2]
    return parts, kept, out[-1]


def backward_kernel(count, blocks, first, last, packed_ref, *refs):
    join = lambda parts, axis: jnp.concatenate(parts, axis=axis) if len(parts) > 1 else parts[0]
    grad = join([ref[...] for ref in refs[:count]], 0)
    kept = refs[count : count + 3 * blocks]
    hidden = join([ref[...] for ref in kept[0::3]], 0)
    act_t, slope = join([ref[0] for ref in kept[1::3]], 1), join([ref[0] for ref in kept[2::3]], 0)
    refs = refs[count + 3 * blocks :]
    down_head_ref, refs = refs[0], refs[1:]
    if not first:
        up_in, act_in = refs[:2]
        refs = refs[2:]
    tile = 256
    grad_act = dot(grad, down_head_ref[...], ((1,), (1,)))
    grad_pre_t = (grad_act * slope.astype(f32)).astype(bf16).T
    act_sum = dot(act_t, grad)
    if not first:
        act_sum = act_sum + act_in[...]
    if last:
        head_ref, keep_ref, give_ref, total = refs
    else:
        up_acc, act_acc = refs
        act_acc[...] = act_sum
    width, ff = hidden.shape[1], act_sum.shape[0]
    for m in range(0, width, tile):
        up_sum = dot(grad_pre_t, hidden[:, m : m + tile])
        if not first:
            up_sum = up_sum + up_in[:, m : m + tile]
        if last:
            total[m : m + tile, :ff] = up_sum.T.astype(bf16)
        else:
            up_acc[:, m : m + tile] = up_sum
    if last:
        core = packed_ref[0] % 2
        act_grad = act_sum.astype(bf16)
        rows = keep_ref.shape[1]
        for m in range(0, width, tile):
            total[m : m + tile, ff:] = dot(head_ref[m : m + tile, :], act_grad, ((1,), (1,))).astype(bf16)
        for half, out_ref in ((core, keep_ref), (1 - core, give_ref)):
            for chip in range(keep_ref.shape[0]):
                at = pl.multiple_of((2 * chip + half) * rows, rows)
                out_ref[chip] = total[pl.ds(at, rows), :]


def backward_blocks(items, packed, hidden_in, down_head, sums, head_weight=None):
    last = head_weight is not None
    whole = pl.BlockSpec(memory_space=pltpu.VMEM)
    args = [grad for grad, _ in items]
    specs = [whole] * len(items)
    places = [place for _, blocks in items for place in blocks]
    rows, width = hidden_in.shape[0] // (2 * RING), hidden_in.shape[1]
    for block, kept, at in places:
        args.append(hidden_in)
        specs.append(pl.BlockSpec((rows, width), block_map(block)))
        for array in kept:
            args.append(array)
            specs.append(pl.BlockSpec((1,) + array.shape[1:], lambda i, packed, at=at: (at, 0, 0)))
    ff, embed = down_head.shape
    args.append(down_head)
    aliases = {}
    if sums is not None:
        if not last:
            aliases = {len(args) + 1: 0, len(args) + 2: 1}
        args += list(sums)
    if last:
        args.append(head_weight)
        shapes = [jax.ShapeDtypeStruct((8, width // 16, 2 * ff), bf16)] * 2
        scratch = [pltpu.VMEM((width, 2 * ff), bf16)]
    else:
        shapes = [jax.ShapeDtypeStruct((ff, width), f32), jax.ShapeDtypeStruct((ff, embed), f32)]
        scratch = []
    specs += [whole] * (len(args) - len(specs))
    return pl.pallas_call(
        functools.partial(backward_kernel, len(items), len(places), sums is None, last),
        grid_spec=pltpu.PrefetchScalarGridSpec(
            num_scalar_prefetch=1,
            grid=(1,),
            in_specs=specs,
            out_specs=[whole] * 2,
            scratch_shapes=scratch,
        ),
        out_shape=shapes,
        input_output_aliases=aliases,
        compiler_params=pltpu.CompilerParams(vmem_limit_bytes=VMEM_BYTES),
        cost_estimate=pl.CostEstimate(flops=0, bytes_accessed=0, transcendentals=0),
    )(packed, *args)


def score_kernel(embed_ref, grad_ref, out_ref):
    wide, inverse = unit_rows(embed_ref[...])
    out_ref[...] = unit_backward(wide, inverse, grad_ref[...].astype(f32))


def score_backward(score_embed, grad_score):
    return pl.pallas_call(
        score_kernel,
        out_shape=jax.ShapeDtypeStruct(score_embed.shape, f32),
        compiler_params=pltpu.CompilerParams(vmem_limit_bytes=VMEM_BYTES),
    )(score_embed, grad_score)


def total_of(*terms):
    return sum(term.astype(f32) for term in terms)


def per_device(hidden_in, up_weight, down_weight, head_weight, score_embed, pair_index):
    y_hi, z, core = (lax.axis_index(name).astype(jnp.int32) for name in ("yhi", "z", "core"))
    rows = hidden_in.shape[0] // (2 * RING)
    group_half = RING * rows
    packed = packed_place(y_hi, z, core)
    up_t = up_weight.T
    saved = {}

    def forward(group, *weights):
        parts, kept, down_head = forward_blocks(group, packed, hidden_in, up_t, *weights)
        for at, block in enumerate(MEMBERS[group]):
            saved[block] = (block, kept, at)
        return parts, down_head

    score_half = lax.all_gather(score_embed, "z", axis=0, tiled=True)
    (other4, other3, own4), down_head = forward(0, down_weight, head_weight)
    fore, across4, came3 = shift(own4, 1), shift_across(other4, 1), swap(other3, "yhi")
    (other2, other1, own3, own3b), _ = forward(1, down_head)
    came2, came1 = swap(other2, "yhi"), swap(other1, "yhi")
    fore = shift(total_of(own3, came3[:rows], fore, across4).astype(bf16), 1)
    back = shift(total_of(own3b, came3[rows:]).astype(bf16), -1)
    (own2, own1), _ = forward(2, down_head)
    for own, came in ((own2, came2), (own1, came1)):
        fore = shift(total_of(own[:rows], came[:rows], fore).astype(bf16), 1)
        back = shift(total_of(own[rows : 2 * rows], came[rows : 2 * rows], back).astype(bf16), -1)
    score_unit = unit_rows(score_half)[0].astype(bf16)
    fore, back, score_unit = lax.optimization_barrier((fore, back, score_unit))
    own_start = y_hi * group_half + z * rows
    own_hidden = lax.dynamic_slice_in_dim(hidden_in, own_start, rows, 0)
    own_proj = dot(own_hidden, head_weight)
    audio_wide, audio_inverse = unit_rows(own_proj + total_of(own1[2 * rows :], came1[2 * rows :], fore, back))
    audio_own = audio_wide.astype(bf16)
    audio_unit = jnp.concatenate([audio_own, swap(audio_own, "yhi")], axis=0)
    far_start = (1 - y_hi) * group_half + z * rows
    partners = jnp.concatenate(
        [lax.dynamic_slice_in_dim(pair_index[0], start, rows, 0) for start in (own_start, far_start)]
    )
    coeffs = pair_coeffs(audio_unit, score_unit, partners, y_hi * group_half)
    grad_audio = dot(coeffs, score_unit)
    grad_audio = grad_audio[:rows] + swap(grad_audio[rows:].astype(bf16), "yhi").astype(f32)
    grad_embed = unit_backward(audio_wide, audio_inverse, grad_audio).astype(bf16)
    score_part = dot(coeffs, audio_unit, ((0,), (0,))).astype(bf16)
    item = lambda grad, *blocks: (grad, [saved[block] for block in blocks])
    pair = lambda step, half: ((half, step), (half, -step))
    both = lambda up, down: jnp.concatenate([up, down], axis=0)
    fore, back = shift(grad_embed, 1), shift(grad_embed, -1)
    own_block, score_part = lax.optimization_barrier((grad_embed, score_part))
    crossed0 = swap(own_block, "yhi")
    ring1 = both(back, fore)
    crossed1 = swap(ring1, "yhi")
    fore, back = shift(fore, 1), shift(back, -1)
    backward = lambda items, sums, *head: backward_blocks(items, packed, hidden_in, down_head, sums, *head)
    sums = backward([item(grad_embed, (0, 0)), item(crossed0, (1, 0)), item(ring1, *pair(1, 0))], None)
    fore, back, sums = lax.optimization_barrier((fore, back, sums))
    ring2 = both(back, fore)
    crossed2 = swap(ring2, "yhi")
    fore, back = shift(fore, 1), shift(back, -1)
    sums = backward([item(crossed1, *pair(1, 1)), item(ring2, *pair(2, 0))], sums)
    fore, back, sums, crossed2, score_part = lax.optimization_barrier((fore, back, sums, crossed2, score_part))
    grad_score = lax.psum_scatter(score_part, "z", scatter_dimension=0, tiled=True)
    ring4, crossed4 = shift(fore, 1), shift_across(fore, 1)
    ring3 = both(back, fore)
    crossed3 = swap(ring3, "yhi")
    sums = backward([item(ring3, *pair(3, 0)), item(crossed2, *pair(2, 1))], sums)
    ring4, crossed4, sums = lax.optimization_barrier((ring4, crossed4, sums))
    items = [item(crossed3, *pair(3, 1)), item(ring4, (0, 4)), item(crossed4, (1, 4))]
    keep, give = backward(items, sums, head_weight)
    chip = total_of(keep, swap(give, "core")).astype(bf16)
    landed = lax.all_to_all(chip, ("ylo", "x"), 0, 0)
    total = jnp.sum(landed.astype(f32), axis=0)
    ff = up_weight.shape[1]
    score_grad = score_backward(score_embed, grad_score)
    return (total[:, :ff], total[:, ff:].T, score_grad)


def solution(mesh):
    fine = Mesh(mesh.devices.reshape(2, 4, 2, 2, RING), ("ylo", "x", "core", "yhi", "z"))
    in_specs = (
        P(AUDIO, None),
        P(None, SCORE),
        P(SCORE, None),
        P(),
        P(AUDIO + SCORE, None),
        P(AUDIO, None),
    )
    out_specs = (P(AUDIO, SCORE), P(SCORE, AUDIO), P(AUDIO + SCORE, None))
    return jax.shard_map(
        per_device, mesh=fine, in_specs=in_specs, out_specs=out_specs, check_vma=False
    )
```

```python
import functools

import jax
import jax.numpy as jnp
from jax import lax
from jax.experimental import pallas as pl
from jax.experimental.pallas import tpu as pltpu
from jax.sharding import Mesh, PartitionSpec as P

logit_scale = 8.0
logit_bias = -3.0
epsilon = 1e-06
gelu_root = 0.7978845608028654
gelu_cubic = 0.044715

AUDIO = ("ylo", "x", "core")
SCORE = ("yhi", "z")
RING = 8
VMEM_BYTES = 56 * 1024 * 1024
f32 = jnp.float32
bf16 = jnp.bfloat16


def dot(left, right, dims=((1,), (0,))):
    return lax.dot_general(left, right, (dims, ((), ())), preferred_element_type=f32)


def unit_rows(values):
    wide = values.astype(f32)
    inverse = lax.rsqrt(jnp.sum(wide * wide, axis=-1, keepdims=True) + epsilon)
    return (wide * inverse, inverse)


def unit_backward(unit_wide, inverse, grad_unit):
    inner = jnp.sum(unit_wide * grad_unit, axis=-1, keepdims=True)
    return inverse * (grad_unit - unit_wide * inner)


def pair_coeffs(left, right, partner, first_column):
    logits = logit_scale * dot(left, right, ((1,), (1,))) + logit_bias
    columns = first_column + lax.iota(jnp.int32, right.shape[0])
    sign = jnp.where(partner[:, None] == columns[None, :], 1.0, -1.0)
    return (-logit_scale * sign * jax.nn.sigmoid(-sign * logits)).astype(bf16)


def swap(value, axis):
    return lax.ppermute(value, axis, [(0, 1), (1, 0)])


def shift(value, step):
    perm = [(i, (i + step) % RING) for i in range(RING)]
    perm += [(RING + i, RING + (i - step) % RING) for i in range(RING)]
    return lax.ppermute(value, ("core", "z"), perm)


def shift_across(value, step):
    to = lambda core, half, place: (core * 2 + half) * RING + place % RING
    perm = [
        (to(core, half, place), to(core, 1 - half, place + (step if core == 0 else -step)))
        for core in range(2)
        for half in range(2)
        for place in range(RING)
    ]
    return lax.ppermute(value, ("core", "yhi", "z"), perm)


GROUPS = (
    (((1, 4),), ((1, 3), (1, -3)), ((0, 4),)),
    (((1, 2), (1, -2)), ((1, 1), (1, -1), (1, 0)), ((0, 3),), ((0, -3),)),
    (((0, 2), (0, -2)), ((0, 1), (0, -1), (0, 0))),
)
MEMBERS = tuple(tuple(block for piece in group for block in piece) for group in GROUPS)


def packed_place(half, place, core):
    return (half * (2 * RING) + place * 2 + core)[None]


def block_map(block):
    half, offset = block

    def index_map(i, packed):
        own_half, place, core = packed[0] // (2 * RING), packed[0] // 2 % RING, packed[0] % 2
        along = lax.rem(place + (1 - 2 * core) * offset + RING, RING)
        return lax.rem(own_half + half, 2) * RING + along, 0

    return index_map


def forward_kernel(pieces, first, packed_ref, *refs):
    count = sum(pieces)
    hidden = [ref[...] for ref in refs[:count]]
    refs = refs[count:]
    if first:
        up_ref, down_ref, head_ref = refs[:3]
        down_head_ref = refs[-1]
        down_head_ref[...] = dot(down_ref[...], head_ref[...]).astype(bf16)
        refs = refs[3:-1]
    else:
        up_ref, down_head_ref = refs[:2]
        refs = refs[2:]
    part_refs = refs[: len(pieces)]
    act_t_ref, slope_ref = refs[len(pieces) :]
    rows = hidden[0].shape[0]
    wide = jnp.concatenate(hidden, axis=0).astype(f32)
    square_mean = jnp.mean(wide * wide, axis=-1, keepdims=True)
    inverse = lax.rsqrt(square_mean + epsilon)
    normed = (wide * inverse).astype(bf16)
    pre = dot(normed, up_ref[...], ((1,), (1,)))
    tangent = jnp.tanh(gelu_root * (pre + gelu_cubic * (pre * pre * pre)))
    act = (0.5 * pre * (1.0 + tangent)).astype(bf16)
    part = dot(act, down_head_ref[...]).astype(bf16)
    at = 0
    for size, part_ref in zip(pieces, part_refs):
        part_ref[...] = part[at * rows : (at + size) * rows, :]
        at += size
    slope = 0.5 * (1.0 + tangent) + 0.5 * pre * (1.0 - tangent * tangent) * gelu_root * (
        1.0 + 3.0 * gelu_cubic * pre * pre
    )
    slope = (inverse * slope).astype(bf16)
    act_t = act.T
    for i in range(count):
        span = slice(i * rows, (i + 1) * rows)
        slope_ref[i] = slope[span, :]
        act_t_ref[i] = act_t[:, span]


def forward_blocks(group, packed, hidden_in, up_t, *weights):
    pieces = tuple(len(piece) for piece in GROUPS[group])
    count = sum(pieces)
    first = len(weights) == 2
    rows = hidden_in.shape[0] // (2 * RING)
    ff, width = up_t.shape
    embed = weights[-1].shape[1]
    flat = lambda i, packed: (0, 0)
    cube = lambda i, packed: (0, 0, 0)
    shapes = [jax.ShapeDtypeStruct((size * rows, embed), bf16) for size in pieces]
    shapes += [jax.ShapeDtypeStruct((count,) + dims, bf16) for dims in ((ff, rows), (rows, ff))]
    shapes += [jax.ShapeDtypeStruct((ff, embed), bf16)] if first else []
    out = pl.pallas_call(
        functools.partial(forward_kernel, pieces, first),
        grid_spec=pltpu.PrefetchScalarGridSpec(
            num_scalar_prefetch=1,
            grid=(1,),
            in_specs=[pl.BlockSpec((rows, width), block_map(block)) for block in MEMBERS[group]]
            + [pl.BlockSpec(w.shape, flat) for w in (up_t,) + weights],
            out_specs=[pl.BlockSpec(shape.shape, cube if len(shape.shape) == 3 else flat) for shape in shapes],
        ),
        out_shape=shapes,
        compiler_params=pltpu.CompilerParams(vmem_limit_bytes=VMEM_BYTES),
        cost_estimate=pl.CostEstimate(
            flops=2 * count * rows * ff * (width + embed),
            bytes_accessed=2 * count * rows * (width + embed + 2 * ff) + 2 * ff * (width + embed),
            transcendentals=count * rows * ff,
        ),
    )(packed, *([hidden_in] * count), up_t, *weights)
    parts, kept = out[: len(pieces)], out[len(pieces) : len(pieces) + 2]
    return parts, kept, out[-1]


def backward_kernel(count, blocks, first, last, packed_ref, *refs):
    join = lambda parts, axis: jnp.concatenate(parts, axis=axis) if len(parts) > 1 else parts[0]
    grad = join([ref[...] for ref in refs[:count]], 0)
    kept = refs[count : count + 3 * blocks]
    hidden = join([ref[...] for ref in kept[0::3]], 0)
    act_t, slope = join([ref[0] for ref in kept[1::3]], 1), join([ref[0] for ref in kept[2::3]], 0)
    refs = refs[count + 3 * blocks :]
    down_head_ref, refs = refs[0], refs[1:]
    if not first:
        up_in, act_in = refs[:2]
        refs = refs[2:]
    tile = 256
    grad_act = dot(grad, down_head_ref[...], ((1,), (1,)))
    grad_pre_t = (grad_act * slope.astype(f32)).astype(bf16).T
    act_sum = dot(act_t, grad)
    if not first:
        act_sum = act_sum + act_in[...]
    if last:
        head_ref, keep_ref, give_ref, total = refs
    else:
        up_acc, act_acc = refs
        act_acc[...] = act_sum
    width, ff = hidden.shape[1], act_sum.shape[0]
    for m in range(0, width, tile):
        up_sum = dot(grad_pre_t, hidden[:, m : m + tile])
        if not first:
            up_sum = up_sum + up_in[:, m : m + tile]
        if last:
            total[m : m + tile, :ff] = up_sum.T.astype(bf16)
        else:
            up_acc[:, m : m + tile] = up_sum
    if last:
        core = packed_ref[0] % 2
        act_grad = act_sum.astype(bf16)
        rows = keep_ref.shape[1]
        for m in range(0, width, tile):
            total[m : m + tile, ff:] = dot(head_ref[m : m + tile, :], act_grad, ((1,), (1,))).astype(bf16)
        for half, out_ref in ((core, keep_ref), (1 - core, give_ref)):
            for chip in range(keep_ref.shape[0]):
                at = pl.multiple_of((2 * chip + half) * rows, rows)
                out_ref[chip] = total[pl.ds(at, rows), :]


def backward_blocks(items, packed, hidden_in, down_head, sums, head_weight=None):
    last = head_weight is not None
    whole = pl.BlockSpec(memory_space=pltpu.VMEM)
    args = [grad for grad, _ in items]
    specs = [whole] * len(items)
    places = [place for _, blocks in items for place in blocks]
    rows, width = hidden_in.shape[0] // (2 * RING), hidden_in.shape[1]
    for block, kept, at in places:
        args.append(hidden_in)
        specs.append(pl.BlockSpec((rows, width), block_map(block)))
        for array in kept:
            args.append(array)
            specs.append(pl.BlockSpec((1,) + array.shape[1:], lambda i, packed, at=at: (at, 0, 0)))
    ff, embed = down_head.shape
    args.append(down_head)
    aliases = {}
    if sums is not None:
        if not last:
            aliases = {len(args) + 1: 0, len(args) + 2: 1}
        args += list(sums)
    if last:
        args.append(head_weight)
        shapes = [jax.ShapeDtypeStruct((8, width // 16, 2 * ff), bf16)] * 2
        scratch = [pltpu.VMEM((width, 2 * ff), bf16)]
    else:
        shapes = [jax.ShapeDtypeStruct((ff, width), f32), jax.ShapeDtypeStruct((ff, embed), f32)]
        scratch = []
    specs += [whole] * (len(args) - len(specs))
    return pl.pallas_call(
        functools.partial(backward_kernel, len(items), len(places), sums is None, last),
        grid_spec=pltpu.PrefetchScalarGridSpec(
            num_scalar_prefetch=1,
            grid=(1,),
            in_specs=specs,
            out_specs=[whole] * 2,
            scratch_shapes=scratch,
        ),
        out_shape=shapes,
        input_output_aliases=aliases,
        compiler_params=pltpu.CompilerParams(vmem_limit_bytes=VMEM_BYTES),
        cost_estimate=pl.CostEstimate(flops=0, bytes_accessed=0, transcendentals=0),
    )(packed, *args)


def score_kernel(embed_ref, grad_ref, out_ref):
    wide, inverse = unit_rows(embed_ref[...])
    out_ref[...] = unit_backward(wide, inverse, grad_ref[...].astype(f32))


def score_backward(score_embed, grad_score):
    return pl.pallas_call(
        score_kernel,
        out_shape=jax.ShapeDtypeStruct(score_embed.shape, f32),
        compiler_params=pltpu.CompilerParams(vmem_limit_bytes=VMEM_BYTES),
    )(score_embed, grad_score)


def total_of(*terms):
    return sum(term.astype(f32) for term in terms)


def per_device(hidden_in, up_weight, down_weight, head_weight, score_embed, pair_index):
    y_hi, z, core = (lax.axis_index(name).astype(jnp.int32) for name in ("yhi", "z", "core"))
    rows = hidden_in.shape[0] // (2 * RING)
    group_half = RING * rows
    packed = packed_place(y_hi, z, core)
    up_t = up_weight.T
    saved = {}

    def forward(group, *weights):
        parts, kept, down_head = forward_blocks(group, packed, hidden_in, up_t, *weights)
        for at, block in enumerate(MEMBERS[group]):
            saved[block] = (block, kept, at)
        return parts, down_head

    score_half = lax.all_gather(score_embed, "z", axis=0, tiled=True)
    (other4, other3, own4), down_head = forward(0, down_weight, head_weight)
    fore, came3 = shift(own4, 1), swap(other3, "yhi")
    (other2, other1, own3, own3b), _ = forward(1, down_head)
    other4, own3 = lax.optimization_barrier((other4, own3))
    across4 = shift_across(other4, 3)
    came2, came1 = swap(other2, "yhi"), swap(other1, "yhi")
    fore = shift(total_of(own3, came3[:rows], fore).astype(bf16), 1)
    back = shift(total_of(own3b, came3[rows:]).astype(bf16), -1)
    (own2, own1), _ = forward(2, down_head)
    for own, came, joins in ((own2, came2, ()), (own1, came1, (across4,))):
        fore = shift(total_of(own[:rows], came[:rows], fore, *joins).astype(bf16), 1)
        back = shift(total_of(own[rows : 2 * rows], came[rows : 2 * rows], back).astype(bf16), -1)
    score_unit = unit_rows(score_half)[0].astype(bf16)
    fore, back, score_unit = lax.optimization_barrier((fore, back, score_unit))
    own_start = y_hi * group_half + z * rows
    own_hidden = lax.dynamic_slice_in_dim(hidden_in, own_start, rows, 0)
    own_proj = dot(own_hidden, head_weight)
    audio_wide, audio_inverse = unit_rows(own_proj + total_of(own1[2 * rows :], came1[2 * rows :], fore, back))
    audio_own = audio_wide.astype(bf16)
    audio_far = swap(audio_own, "yhi")
    far_start = (1 - y_hi) * group_half + z * rows
    contrast = lambda audio, start: pair_coeffs(
        audio, score_unit, lax.dynamic_slice_in_dim(pair_index[0], start, rows, 0), y_hi * group_half
    )
    coeffs_own = contrast(audio_own, own_start)
    audio_far, grad_own = lax.optimization_barrier((audio_far, dot(coeffs_own, score_unit)))
    coeffs_far = contrast(audio_far, far_start)
    grad_far = dot(coeffs_far, score_unit).astype(bf16)
    grad_audio = grad_own + swap(grad_far, "yhi").astype(f32)
    grad_embed = unit_backward(audio_wide, audio_inverse, grad_audio).astype(bf16)
    coeffs = jnp.concatenate([coeffs_own, coeffs_far], axis=0)
    score_part = dot(coeffs, jnp.concatenate([audio_own, audio_far], axis=0), ((0,), (0,))).astype(bf16)
    item = lambda grad, *blocks: (grad, [saved[block] for block in blocks])
    pair = lambda step, half: ((half, step), (half, -step))
    both = lambda up, down: jnp.concatenate([up, down], axis=0)
    fore, back = shift(grad_embed, 1), shift(grad_embed, -1)
    own_block, score_part = lax.optimization_barrier((grad_embed, score_part))
    crossed0 = swap(own_block, "yhi")
    ring1 = both(back, fore)
    crossed1 = swap(ring1, "yhi")
    fore, back = shift(fore, 1), shift(back, -1)
    backward = lambda items, sums, *head: backward_blocks(items, packed, hidden_in, down_head, sums, *head)
    sums = backward([item(grad_embed, (0, 0)), item(crossed0, (1, 0)), item(ring1, *pair(1, 0))], None)
    fore, back, sums, score_part = lax.optimization_barrier((fore, back, sums, score_part))
    grad_score = lax.psum_scatter(score_part, "z", scatter_dimension=0, tiled=True)
    ring2 = both(back, fore)
    crossed2 = swap(ring2, "yhi")
    fore, back = shift(fore, 1), shift(back, -1)
    sums = backward([item(crossed1, *pair(1, 1)), item(ring2, *pair(2, 0))], sums)
    fore, back, sums, crossed2 = lax.optimization_barrier((fore, back, sums, crossed2))
    ring4, crossed4 = shift(fore, 1), shift_across(fore, 1)
    ring3 = both(back, fore)
    crossed3 = swap(ring3, "yhi")
    sums = backward([item(ring3, *pair(3, 0)), item(crossed2, *pair(2, 1))], sums)
    ring4, crossed4, sums = lax.optimization_barrier((ring4, crossed4, sums))
    items = [item(crossed3, *pair(3, 1)), item(ring4, (0, 4)), item(crossed4, (1, 4))]
    keep, give = backward(items, sums, head_weight)
    chip = total_of(keep, swap(give, "core")).astype(bf16)
    landed = lax.all_to_all(chip, ("ylo", "x"), 0, 0)
    total = jnp.sum(landed.astype(f32), axis=0)
    ff = up_weight.shape[1]
    score_grad = score_backward(score_embed, grad_score)
    return (total[:, :ff], total[:, ff:].T, score_grad)


def solution(mesh):
    fine = Mesh(mesh.devices.reshape(2, 4, 2, 2, RING), ("ylo", "x", "core", "yhi", "z"))
    in_specs = (
        P(AUDIO, None),
        P(None, SCORE),
        P(SCORE, None),
        P(),
        P(AUDIO + SCORE, None),
        P(AUDIO, None),
    )
    out_specs = (P(AUDIO, SCORE), P(SCORE, AUDIO), P(AUDIO + SCORE, None))
    return jax.shard_map(
        per_device, mesh=fine, in_specs=in_specs, out_specs=out_specs, check_vma=False
    )
```

```python
import functools

import jax
import jax.numpy as jnp
from jax import lax
from jax.experimental import pallas as pl
from jax.experimental.pallas import tpu as pltpu
from jax.sharding import Mesh, PartitionSpec as P

logit_scale = 8.0
logit_bias = -3.0
epsilon = 1e-06
gelu_root = 0.7978845608028654
gelu_cubic = 0.044715

AUDIO = ("ylo", "x", "core")
SCORE = ("yhi", "z")
RING = 8
VMEM_BYTES = 56 * 1024 * 1024
f32 = jnp.float32
bf16 = jnp.bfloat16


def dot(left, right, dims=((1,), (0,))):
    return lax.dot_general(left, right, (dims, ((), ())), preferred_element_type=f32)


def unit_rows(values):
    wide = values.astype(f32)
    inverse = lax.rsqrt(jnp.sum(wide * wide, axis=-1, keepdims=True) + epsilon)
    return (wide * inverse, inverse)


def unit_backward(unit_wide, inverse, grad_unit):
    inner = jnp.sum(unit_wide * grad_unit, axis=-1, keepdims=True)
    return inverse * (grad_unit - unit_wide * inner)


def pair_coeffs(left, right, partner, first_column):
    logits = logit_scale * dot(left, right, ((1,), (1,))) + logit_bias
    columns = first_column + lax.iota(jnp.int32, right.shape[0])
    sign = jnp.where(partner[:, None] == columns[None, :], 1.0, -1.0)
    return (-logit_scale * sign * jax.nn.sigmoid(-sign * logits)).astype(bf16)


def swap(value, axis):
    return lax.ppermute(value, axis, [(0, 1), (1, 0)])


def shift(value, step):
    perm = [(i, (i + step) % RING) for i in range(RING)]
    perm += [(RING + i, RING + (i - step) % RING) for i in range(RING)]
    return lax.ppermute(value, ("core", "z"), perm)


def shift_across(value, step):
    to = lambda core, half, place: (core * 2 + half) * RING + place % RING
    perm = [
        (to(core, half, place), to(core, 1 - half, place + (step if core == 0 else -step)))
        for core in range(2)
        for half in range(2)
        for place in range(RING)
    ]
    return lax.ppermute(value, ("core", "yhi", "z"), perm)


GROUPS = (
    (((1, 4),), ((1, 3), (1, -3)), ((0, 4),)),
    (((1, 2), (1, -2)), ((1, 1), (1, -1), (1, 0)), ((0, 3),), ((0, -3),)),
    (((0, 2), (0, -2)), ((0, 1), (0, -1), (0, 0))),
)
MEMBERS = tuple(tuple(block for piece in group for block in piece) for group in GROUPS)


def packed_place(half, place, core):
    return (half * (2 * RING) + place * 2 + core)[None]


def block_map(block):
    half, offset = block

    def index_map(i, packed):
        own_half, place, core = packed[0] // (2 * RING), packed[0] // 2 % RING, packed[0] % 2
        along = lax.rem(place + (1 - 2 * core) * offset + RING, RING)
        return lax.rem(own_half + half, 2) * RING + along, 0

    return index_map


def forward_kernel(pieces, first, packed_ref, *refs):
    count = sum(pieces)
    hidden = [ref[...] for ref in refs[:count]]
    refs = refs[count:]
    if first:
        up_ref, down_ref, head_ref = refs[:3]
        down_head_ref = refs[-1]
        down_head_ref[...] = dot(down_ref[...], head_ref[...]).astype(bf16)
        refs = refs[3:-1]
    else:
        up_ref, down_head_ref = refs[:2]
        refs = refs[2:]
    part_refs = refs[: len(pieces)]
    act_t_ref, slope_ref = refs[len(pieces) :]
    rows = hidden[0].shape[0]
    wide = jnp.concatenate(hidden, axis=0).astype(f32)
    square_mean = jnp.mean(wide * wide, axis=-1, keepdims=True)
    inverse = lax.rsqrt(square_mean + epsilon)
    normed = (wide * inverse).astype(bf16)
    pre = dot(normed, up_ref[...], ((1,), (1,)))
    tangent = jnp.tanh(gelu_root * (pre + gelu_cubic * (pre * pre * pre)))
    act = (0.5 * pre * (1.0 + tangent)).astype(bf16)
    part = dot(act, down_head_ref[...]).astype(bf16)
    at = 0
    for size, part_ref in zip(pieces, part_refs):
        part_ref[...] = part[at * rows : (at + size) * rows, :]
        at += size
    slope = 0.5 * (1.0 + tangent) + 0.5 * pre * (1.0 - tangent * tangent) * gelu_root * (
        1.0 + 3.0 * gelu_cubic * pre * pre
    )
    slope = (inverse * slope).astype(bf16)
    act_t = act.T
    for i in range(count):
        span = slice(i * rows, (i + 1) * rows)
        slope_ref[i] = slope[span, :]
        act_t_ref[i] = act_t[:, span]


def forward_blocks(group, packed, hidden_in, up_t, *weights):
    pieces = tuple(len(piece) for piece in GROUPS[group])
    count = sum(pieces)
    first = len(weights) == 2
    rows = hidden_in.shape[0] // (2 * RING)
    ff, width = up_t.shape
    embed = weights[-1].shape[1]
    flat = lambda i, packed: (0, 0)
    cube = lambda i, packed: (0, 0, 0)
    shapes = [jax.ShapeDtypeStruct((size * rows, embed), bf16) for size in pieces]
    shapes += [jax.ShapeDtypeStruct((count,) + dims, bf16) for dims in ((ff, rows), (rows, ff))]
    shapes += [jax.ShapeDtypeStruct((ff, embed), bf16)] if first else []
    out = pl.pallas_call(
        functools.partial(forward_kernel, pieces, first),
        grid_spec=pltpu.PrefetchScalarGridSpec(
            num_scalar_prefetch=1,
            grid=(1,),
            in_specs=[pl.BlockSpec((rows, width), block_map(block)) for block in MEMBERS[group]]
            + [pl.BlockSpec(w.shape, flat) for w in (up_t,) + weights],
            out_specs=[pl.BlockSpec(shape.shape, cube if len(shape.shape) == 3 else flat) for shape in shapes],
        ),
        out_shape=shapes,
        compiler_params=pltpu.CompilerParams(vmem_limit_bytes=VMEM_BYTES),
        cost_estimate=pl.CostEstimate(
            flops=2 * count * rows * ff * (width + embed),
            bytes_accessed=2 * count * rows * (width + embed + 2 * ff) + 2 * ff * (width + embed),
            transcendentals=count * rows * ff,
        ),
    )(packed, *([hidden_in] * count), up_t, *weights)
    parts, kept = out[: len(pieces)], out[len(pieces) : len(pieces) + 2]
    return parts, kept, out[-1]


def backward_kernel(count, blocks, first, last, packed_ref, *refs):
    join = lambda parts, axis: jnp.concatenate(parts, axis=axis) if len(parts) > 1 else parts[0]
    grad = join([ref[...] for ref in refs[:count]], 0)
    kept = refs[count : count + 3 * blocks]
    hidden = join([ref[...] for ref in kept[0::3]], 0)
    act_t, slope = join([ref[0] for ref in kept[1::3]], 1), join([ref[0] for ref in kept[2::3]], 0)
    refs = refs[count + 3 * blocks :]
    down_head_ref, refs = refs[0], refs[1:]
    if not first:
        up_in, act_in = refs[:2]
        refs = refs[2:]
    tile = 256
    grad_act = dot(grad, down_head_ref[...], ((1,), (1,)))
    grad_pre_t = (grad_act * slope.astype(f32)).astype(bf16).T
    act_sum = dot(act_t, grad)
    if not first:
        act_sum = act_sum + act_in[...].astype(f32)
    if last:
        head_ref, keep_ref, give_ref, total, sems = refs
    else:
        up_acc, act_acc = refs
        act_acc[...] = act_sum.astype(bf16)
    width, ff = hidden.shape[1], act_sum.shape[0]
    for m in range(0, width, tile):
        up_sum = dot(grad_pre_t, hidden[:, m : m + tile])
        if not first:
            up_sum = up_sum + up_in[:, m : m + tile].astype(f32)
        if last:
            total[m : m + tile, :ff] = up_sum.T.astype(bf16)
        else:
            up_acc[:, m : m + tile] = up_sum.astype(bf16)
    if last:
        core = packed_ref[0] % 2
        act_grad = act_sum.astype(bf16)
        rows = keep_ref.shape[1]
        for m in range(0, width, tile):
            total[m : m + tile, ff:] = dot(head_ref[m : m + tile, :], act_grad, ((1,), (1,))).astype(bf16)
        copies = []
        for half, out_ref in ((core, keep_ref), (1 - core, give_ref)):
            for chip in range(keep_ref.shape[0]):
                at = pl.multiple_of((2 * chip + half) * rows, rows)
                copies.append(
                    pltpu.make_async_copy(total.at[pl.ds(at, rows), :], out_ref.at[chip], sems.at[len(copies)])
                )
                copies[-1].start()
        for copy in copies:
            copy.wait()


def backward_blocks(items, packed, hidden_in, down_head, sums, head_weight=None):
    last = head_weight is not None
    whole = pl.BlockSpec(memory_space=pltpu.VMEM)
    args = [grad for grad, _ in items]
    specs = [whole] * len(items)
    places = [place for _, blocks in items for place in blocks]
    rows, width = hidden_in.shape[0] // (2 * RING), hidden_in.shape[1]
    for block, kept, at in places:
        args.append(hidden_in)
        specs.append(pl.BlockSpec((rows, width), block_map(block)))
        for array in kept:
            args.append(array)
            specs.append(pl.BlockSpec((1,) + array.shape[1:], lambda i, packed, at=at: (at, 0, 0)))
    ff, embed = down_head.shape
    args.append(down_head)
    aliases = {}
    if sums is not None:
        if not last:
            aliases = {len(args) + 1: 0, len(args) + 2: 1}
        args += list(sums)
    if last:
        args.append(head_weight)
        shapes = [jax.ShapeDtypeStruct((8, width // 16, 2 * ff), bf16)] * 2
        scratch = [pltpu.VMEM((width, 2 * ff), bf16), pltpu.SemaphoreType.DMA((16,))]
    else:
        shapes = [jax.ShapeDtypeStruct((ff, width), bf16), jax.ShapeDtypeStruct((ff, embed), bf16)]
        scratch = []
    specs += [whole] * (len(args) - len(specs))
    return pl.pallas_call(
        functools.partial(backward_kernel, len(items), len(places), sums is None, last),
        grid_spec=pltpu.PrefetchScalarGridSpec(
            num_scalar_prefetch=1,
            grid=(1,),
            in_specs=specs,
            out_specs=[pl.BlockSpec(memory_space=pl.ANY) if last else whole] * 2,
            scratch_shapes=scratch,
        ),
        out_shape=shapes,
        input_output_aliases=aliases,
        compiler_params=pltpu.CompilerParams(vmem_limit_bytes=VMEM_BYTES),
        cost_estimate=pl.CostEstimate(flops=0, bytes_accessed=0, transcendentals=0),
    )(packed, *args)


def score_kernel(embed_ref, grad_ref, out_ref):
    wide, inverse = unit_rows(embed_ref[...])
    out_ref[...] = unit_backward(wide, inverse, grad_ref[...].astype(f32))


def score_backward(score_embed, grad_score):
    return pl.pallas_call(
        score_kernel,
        out_shape=jax.ShapeDtypeStruct(score_embed.shape, f32),
        compiler_params=pltpu.CompilerParams(vmem_limit_bytes=VMEM_BYTES),
    )(score_embed, grad_score)


def total_of(*terms):
    return sum(term.astype(f32) for term in terms)


def per_device(hidden_in, up_weight, down_weight, head_weight, score_embed, pair_index):
    y_hi, z, core = (lax.axis_index(name).astype(jnp.int32) for name in ("yhi", "z", "core"))
    rows = hidden_in.shape[0] // (2 * RING)
    group_half = RING * rows
    packed = packed_place(y_hi, z, core)
    up_t = up_weight.T
    saved = {}

    def forward(group, *weights):
        parts, kept, down_head = forward_blocks(group, packed, hidden_in, up_t, *weights)
        for at, block in enumerate(MEMBERS[group]):
            saved[block] = (block, kept, at)
        return parts, down_head

    score_half = lax.all_gather(score_embed, "z", axis=0, tiled=True)
    (other4, other3, own4), down_head = forward(0, down_weight, head_weight)
    fore, across4, came3 = shift(own4, 1), shift_across(other4, 1), swap(other3, "yhi")
    (other2, other1, own3, own3b), _ = forward(1, down_head)
    came2, came1 = swap(other2, "yhi"), swap(other1, "yhi")
    fore = shift(total_of(own3, came3[:rows], fore, across4).astype(bf16), 1)
    back = shift(total_of(own3b, came3[rows:]).astype(bf16), -1)
    (own2, own1), _ = forward(2, down_head)
    for own, came in ((own2, came2), (own1, came1)):
        fore = shift(total_of(own[:rows], came[:rows], fore).astype(bf16), 1)
        back = shift(total_of(own[rows : 2 * rows], came[rows : 2 * rows], back).astype(bf16), -1)
    score_unit = unit_rows(score_half)[0].astype(bf16)
    fore, back, score_unit = lax.optimization_barrier((fore, back, score_unit))
    own_start = y_hi * group_half + z * rows
    own_hidden = lax.dynamic_slice_in_dim(hidden_in, own_start, rows, 0)
    own_proj = dot(own_hidden, head_weight)
    audio_wide, audio_inverse = unit_rows(own_proj + total_of(own1[2 * rows :], came1[2 * rows :], fore, back))
    audio_own = audio_wide.astype(bf16)
    audio_unit = jnp.concatenate([audio_own, swap(audio_own, "yhi")], axis=0)
    far_start = (1 - y_hi) * group_half + z * rows
    partners = jnp.concatenate(
        [lax.dynamic_slice_in_dim(pair_index[0], start, rows, 0) for start in (own_start, far_start)]
    )
    coeffs = pair_coeffs(audio_unit, score_unit, partners, y_hi * group_half)
    grad_audio = dot(coeffs, score_unit)
    grad_audio = grad_audio[:rows] + swap(grad_audio[rows:].astype(bf16), "yhi").astype(f32)
    grad_embed = unit_backward(audio_wide, audio_inverse, grad_audio).astype(bf16)
    score_part = dot(coeffs, audio_unit, ((0,), (0,))).astype(bf16)
    item = lambda grad, *blocks: (grad, [saved[block] for block in blocks])
    pair = lambda step, half: ((half, step), (half, -step))
    both = lambda up, down: jnp.concatenate([up, down], axis=0)
    fore, back = shift(grad_embed, 1), shift(grad_embed, -1)
    own_block, score_part = lax.optimization_barrier((grad_embed, score_part))
    crossed0 = swap(own_block, "yhi")
    ring1 = both(back, fore)
    crossed1 = swap(ring1, "yhi")
    fore, back = shift(fore, 1), shift(back, -1)
    backward = lambda items, sums, *head: backward_blocks(items, packed, hidden_in, down_head, sums, *head)
    sums = backward([item(grad_embed, (0, 0)), item(crossed0, (1, 0)), item(ring1, *pair(1, 0))], None)
    fore, back, sums = lax.optimization_barrier((fore, back, sums))
    ring2 = both(back, fore)
    crossed2 = swap(ring2, "yhi")
    fore, back = shift(fore, 1), shift(back, -1)
    sums = backward([item(crossed1, *pair(1, 1)), item(ring2, *pair(2, 0))], sums)
    fore, back, sums, crossed2, score_part = lax.optimization_barrier((fore, back, sums, crossed2, score_part))
    grad_score = lax.psum_scatter(score_part, "z", scatter_dimension=0, tiled=True)
    ring4, crossed4 = shift(fore, 1), shift_across(fore, 1)
    ring3 = both(back, fore)
    crossed3 = swap(ring3, "yhi")
    sums = backward([item(ring3, *pair(3, 0)), item(crossed2, *pair(2, 1))], sums)
    ring4, crossed4, sums = lax.optimization_barrier((ring4, crossed4, sums))
    items = [item(crossed3, *pair(3, 1)), item(ring4, (0, 4)), item(crossed4, (1, 4))]
    keep, give = backward(items, sums, head_weight)
    chip = total_of(keep, swap(give, "core")).astype(bf16)
    landed = lax.all_to_all(chip, ("ylo", "x"), 0, 0)
    total = jnp.sum(landed.astype(f32), axis=0)
    ff = up_weight.shape[1]
    score_grad = score_backward(score_embed, grad_score)
    return (total[:, :ff], total[:, ff:].T, score_grad)


def solution(mesh):
    fine = Mesh(mesh.devices.reshape(2, 4, 2, 2, RING), ("ylo", "x", "core", "yhi", "z"))
    in_specs = (
        P(AUDIO, None),
        P(None, SCORE),
        P(SCORE, None),
        P(),
        P(AUDIO + SCORE, None),
        P(AUDIO, None),
    )
    out_specs = (P(AUDIO, SCORE), P(SCORE, AUDIO), P(AUDIO + SCORE, None))
    return jax.shard_map(
        per_device, mesh=fine, in_specs=in_specs, out_specs=out_specs, check_vma=False
    )
```

```python
import functools

import jax
import jax.numpy as jnp
from jax import lax
from jax.experimental import pallas as pl
from jax.experimental.pallas import tpu as pltpu
from jax.sharding import Mesh, PartitionSpec as P

logit_scale = 8.0
logit_bias = -3.0
epsilon = 1e-06
gelu_root = 0.7978845608028654
gelu_cubic = 0.044715

AUDIO = ("ylo", "x", "core")
SCORE = ("yhi", "z")
RING = 8
VMEM_BYTES = 56 * 1024 * 1024
f32 = jnp.float32
bf16 = jnp.bfloat16


def dot(left, right, dims=((1,), (0,))):
    return lax.dot_general(left, right, (dims, ((), ())), preferred_element_type=f32)


def unit_rows(values):
    wide = values.astype(f32)
    inverse = lax.rsqrt(jnp.sum(wide * wide, axis=-1, keepdims=True) + epsilon)
    return (wide * inverse, inverse)


def unit_backward(unit_wide, inverse, grad_unit):
    inner = jnp.sum(unit_wide * grad_unit, axis=-1, keepdims=True)
    return inverse * (grad_unit - unit_wide * inner)


def pair_coeffs(left, right, partner, first_column):
    logits = logit_scale * dot(left, right, ((1,), (1,))) + logit_bias
    columns = first_column + lax.iota(jnp.int32, right.shape[0])
    sign = jnp.where(partner[:, None] == columns[None, :], 1.0, -1.0)
    return (-logit_scale * sign * jax.nn.sigmoid(-sign * logits)).astype(bf16)


def swap(value, axis):
    return lax.ppermute(value, axis, [(0, 1), (1, 0)])


def shift(value, step):
    perm = [(i, (i + step) % RING) for i in range(RING)]
    perm += [(RING + i, RING + (i - step) % RING) for i in range(RING)]
    return lax.ppermute(value, ("core", "z"), perm)


def shift_across(value, step):
    to = lambda core, half, place: (core * 2 + half) * RING + place % RING
    perm = [
        (to(core, half, place), to(core, 1 - half, place + (step if core == 0 else -step)))
        for core in range(2)
        for half in range(2)
        for place in range(RING)
    ]
    return lax.ppermute(value, ("core", "yhi", "z"), perm)


GROUPS = (
    (((1, 4),), ((1, 3), (1, -3)), ((0, 4),)),
    (((1, 2), (1, -2)), ((1, 1), (1, -1), (1, 0)), ((0, 3),), ((0, -3),)),
    (((0, 2), (0, -2)), ((0, 1), (0, -1), (0, 0))),
)
MEMBERS = tuple(tuple(block for piece in group for block in piece) for group in GROUPS)


def packed_place(half, place, core):
    return (half * (2 * RING) + place * 2 + core)[None]


def block_map(block):
    half, offset = block

    def index_map(i, packed):
        own_half, place, core = packed[0] // (2 * RING), packed[0] // 2 % RING, packed[0] % 2
        along = lax.rem(place + (1 - 2 * core) * offset + RING, RING)
        return lax.rem(own_half + half, 2) * RING + along, 0

    return index_map


def forward_kernel(pieces, first, packed_ref, *refs):
    count = sum(pieces)
    hidden = [ref[...] for ref in refs[:count]]
    refs = refs[count:]
    if first:
        up_ref, down_ref, head_ref = refs[:3]
        down_head_ref = refs[-1]
        down_head_ref[...] = dot(down_ref[...], head_ref[...]).astype(bf16)
        refs = refs[3:-1]
    else:
        up_ref, down_head_ref = refs[:2]
        refs = refs[2:]
    part_refs = refs[: len(pieces)]
    act_t_ref, slope_ref = refs[len(pieces) :]
    rows = hidden[0].shape[0]
    wide = jnp.concatenate(hidden, axis=0).astype(f32)
    square_mean = jnp.mean(wide * wide, axis=-1, keepdims=True)
    inverse = lax.rsqrt(square_mean + epsilon)
    normed = (wide * inverse).astype(bf16)
    pre = dot(normed, up_ref[...], ((1,), (1,)))
    tangent = jnp.tanh(gelu_root * (pre + gelu_cubic * (pre * pre * pre)))
    act = (0.5 * pre * (1.0 + tangent)).astype(bf16)
    part = dot(act, down_head_ref[...]).astype(bf16)
    at = 0
    for size, part_ref in zip(pieces, part_refs):
        part_ref[...] = part[at * rows : (at + size) * rows, :]
        at += size
    slope = 0.5 * (1.0 + tangent) + 0.5 * pre * (1.0 - tangent * tangent) * gelu_root * (
        1.0 + 3.0 * gelu_cubic * pre * pre
    )
    slope = (inverse * slope).astype(bf16)
    act_t = act.T
    for i in range(count):
        span = slice(i * rows, (i + 1) * rows)
        slope_ref[i] = slope[span, :]
        act_t_ref[i] = act_t[:, span]


def forward_blocks(group, packed, hidden_in, up_t, *weights):
    pieces = tuple(len(piece) for piece in GROUPS[group])
    count = sum(pieces)
    first = len(weights) == 2
    rows = hidden_in.shape[0] // (2 * RING)
    ff, width = up_t.shape
    embed = weights[-1].shape[1]
    flat = lambda i, packed: (0, 0)
    cube = lambda i, packed: (0, 0, 0)
    shapes = [jax.ShapeDtypeStruct((size * rows, embed), bf16) for size in pieces]
    shapes += [jax.ShapeDtypeStruct((count,) + dims, bf16) for dims in ((ff, rows), (rows, ff))]
    shapes += [jax.ShapeDtypeStruct((ff, embed), bf16)] if first else []
    out = pl.pallas_call(
        functools.partial(forward_kernel, pieces, first),
        grid_spec=pltpu.PrefetchScalarGridSpec(
            num_scalar_prefetch=1,
            grid=(1,),
            in_specs=[pl.BlockSpec((rows, width), block_map(block)) for block in MEMBERS[group]]
            + [pl.BlockSpec(w.shape, flat) for w in (up_t,) + weights],
            out_specs=[pl.BlockSpec(shape.shape, cube if len(shape.shape) == 3 else flat) for shape in shapes],
        ),
        out_shape=shapes,
        compiler_params=pltpu.CompilerParams(vmem_limit_bytes=VMEM_BYTES),
        cost_estimate=pl.CostEstimate(
            flops=2 * count * rows * ff * (width + embed),
            bytes_accessed=2 * count * rows * (width + embed + 2 * ff) + 2 * ff * (width + embed),
            transcendentals=count * rows * ff,
        ),
    )(packed, *([hidden_in] * count), up_t, *weights)
    parts, kept = out[: len(pieces)], out[len(pieces) : len(pieces) + 2]
    return parts, kept, out[-1]


def backward_kernel(count, blocks, first, last, packed_ref, *refs):
    join = lambda parts, axis: jnp.concatenate(parts, axis=axis) if len(parts) > 1 else parts[0]
    grad = join([ref[...] for ref in refs[:count]], 0)
    kept = refs[count : count + 3 * blocks]
    hidden = join([ref[...] for ref in kept[0::3]], 0)
    act_t, slope = join([ref[0] for ref in kept[1::3]], 1), join([ref[0] for ref in kept[2::3]], 0)
    refs = refs[count + 3 * blocks :]
    down_head_ref, refs = refs[0], refs[1:]
    if not first:
        up_in, act_in = refs[:2]
        refs = refs[2:]
    tile = 256
    grad_act = dot(grad, down_head_ref[...], ((1,), (1,)))
    grad_pre_t = (grad_act * slope.astype(f32)).astype(bf16).T
    act_sum = dot(act_t, grad)
    if not first:
        act_sum = act_sum + act_in[...].astype(f32)
    if last:
        head_ref, keep_ref, give_ref, total, sems = refs
    else:
        up_acc, act_acc = refs
        act_acc[...] = act_sum
    width, ff = hidden.shape[1], act_sum.shape[0]
    for m in range(0, width, tile):
        up_sum = dot(grad_pre_t, hidden[:, m : m + tile])
        if not first:
            up_sum = up_sum + up_in[:, m : m + tile].astype(f32)
        if last:
            total[m : m + tile, :ff] = up_sum.T.astype(bf16)
        else:
            up_acc[:, m : m + tile] = up_sum
    if last:
        core = packed_ref[0] % 2
        act_grad = act_sum.astype(bf16)
        rows = keep_ref.shape[1]
        for m in range(0, width, tile):
            total[m : m + tile, ff:] = dot(head_ref[m : m + tile, :], act_grad, ((1,), (1,))).astype(bf16)
        copies = []
        for half, out_ref in ((core, keep_ref), (1 - core, give_ref)):
            for chip in range(keep_ref.shape[0]):
                at = pl.multiple_of((2 * chip + half) * rows, rows)
                copies.append(
                    pltpu.make_async_copy(total.at[pl.ds(at, rows), :], out_ref.at[chip], sems.at[len(copies)])
                )
                copies[-1].start()
        for copy in copies:
            copy.wait()


def backward_blocks(items, packed, hidden_in, down_head, sums, head_weight=None):
    last = head_weight is not None
    whole = pl.BlockSpec(memory_space=pltpu.VMEM)
    args = [grad for grad, _ in items]
    specs = [whole] * len(items)
    places = [place for _, blocks in items for place in blocks]
    rows, width = hidden_in.shape[0] // (2 * RING), hidden_in.shape[1]
    for block, kept, at in places:
        args.append(hidden_in)
        specs.append(pl.BlockSpec((rows, width), block_map(block)))
        for array in kept:
            args.append(array)
            specs.append(pl.BlockSpec((1,) + array.shape[1:], lambda i, packed, at=at: (at, 0, 0)))
    ff, embed = down_head.shape
    args.append(down_head)
    aliases = {}
    if sums is not None:
        if not last:
            aliases = {len(args) + 1: 0, len(args) + 2: 1}
        args += list(sums)
    if last:
        args.append(head_weight)
        shapes = [jax.ShapeDtypeStruct((8, width // 16, 2 * ff), bf16)] * 2
        scratch = [pltpu.VMEM((width, 2 * ff), bf16), pltpu.SemaphoreType.DMA((16,))]
    else:
        shapes = [jax.ShapeDtypeStruct((ff, width), f32), jax.ShapeDtypeStruct((ff, embed), f32)]
        scratch = []
    specs += [whole] * (len(args) - len(specs))
    return pl.pallas_call(
        functools.partial(backward_kernel, len(items), len(places), sums is None, last),
        grid_spec=pltpu.PrefetchScalarGridSpec(
            num_scalar_prefetch=1,
            grid=(1,),
            in_specs=specs,
            out_specs=[pl.BlockSpec(memory_space=pl.ANY) if last else whole] * 2,
            scratch_shapes=scratch,
        ),
        out_shape=shapes,
        input_output_aliases=aliases,
        compiler_params=pltpu.CompilerParams(vmem_limit_bytes=VMEM_BYTES),
        cost_estimate=pl.CostEstimate(flops=0, bytes_accessed=0, transcendentals=0),
    )(packed, *args)


def score_kernel(embed_ref, grad_ref, out_ref):
    wide, inverse = unit_rows(embed_ref[...])
    out_ref[...] = unit_backward(wide, inverse, grad_ref[...].astype(f32))


def score_backward(score_embed, grad_score):
    return pl.pallas_call(
        score_kernel,
        out_shape=jax.ShapeDtypeStruct(score_embed.shape, f32),
        compiler_params=pltpu.CompilerParams(vmem_limit_bytes=VMEM_BYTES),
    )(score_embed, grad_score)


def total_of(*terms):
    return sum(term.astype(f32) for term in terms)


def per_device(hidden_in, up_weight, down_weight, head_weight, score_embed, pair_index):
    y_hi, z, core = (lax.axis_index(name).astype(jnp.int32) for name in ("yhi", "z", "core"))
    rows = hidden_in.shape[0] // (2 * RING)
    group_half = RING * rows
    packed = packed_place(y_hi, z, core)
    up_t = up_weight.T
    saved = {}

    def forward(group, *weights):
        parts, kept, down_head = forward_blocks(group, packed, hidden_in, up_t, *weights)
        for at, block in enumerate(MEMBERS[group]):
            saved[block] = (block, kept, at)
        return parts, down_head

    score_half = lax.all_gather(score_embed, "z", axis=0, tiled=True)
    (other4, other3, own4), down_head = forward(0, down_weight, head_weight)
    fore, across4, came3 = shift(own4, 1), shift_across(other4, 1), swap(other3, "yhi")
    (other2, other1, own3, own3b), _ = forward(1, down_head)
    came2, came1 = swap(other2, "yhi"), swap(other1, "yhi")
    fore = shift(total_of(own3, came3[:rows], fore, across4).astype(bf16), 1)
    back = shift(total_of(own3b, came3[rows:]).astype(bf16), -1)
    (own2, own1), _ = forward(2, down_head)
    for own, came in ((own2, came2), (own1, came1)):
        fore = shift(total_of(own[:rows], came[:rows], fore).astype(bf16), 1)
        back = shift(total_of(own[rows : 2 * rows], came[rows : 2 * rows], back).astype(bf16), -1)
    score_unit = unit_rows(score_half)[0].astype(bf16)
    fore, back, score_unit = lax.optimization_barrier((fore, back, score_unit))
    own_start = y_hi * group_half + z * rows
    own_hidden = lax.dynamic_slice_in_dim(hidden_in, own_start, rows, 0)
    own_proj = dot(own_hidden, head_weight)
    audio_wide, audio_inverse = unit_rows(own_proj + total_of(own1[2 * rows :], came1[2 * rows :], fore, back))
    audio_own = audio_wide.astype(bf16)
    audio_unit = jnp.concatenate([audio_own, swap(audio_own, "yhi")], axis=0)
    far_start = (1 - y_hi) * group_half + z * rows
    partners = jnp.concatenate(
        [lax.dynamic_slice_in_dim(pair_index[0], start, rows, 0) for start in (own_start, far_start)]
    )
    coeffs = pair_coeffs(audio_unit, score_unit, partners, y_hi * group_half)
    grad_audio = dot(coeffs, score_unit)
    grad_audio = grad_audio[:rows] + swap(grad_audio[rows:].astype(bf16), "yhi").astype(f32)
    grad_embed = unit_backward(audio_wide, audio_inverse, grad_audio).astype(bf16)
    score_part = dot(coeffs, audio_unit, ((0,), (0,))).astype(bf16)
    item = lambda grad, *blocks: (grad, [saved[block] for block in blocks])
    pair = lambda step, half: ((half, step), (half, -step))
    both = lambda up, down: jnp.concatenate([up, down], axis=0)
    fore, back = shift(grad_embed, 1), shift(grad_embed, -1)
    own_block, score_part = lax.optimization_barrier((grad_embed, score_part))
    crossed0 = swap(own_block, "yhi")
    ring1 = both(back, fore)
    crossed1 = swap(ring1, "yhi")
    fore, back = shift(fore, 1), shift(back, -1)
    backward = lambda items, sums, *head: backward_blocks(items, packed, hidden_in, down_head, sums, *head)
    sums = backward([item(grad_embed, (0, 0)), item(crossed0, (1, 0)), item(ring1, *pair(1, 0))], None)
    fore, back, sums = lax.optimization_barrier((fore, back, sums))
    ring2 = both(back, fore)
    crossed2 = swap(ring2, "yhi")
    fore, back = shift(fore, 1), shift(back, -1)
    sums = backward([item(crossed1, *pair(1, 1)), item(ring2, *pair(2, 0))], sums)
    fore, back, sums, crossed2, score_part = lax.optimization_barrier((fore, back, sums, crossed2, score_part))
    grad_score = lax.psum_scatter(score_part, "z", scatter_dimension=0, tiled=True)
    ring4, crossed4 = shift(fore, 1), shift_across(fore, 1)
    ring3 = both(back, fore)
    crossed3 = swap(ring3, "yhi")
    sums = backward([item(ring3, *pair(3, 0)), item(crossed2, *pair(2, 1))], sums)
    ring4, crossed4, sums = lax.optimization_barrier((ring4, crossed4, sums))
    items = [item(crossed3, *pair(3, 1)), item(ring4, (0, 4)), item(crossed4, (1, 4))]
    keep, give = backward(items, sums, head_weight)
    chip = total_of(keep, swap(give, "core")).astype(bf16)
    landed = lax.all_to_all(chip, ("ylo", "x"), 0, 0)
    total = jnp.sum(landed.astype(f32), axis=0)
    ff = up_weight.shape[1]
    score_grad = score_backward(score_embed, grad_score)
    return (total[:, :ff], total[:, ff:].T, score_grad)


def solution(mesh):
    fine = Mesh(mesh.devices.reshape(2, 4, 2, 2, RING), ("ylo", "x", "core", "yhi", "z"))
    in_specs = (
        P(AUDIO, None),
        P(None, SCORE),
        P(SCORE, None),
        P(),
        P(AUDIO + SCORE, None),
        P(AUDIO, None),
    )
    out_specs = (P(AUDIO, SCORE), P(SCORE, AUDIO), P(AUDIO + SCORE, None))
    return jax.shard_map(
        per_device, mesh=fine, in_specs=in_specs, out_specs=out_specs, check_vma=False
    )
```

```python
import functools

import jax
import jax.numpy as jnp
from jax import lax
from jax.experimental import pallas as pl
from jax.experimental.pallas import tpu as pltpu
from jax.sharding import Mesh, PartitionSpec as P

logit_scale = 8.0
logit_bias = -3.0
epsilon = 1e-06
gelu_root = 0.7978845608028654
gelu_cubic = 0.044715

AUDIO = ("ylo", "x", "core")
SCORE = ("yhi", "z")
RING = 8
VMEM_BYTES = 56 * 1024 * 1024
f32 = jnp.float32
bf16 = jnp.bfloat16


def dot(left, right, dims=((1,), (0,))):
    return lax.dot_general(left, right, (dims, ((), ())), preferred_element_type=f32)


def unit_rows(values):
    wide = values.astype(f32)
    inverse = lax.rsqrt(jnp.sum(wide * wide, axis=-1, keepdims=True) + epsilon)
    return (wide * inverse, inverse)


def unit_backward(unit_wide, inverse, grad_unit):
    inner = jnp.sum(unit_wide * grad_unit, axis=-1, keepdims=True)
    return inverse * (grad_unit - unit_wide * inner)


def pair_coeffs(left, right, partner, first_column):
    logits = logit_scale * dot(left, right, ((1,), (1,))) + logit_bias
    columns = first_column + lax.iota(jnp.int32, right.shape[0])
    sign = jnp.where(partner[:, None] == columns[None, :], 1.0, -1.0)
    return (-logit_scale * sign * jax.nn.sigmoid(-sign * logits)).astype(bf16)


def swap(value, axis):
    return lax.ppermute(value, axis, [(0, 1), (1, 0)])


def shift(value, step):
    perm = [(i, (i + step) % RING) for i in range(RING)]
    perm += [(RING + i, RING + (i - step) % RING) for i in range(RING)]
    return lax.ppermute(value, ("core", "z"), perm)


def shift_across(value, step):
    to = lambda core, half, place: (core * 2 + half) * RING + place % RING
    perm = [
        (to(core, half, place), to(core, 1 - half, place + (step if core == 0 else -step)))
        for core in range(2)
        for half in range(2)
        for place in range(RING)
    ]
    return lax.ppermute(value, ("core", "yhi", "z"), perm)


GROUPS = (
    (((1, 4),), ((1, 3), (1, -3)), ((0, 4),)),
    (((1, 2), (1, -2)), ((1, 1), (1, -1), (1, 0)), ((0, 3),), ((0, -3),)),
    (((0, 2), (0, -2)), ((0, 1), (0, -1), (0, 0))),
)
MEMBERS = tuple(tuple(block for piece in group for block in piece) for group in GROUPS)


def packed_place(half, place, core):
    return (half * (2 * RING) + place * 2 + core)[None]


def block_map(block):
    half, offset = block

    def index_map(i, packed):
        own_half, place, core = packed[0] // (2 * RING), packed[0] // 2 % RING, packed[0] % 2
        along = lax.rem(place + (1 - 2 * core) * offset + RING, RING)
        return lax.rem(own_half + half, 2) * RING + along, 0

    return index_map


def forward_kernel(pieces, first, packed_ref, *refs):
    count = sum(pieces)
    hidden = [ref[...] for ref in refs[:count]]
    refs = refs[count:]
    if first:
        up_ref, down_ref, head_ref = refs[:3]
        down_head_ref = refs[-1]
        down_head_ref[...] = dot(down_ref[...], head_ref[...]).astype(bf16)
        refs = refs[3:-1]
    else:
        up_ref, down_head_ref = refs[:2]
        refs = refs[2:]
    part_refs = refs[: len(pieces)]
    act_t_ref, slope_ref = refs[len(pieces) :]
    rows = hidden[0].shape[0]
    wide = jnp.concatenate(hidden, axis=0).astype(f32)
    square_mean = jnp.mean(wide * wide, axis=-1, keepdims=True)
    inverse = lax.rsqrt(square_mean + epsilon)
    normed = (wide * inverse).astype(bf16)
    pre = dot(normed, up_ref[...], ((1,), (1,)))
    tangent = jnp.tanh(gelu_root * (pre + gelu_cubic * (pre * pre * pre)))
    act = (0.5 * pre * (1.0 + tangent)).astype(bf16)
    part = dot(act, down_head_ref[...]).astype(bf16)
    at = 0
    for size, part_ref in zip(pieces, part_refs):
        part_ref[...] = part[at * rows : (at + size) * rows, :]
        at += size
    slope = 0.5 * (1.0 + tangent) + 0.5 * pre * (1.0 - tangent * tangent) * gelu_root * (
        1.0 + 3.0 * gelu_cubic * pre * pre
    )
    slope = (inverse * slope).astype(bf16)
    act_t = act.T
    for i in range(count):
        span = slice(i * rows, (i + 1) * rows)
        slope_ref[i] = slope[span, :]
        act_t_ref[i] = act_t[:, span]


def forward_blocks(group, packed, hidden_in, up_t, *weights):
    pieces = tuple(len(piece) for piece in GROUPS[group])
    count = sum(pieces)
    first = len(weights) == 2
    rows = hidden_in.shape[0] // (2 * RING)
    ff, width = up_t.shape
    embed = weights[-1].shape[1]
    flat = lambda i, packed: (0, 0)
    cube = lambda i, packed: (0, 0, 0)
    shapes = [jax.ShapeDtypeStruct((size * rows, embed), bf16) for size in pieces]
    shapes += [jax.ShapeDtypeStruct((count,) + dims, bf16) for dims in ((ff, rows), (rows, ff))]
    shapes += [jax.ShapeDtypeStruct((ff, embed), bf16)] if first else []
    out = pl.pallas_call(
        functools.partial(forward_kernel, pieces, first),
        grid_spec=pltpu.PrefetchScalarGridSpec(
            num_scalar_prefetch=1,
            grid=(1,),
            in_specs=[pl.BlockSpec((rows, width), block_map(block)) for block in MEMBERS[group]]
            + [pl.BlockSpec(w.shape, flat) for w in (up_t,) + weights],
            out_specs=[pl.BlockSpec(shape.shape, cube if len(shape.shape) == 3 else flat) for shape in shapes],
        ),
        out_shape=shapes,
        compiler_params=pltpu.CompilerParams(vmem_limit_bytes=VMEM_BYTES),
        cost_estimate=pl.CostEstimate(
            flops=2 * count * rows * ff * (width + embed),
            bytes_accessed=2 * count * rows * (width + embed + 2 * ff) + 2 * ff * (width + embed),
            transcendentals=count * rows * ff,
        ),
    )(packed, *([hidden_in] * count), up_t, *weights)
    parts, kept = out[: len(pieces)], out[len(pieces) : len(pieces) + 2]
    return parts, kept, out[-1]


def backward_kernel(count, blocks, first, last, packed_ref, *refs):
    join = lambda parts, axis: jnp.concatenate(parts, axis=axis) if len(parts) > 1 else parts[0]
    grad = join([ref[...] for ref in refs[:count]], 0)
    kept = refs[count : count + 3 * blocks]
    hidden = join([ref[...] for ref in kept[0::3]], 0)
    act_t, slope = join([ref[0] for ref in kept[1::3]], 1), join([ref[0] for ref in kept[2::3]], 0)
    refs = refs[count + 3 * blocks :]
    down_head_ref, refs = refs[0], refs[1:]
    if not first:
        up_in, act_in = refs[:2]
        refs = refs[2:]
    tile = 256
    grad_act = dot(grad, down_head_ref[...], ((1,), (1,)))
    grad_pre_t = (grad_act * slope.astype(f32)).astype(bf16).T
    act_sum = dot(act_t, grad)
    if not first:
        act_sum = act_sum + act_in[...].astype(f32)
    if last:
        head_ref, keep_ref, give_ref, total, sems = refs
    else:
        up_acc, act_acc = refs
        act_acc[...] = act_sum
    width, ff = hidden.shape[1], act_sum.shape[0]
    for m in range(0, width, tile):
        up_sum = dot(grad_pre_t, hidden[:, m : m + tile])
        if not first:
            up_sum = up_sum + up_in[:, m : m + tile].astype(f32)
        if last:
            total[m : m + tile, :ff] = up_sum.T.astype(bf16)
        else:
            up_acc[:, m : m + tile] = up_sum.astype(bf16)
    if last:
        core = packed_ref[0] % 2
        act_grad = act_sum.astype(bf16)
        rows = keep_ref.shape[1]
        for m in range(0, width, tile):
            total[m : m + tile, ff:] = dot(head_ref[m : m + tile, :], act_grad, ((1,), (1,))).astype(bf16)
        copies = []
        for half, out_ref in ((core, keep_ref), (1 - core, give_ref)):
            for chip in range(keep_ref.shape[0]):
                at = pl.multiple_of((2 * chip + half) * rows, rows)
                copies.append(
                    pltpu.make_async_copy(total.at[pl.ds(at, rows), :], out_ref.at[chip], sems.at[len(copies)])
                )
                copies[-1].start()
        for copy in copies:
            copy.wait()


def backward_blocks(items, packed, hidden_in, down_head, sums, head_weight=None):
    last = head_weight is not None
    whole = pl.BlockSpec(memory_space=pltpu.VMEM)
    args = [grad for grad, _ in items]
    specs = [whole] * len(items)
    places = [place for _, blocks in items for place in blocks]
    rows, width = hidden_in.shape[0] // (2 * RING), hidden_in.shape[1]
    for block, kept, at in places:
        args.append(hidden_in)
        specs.append(pl.BlockSpec((rows, width), block_map(block)))
        for array in kept:
            args.append(array)
            specs.append(pl.BlockSpec((1,) + array.shape[1:], lambda i, packed, at=at: (at, 0, 0)))
    ff, embed = down_head.shape
    args.append(down_head)
    aliases = {}
    if sums is not None:
        if not last:
            aliases = {len(args) + 1: 0, len(args) + 2: 1}
        args += list(sums)
    if last:
        args.append(head_weight)
        shapes = [jax.ShapeDtypeStruct((8, width // 16, 2 * ff), bf16)] * 2
        scratch = [pltpu.VMEM((width, 2 * ff), bf16), pltpu.SemaphoreType.DMA((16,))]
    else:
        shapes = [jax.ShapeDtypeStruct((ff, width), bf16), jax.ShapeDtypeStruct((ff, embed), f32)]
        scratch = []
    specs += [whole] * (len(args) - len(specs))
    return pl.pallas_call(
        functools.partial(backward_kernel, len(items), len(places), sums is None, last),
        grid_spec=pltpu.PrefetchScalarGridSpec(
            num_scalar_prefetch=1,
            grid=(1,),
            in_specs=specs,
            out_specs=[pl.BlockSpec(memory_space=pl.ANY) if last else whole] * 2,
            scratch_shapes=scratch,
        ),
        out_shape=shapes,
        input_output_aliases=aliases,
        compiler_params=pltpu.CompilerParams(vmem_limit_bytes=VMEM_BYTES),
        cost_estimate=pl.CostEstimate(flops=0, bytes_accessed=0, transcendentals=0),
    )(packed, *args)


def score_kernel(embed_ref, grad_ref, out_ref):
    wide, inverse = unit_rows(embed_ref[...])
    out_ref[...] = unit_backward(wide, inverse, grad_ref[...].astype(f32))


def score_backward(score_embed, grad_score):
    return pl.pallas_call(
        score_kernel,
        out_shape=jax.ShapeDtypeStruct(score_embed.shape, f32),
        compiler_params=pltpu.CompilerParams(vmem_limit_bytes=VMEM_BYTES),
    )(score_embed, grad_score)


def total_of(*terms):
    return sum(term.astype(f32) for term in terms)


def per_device(hidden_in, up_weight, down_weight, head_weight, score_embed, pair_index):
    y_hi, z, core = (lax.axis_index(name).astype(jnp.int32) for name in ("yhi", "z", "core"))
    rows = hidden_in.shape[0] // (2 * RING)
    group_half = RING * rows
    packed = packed_place(y_hi, z, core)
    up_t = up_weight.T
    saved = {}

    def forward(group, *weights):
        parts, kept, down_head = forward_blocks(group, packed, hidden_in, up_t, *weights)
        for at, block in enumerate(MEMBERS[group]):
            saved[block] = (block, kept, at)
        return parts, down_head

    score_half = lax.all_gather(score_embed, "z", axis=0, tiled=True)
    (other4, other3, own4), down_head = forward(0, down_weight, head_weight)
    fore, across4, came3 = shift(own4, 1), shift_across(other4, 1), swap(other3, "yhi")
    (other2, other1, own3, own3b), _ = forward(1, down_head)
    came2, came1 = swap(other2, "yhi"), swap(other1, "yhi")
    fore = shift(total_of(own3, came3[:rows], fore, across4).astype(bf16), 1)
    back = shift(total_of(own3b, came3[rows:]).astype(bf16), -1)
    (own2, own1), _ = forward(2, down_head)
    for own, came in ((own2, came2), (own1, came1)):
        fore = shift(total_of(own[:rows], came[:rows], fore).astype(bf16), 1)
        back = shift(total_of(own[rows : 2 * rows], came[rows : 2 * rows], back).astype(bf16), -1)
    score_unit = unit_rows(score_half)[0].astype(bf16)
    fore, back, score_unit = lax.optimization_barrier((fore, back, score_unit))
    own_start = y_hi * group_half + z * rows
    own_hidden = lax.dynamic_slice_in_dim(hidden_in, own_start, rows, 0)
    own_proj = dot(own_hidden, head_weight)
    audio_wide, audio_inverse = unit_rows(own_proj + total_of(own1[2 * rows :], came1[2 * rows :], fore, back))
    audio_own = audio_wide.astype(bf16)
    audio_unit = jnp.concatenate([audio_own, swap(audio_own, "yhi")], axis=0)
    far_start = (1 - y_hi) * group_half + z * rows
    partners = jnp.concatenate(
        [lax.dynamic_slice_in_dim(pair_index[0], start, rows, 0) for start in (own_start, far_start)]
    )
    coeffs = pair_coeffs(audio_unit, score_unit, partners, y_hi * group_half)
    grad_audio = dot(coeffs, score_unit)
    grad_audio = grad_audio[:rows] + swap(grad_audio[rows:].astype(bf16), "yhi").astype(f32)
    grad_embed = unit_backward(audio_wide, audio_inverse, grad_audio).astype(bf16)
    score_part = dot(coeffs, audio_unit, ((0,), (0,))).astype(bf16)
    item = lambda grad, *blocks: (grad, [saved[block] for block in blocks])
    pair = lambda step, half: ((half, step), (half, -step))
    both = lambda up, down: jnp.concatenate([up, down], axis=0)
    fore, back = shift(grad_embed, 1), shift(grad_embed, -1)
    own_block, score_part = lax.optimization_barrier((grad_embed, score_part))
    crossed0 = swap(own_block, "yhi")
    ring1 = both(back, fore)
    crossed1 = swap(ring1, "yhi")
    fore, back = shift(fore, 1), shift(back, -1)
    backward = lambda items, sums, *head: backward_blocks(items, packed, hidden_in, down_head, sums, *head)
    sums = backward([item(grad_embed, (0, 0)), item(crossed0, (1, 0)), item(ring1, *pair(1, 0))], None)
    fore, back, sums = lax.optimization_barrier((fore, back, sums))
    ring2 = both(back, fore)
    crossed2 = swap(ring2, "yhi")
    fore, back = shift(fore, 1), shift(back, -1)
    sums = backward([item(crossed1, *pair(1, 1)), item(ring2, *pair(2, 0))], sums)
    fore, back, sums, crossed2, score_part = lax.optimization_barrier((fore, back, sums, crossed2, score_part))
    grad_score = lax.psum_scatter(score_part, "z", scatter_dimension=0, tiled=True)
    ring4, crossed4 = shift(fore, 1), shift_across(fore, 1)
    ring3 = both(back, fore)
    crossed3 = swap(ring3, "yhi")
    sums = backward([item(ring3, *pair(3, 0)), item(crossed2, *pair(2, 1))], sums)
    ring4, crossed4, sums = lax.optimization_barrier((ring4, crossed4, sums))
    items = [item(crossed3, *pair(3, 1)), item(ring4, (0, 4)), item(crossed4, (1, 4))]
    keep, give = backward(items, sums, head_weight)
    chip = total_of(keep, swap(give, "core")).astype(bf16)
    landed = lax.all_to_all(chip, ("ylo", "x"), 0, 0)
    total = jnp.sum(landed.astype(f32), axis=0)
    ff = up_weight.shape[1]
    score_grad = score_backward(score_embed, grad_score)
    return (total[:, :ff], total[:, ff:].T, score_grad)


def solution(mesh):
    fine = Mesh(mesh.devices.reshape(2, 4, 2, 2, RING), ("ylo", "x", "core", "yhi", "z"))
    in_specs = (
        P(AUDIO, None),
        P(None, SCORE),
        P(SCORE, None),
        P(),
        P(AUDIO + SCORE, None),
        P(AUDIO, None),
    )
    out_specs = (P(AUDIO, SCORE), P(SCORE, AUDIO), P(AUDIO + SCORE, None))
    return jax.shard_map(
        per_device, mesh=fine, in_specs=in_specs, out_specs=out_specs, check_vma=False
    )
```
